128 devices in a mesh: section: 2 (over x_hi), dp: 16 (over y, z), seq: 4 (over x_lo, core).
Axes of the slice: x: 4 (x_hi: 2, x_lo: 2; x = x_hi * 2 + x_lo), y: 4, z: 4, core: 2. Of those that a mesh axis runs over, the one named last changes fastest.
Arguments:
- latents: bfloat16 [2, 16, 1024, 768], P(None, 'dp', 'seq'), may hold values from -6 to 6
- conditions: float32 [2, 16, 768], P(None, 'dp'), may hold values from -6 to 6
- output_cotangent: bfloat16 [2, 16, 1024, 768], P(None, 'dp', 'seq'), may hold values from -6 to 6
- modulation_weight: bfloat16 [2, 768, 4608], P('section', 'dp'), may hold values from -0.21875 to 0.21875
- modulation_bias: bfloat16 [2, 4608], P('section', 'dp'), may hold values from -3 to 3
- projection_weight: bfloat16 [2, 768, 2304], P('section', 'dp'), may hold values from -0.21875 to 0.21875
- projection_bias: bfloat16 [2, 1536], P('section', 'dp'), may hold values from -3 to 3
- attention_weight: bfloat16 [2, 768, 768], P('section', 'dp'), may hold values from -1.75 to 1.75
- attention_bias: bfloat16 [2, 768], P('section', 'dp'), may hold values from -2 to 2
- expand_weight: bfloat16 [2, 768, 3072], P('section', 'dp'), may hold values from -0.21875 to 0.21875
- expand_bias: bfloat16 [2, 3072], P('section', 'dp'), may hold values from -3 to 3
- contract_weight: bfloat16 [2, 3072, 768], P('section', 'dp'), may hold values from -0.109375 to 0.109375
- contract_bias: bfloat16 [2, 768], P('section', 'dp'), may hold values from -2 to 2
Outputs:
- section_outputs: bfloat16 [2, 2, 16, 1024, 768], P('section', None, 'dp', 'seq')
- input_grads: float32 [2, 2, 16, 1024, 768], P('section', None, 'dp', 'seq')
- condition_grads: float32 [2, 16, 768], P(None, 'dp')
- modulation_weight_grad: float32 [2, 768, 4608], P('section', 'dp')
- modulation_bias_grad: float32 [2, 4608], P('section', 'dp')
- projection_weight_grad: float32 [2, 768, 2304], P('section', 'dp')
- projection_bias_grad: float32 [2, 1536], P('section', 'dp')
- attention_weight_grad: float32 [2, 768, 768], P('section', 'dp')
- attention_bias_grad: float32 [2, 768], P('section', 'dp')
- expand_weight_grad: float32 [2, 768, 3072], P('section', 'dp')
- expand_bias_grad: float32 [2, 3072], P('section', 'dp')
- contract_weight_grad: float32 [2, 3072, 768], P('section', 'dp')
- contract_bias_grad: float32 [2, 768], P('section', 'dp')
The draws below stay inside these ranges and needn't reach their ends.
All inputs are finite; a program needn't handle non-finite values.
Results may differ from the reference program's by a relative error of at most 0.02.
The reference program's roundings to bfloat16 on the way count: a program that leaves them out, or rounds other values in their place, can miss the bound.
Values may be sent and summed in bfloat16 or wider, within the bound.
A program may use at most 192 MiB of HBM per device.

```python
import jax
import jax.numpy as jnp
from jax import lax

D = 768
HEADS = 12
HEAD = 64
FF = 3072
LEN = 1024
MICRO = 2
SECTIONS = 2
LATENTS = 16


def level_of(own_key, dims, cuts, least, high):
    gain, own = 1.0, jax.random.fold_in(own_key, 6)
    for position, shards_of in cuts:
        heights = jnp.exp(jax.random.uniform(jax.random.fold_in(own, position), (shards_of,), jnp.float32, least / len(cuts), high / len(cuts)))
        gain = gain * jnp.repeat(heights, dims[position] // shards_of).reshape([-1 if axis == position else 1 for axis in range(len(dims))])
    return gain


def scatter_about(stream_key, extent, spread, most, pieces=(), dtype=jnp.bfloat16):
    values = spread * jax.random.normal(stream_key, extent, jnp.float32)
    if pieces:
        values = values * level_of(stream_key, extent, pieces, -0.22, 0.18)
    return jnp.clip(values, -most, most).astype(dtype)


def setup_inputs(seed: int = 0) -> dict:
    splits = jax.random.split(jax.random.key(seed), 14)
    return {
        "latents": scatter_about(splits[0], (MICRO, LATENTS, LEN, D), 1.0, 6.0, ((1, 16), (2, 4))),
        "conditions": scatter_about(splits[1], (MICRO, LATENTS, D), 1.0, 6.0, ((1, 16),), jnp.float32),
        "output_cotangent": scatter_about(splits[2], (MICRO, LATENTS, LEN, D), 1.0, 6.0, ((1, 16), (2, 4))),
        "modulation_weight": scatter_about(splits[3], (SECTIONS, D, 6 * D), D ** -0.5, 0.21875, ((0, 2), (1, 16))),
        "modulation_bias": scatter_about(splits[4], (SECTIONS, 6 * D), 0.5, 3.0, ((0, 2), (1, 16))),
        "projection_weight": scatter_about(splits[5], (SECTIONS, D, 3 * D), D ** -0.5, 0.21875, ((0, 2), (1, 16))),
        "projection_bias": scatter_about(splits[6], (SECTIONS, 2 * D), 0.5, 3.0, ((0, 2), (1, 16))),
        "attention_weight": scatter_about(splits[7], (SECTIONS, D, D), (D // 64) ** -0.5, 1.75, ((0, 2), (1, 16))),
        "attention_bias": scatter_about(splits[8], (SECTIONS, D), 0.3, 2.0, ((0, 2), (1, 16))),
        "expand_weight": scatter_about(splits[9], (SECTIONS, D, FF), D ** -0.5, 0.21875, ((0, 2), (1, 16))),
        "expand_bias": scatter_about(splits[10], (SECTIONS, FF), 0.5, 3.0, ((0, 2), (1, 16))),
        "contract_weight": scatter_about(splits[11], (SECTIONS, FF, D), FF ** -0.5, 0.109375, ((0, 2), (1, 16))),
        "contract_bias": scatter_about(splits[12], (SECTIONS, D), 0.3, 2.0, ((0, 2), (1, 16))),
    }


@jax.custom_vjp
def low(v):
    return lax.optimization_barrier(v.astype(jnp.bfloat16)).astype(jnp.float32)

@jax.custom_vjp
def low_back(v):
    return v

def low_keep(v):
    return (low(v), None)

def low_pass(kept, grad):
    return (grad,)

def back_keep(v):
    return (v, None)

def back_low(kept, grad):
    return (low(grad),)
low.defvjp(low_keep, low_pass)
low_back.defvjp(back_keep, back_low)
PRECISE = lax.Precision.HIGHEST

def matmul(left, right):
    return jnp.dot(left, right, precision=PRECISE, preferred_element_type=jnp.float32)

def norm_rows(values):
    row_mean = lax.optimization_barrier(jnp.mean(values, axis=-1, keepdims=True))
    centered = values - row_mean
    variance = lax.optimization_barrier(jnp.mean(centered * centered, axis=-1, keepdims=True))
    return centered * lax.rsqrt(variance + 1e-06)

def attend_block(queries, key_rows, value_rows):
    scores = jnp.einsum('qhd,khd->hqk', queries, key_rows, precision=PRECISE) * HEAD ** (-0.5)
    scores = low_back(scores)
    row_top = lax.optimization_barrier(jnp.max(scores, axis=-1, keepdims=True))
    log_total = row_top + jnp.log(lax.optimization_barrier(jnp.sum(jnp.exp(scores - row_top), axis=-1, keepdims=True)))
    weights = low(jnp.exp(scores - log_total))
    return jnp.einsum('hqk,khd->qhd', weights, value_rows, precision=PRECISE)

def layer_one(tokens, condition, weights):
    modulation_weight, modulation_bias, projection_weight, projection_bias, attention_weight, attention_bias, expand_weight, expand_bias, contract_weight, contract_bias = weights
    silu_cond = low(jax.nn.silu(condition))
    modulation = low_back(matmul(silu_cond[None, :], modulation_weight)[0] + modulation_bias)
    shift_one, scale_one, gate_one, shift_two, scale_two, gate_two = jnp.split(modulation, 6)
    mixed_one = low(norm_rows(tokens) * (1.0 + scale_one) + shift_one)
    full_bias = jnp.concatenate([projection_bias[:D], jnp.zeros((D,), jnp.float32), projection_bias[D:]])
    projected = low_back(low(matmul(mixed_one, projection_weight) + full_bias))
    queries = projected[:, :D].reshape(LEN, HEADS, HEAD)
    key_rows = projected[:, D:2 * D].reshape(LEN, HEADS, HEAD)
    value_rows = projected[:, 2 * D:].reshape(LEN, HEADS, HEAD)
    block_rows = min(512, LEN)
    query_blocks = queries.reshape(LEN // block_rows, block_rows, HEADS, HEAD)
    attended = lax.map(jax.checkpoint(lambda query_block: attend_block(query_block, key_rows, value_rows)), query_blocks)
    attended = low_back(low(attended.reshape(LEN, D)))
    branch_one = low_back(matmul(attended, attention_weight) + attention_bias)
    middle = tokens + gate_one * branch_one
    mixed_two = low(norm_rows(middle) * (1.0 + scale_two) + shift_two)
    expanded = low_back(matmul(mixed_two, expand_weight) + expand_bias)
    activated = low(jax.nn.gelu(expanded, approximate=True))
    branch_two = low_back(matmul(activated, contract_weight) + contract_bias)
    return middle + gate_two * branch_two

def layer_all(tokens, conditions, weights):
    flat_tokens = tokens.reshape(MICRO * LATENTS, LEN, D)
    flat_conds = conditions.reshape(MICRO * LATENTS, D)
    layer_step = jax.checkpoint(lambda latent_pair: layer_one(latent_pair[0], latent_pair[1], weights))
    result = lax.map(layer_step, (flat_tokens, flat_conds))
    return result.reshape(MICRO, LATENTS, LEN, D)

def reference(latents, conditions, output_cotangent, modulation_weight, modulation_bias, projection_weight, projection_bias, attention_weight, attention_bias, expand_weight, expand_bias, contract_weight, contract_bias):
    params = tuple((weight.astype(jnp.float32) for weight in (modulation_weight, modulation_bias, projection_weight, projection_bias, attention_weight, attention_bias, expand_weight, expand_bias, contract_weight, contract_bias)))
    inputs = latents.astype(jnp.float32)
    cotangent = output_cotangent.astype(jnp.float32)
    probe = jnp.zeros_like(inputs)

    def forward_pass(inputs, conditions, probe, params):
        first_layer = tuple((weight[0] for weight in params))
        second_layer = tuple((weight[1] for weight in params))
        sent = low(layer_all(inputs, conditions, first_layer))
        hidden = low_back(sent + probe)
        return (sent, layer_all(hidden, conditions, second_layer))
    (section_zero, section_one), pull_back = jax.vjp(forward_pass, inputs, conditions, probe, params)
    input_grad, condition_grads, probe_grad, param_grads = pull_back((jnp.zeros_like(section_zero), cotangent))
    section_outputs = jnp.stack([section_zero, section_one]).astype(jnp.bfloat16)
    input_grads = jnp.stack([input_grad, probe_grad])
    return (section_outputs, input_grads, condition_grads, param_grads[0], param_grads[1], param_grads[2], param_grads[3], param_grads[4], param_grads[5], param_grads[6], param_grads[7], param_grads[8], param_grads[9])
```

```python
import functools

import jax
import jax.numpy as jnp
from jax import lax
from jax.experimental import pallas as pl
from jax.experimental.pallas import tpu as pltpu
from jax.sharding import PartitionSpec as P

HEAD = 64


MESH = pl.DeviceIdType.MESH
ROWS = 608
HALF = ROWS // 2
TOP = 160
LOW = HALF - TOP
WIDE = 768
OFFSETS = (0, 3, 1, 2)


class Place:
    def __init__(self):
        self.s = lax.axis_index("section")
        self.d = lax.axis_index("dp")
        self.q = lax.axis_index("seq")
        y, z = self.d // 4, lax.rem(self.d, 4)
        self.xl, self.c = self.q // 2, lax.rem(self.q, 2)
        self.a = (1 - self.c) * z + self.c * y
        self.b = (1 - self.c) * y + self.c * z

    def dp(self, ka, kb):
        aa = lax.rem(self.a + ka, 4)
        bb = lax.rem(self.b + kb, 4)
        return aa * (1 + 3 * self.c) + bb * (4 - 3 * self.c)

    def ring(self, ka, kb):
        return (self.s, self.dp(ka, kb), self.q)

    def sibling(self):
        return (self.s, self.d, self.xl * 2 + 1 - self.c)

    def across(self):
        return (1 - self.s, self.d, (1 - self.xl) * 2 + self.c)

    def beside(self):
        return (self.s, self.d, (1 - self.xl) * 2 + self.c)

    def askew(self):
        return (self.s, self.d, (1 - self.xl) * 2 + 1 - self.c)

    def flipped(self):
        return (1 - self.s, self.d, self.q)

    def grid_peers(self):
        return [self.ring(k, 0) for k in (1, 3, 2)] + [self.ring(0, k) for k in (1, 3, 2)]


def greet(devices):
    barrier = pltpu.get_barrier_semaphore()
    for device in devices:
        pl.semaphore_signal(barrier, inc=1, device_id=device, device_id_type=MESH)
    pl.semaphore_wait(barrier, len(devices))


def half_rows(core, offset, count):
    return pl.ds(pl.multiple_of(core * HALF + offset, 16), count)


class Wires:
    def __init__(self, send, recv):
        self.send, self.recv, self.started = send, recv, []

    def push(self, index, source, target, device, landing=None):
        item = pltpu.make_async_remote_copy(
            src_ref=source,
            dst_ref=target,
            send_sem=self.send.at[index],
            recv_sem=self.recv.at[index if landing is None else landing],
            device_id=device,
            device_id_type=MESH,
        )
        item.start()
        self.started.append(item)

    def got(self, index, target, device):
        pltpu.make_async_remote_copy(
            src_ref=target,
            dst_ref=target,
            send_sem=self.send.at[0],
            recv_sem=self.recv.at[index],
            device_id=device,
            device_id_type=MESH,
        ).wait_recv()

    def finish(self):
        for item in self.started:
            item.wait_send()


TOKENS = 256
PAIR = 128
EXPAND_ROWS = (192, 240, 304, 352)
CONTRACT_ROW = 400
BIAS_ROW = 288
ROOT = (2.0 / 3.141592653589793) ** 0.5


def norm_rows(values):
    row_mean = jnp.mean(values, axis=-1, keepdims=True)
    centered = values - row_mean
    variance = jnp.mean(centered * centered, axis=-1, keepdims=True)
    inv_std = lax.rsqrt(variance + 1e-06)
    return (centered * inv_std, inv_std)


def norm_back(gradient, normed, inv_std):
    row_mean = jnp.mean(gradient, axis=-1, keepdims=True)
    along = jnp.mean(gradient * normed, axis=-1, keepdims=True)
    return inv_std * (gradient - row_mean - normed * along)


def dot(left, right, left_dim=1, right_dim=0):
    return lax.dot_general(
        left, right, (((left_dim,), (right_dim,)), ((), ())), preferred_element_type=jnp.float32
    )


def column_sum(values):
    return jnp.sum(values.astype(jnp.float32), axis=0, keepdims=True)


def square(w, row):
    return w[:, row : row + 48, :].reshape(WIDE, WIDE)


def contract_square(w, part):
    return w[4 * part : 4 * part + 4, CONTRACT_ROW : CONTRACT_ROW + 192, :].reshape(WIDE, WIDE)


def side_by_side(ref, lead=()):
    return jnp.concatenate([ref[(*lead, pair)] for pair in range(6)], axis=1)


def head_lanes(head):
    lane = lax.broadcasted_iota(jnp.int32, (1, PAIR), 1)
    return (lane // HEAD) == head


def only_head(values, head):
    return jnp.where(head_lanes(head), values, jnp.zeros_like(values))


def gather_steps(me, wires, base, source, w_ref, local):
    right_a, left_a = me.ring(1, 0), me.ring(3, 0)
    right_b, left_b = me.ring(0, 1), me.ring(0, 3)
    sibling = me.sibling()

    def slot(ka, kb, offset=0, count=HALF):
        return w_ref.at[me.dp(ka, kb), half_rows(me.c, offset, count), :]

    def got(index, target):
        wires.got(base + index, target, sibling)

    def push(index, origin, target, device):
        wires.push(base + index, origin, target, device)

    def to_side(ka, kb, origin=None):
        block = slot(ka, kb)
        push(20 + 4 * ka + kb, block if origin is None else origin, block, sibling)

    def spread_b(ka, origin=None):
        block = slot(ka, 0)
        origin = block if origin is None else origin
        push(4 + 4 * ka, origin, block, right_b)
        push(5 + 4 * ka, origin, block, left_b)

    own = pltpu.make_async_copy(source, slot(0, 0), local)

    def start():
        own.start()
        push(0, source, slot(0, 0), right_a)
        push(1, source, slot(0, 0), left_a)
        spread_b(0, source)
        to_side(0, 0, source)

    def forward_a():
        got(0, slot(3, 0))
        push(2, slot(3, 0, 0, TOP), slot(3, 0, 0, TOP), right_a)
        spread_b(3)
        to_side(3, 0)
        got(1, slot(1, 0))
        push(3, slot(1, 0, TOP, LOW), slot(1, 0, TOP, LOW), left_a)
        spread_b(1)
        to_side(1, 0)

    def end_a():
        got(2, slot(2, 0, 0, TOP))
        got(3, slot(2, 0, TOP, LOW))
        spread_b(2)
        to_side(2, 0)

    def forward_b(ka):
        at = 4 + 4 * ka
        got(at, slot(ka, 3))
        push(at + 2, slot(ka, 3, 0, TOP), slot(ka, 3, 0, TOP), right_b)
        to_side(ka, 3)
        got(at + 1, slot(ka, 1))
        push(at + 3, slot(ka, 1, TOP, LOW), slot(ka, 1, TOP, LOW), left_b)
        to_side(ka, 1)

    def end_b(ka):
        at = 4 + 4 * ka
        got(at + 2, slot(ka, 2, 0, TOP))
        got(at + 3, slot(ka, 2, TOP, LOW))
        to_side(ka, 2)

    def finish():
        own.wait()
        for ka in range(4):
            for kb in range(4):
                got(20 + 4 * ka + kb, w_ref.at[me.dp(kb, ka), half_rows(1 - me.c, 0, HALF), :])

    steps = [start, forward_a, end_a]
    steps += [functools.partial(forward_b, ka) for ka in OFFSETS]
    steps += [functools.partial(end_b, ka) for ka in OFFSETS]
    return steps + [finish]


def swap_steps(me, wires, base, pieces, first, second, result):
    def start():
        for ka in range(4):
            for kb in range(4):
                first[0, ka, kb] = pieces[me.dp(ka, kb)]
        for k in (1, 2, 3):
            wires.push(base + k - 1, first.at[0, k], first.at[1, k], me.ring(k, 0))

    def middle():
        for kb in range(4):
            second[0, kb, 0] = first[0, 0, kb]
        for k in (1, 2, 3):
            wires.got(base + k - 1, first.at[1, k], me.sibling())
            for kb in range(4):
                second[0, kb, k] = first[1, k, kb]
        for k in (1, 2, 3):
            wires.push(base + 2 + k, second.at[0, k], second.at[1, k], me.ring(0, k))

    def end():
        for ka in range(4):
            result[me.dp((4 - ka) % 4, 0)] = second[0, 0, ka]
        for k in (1, 2, 3):
            wires.got(base + 2 + k, second.at[1, k], me.sibling())
            for ka in range(4):
                result[me.dp((4 - ka) % 4, 4 - k)] = second[1, k, ka]

    return [start, middle, end]


def modulation_steps(me, wires, base, conds_ref, weight_ref, columns_ref, mod_ref, first, second, partial, b_sums, a_sums, across_sums):
    swap = swap_steps(me, wires, base, conds_ref, first, second, columns_ref)

    def multiply():
        swap[2]()
        rows = lax.broadcasted_iota(jnp.int32, (8, 32), 0)
        taken = lax.broadcasted_iota(jnp.int32, (8, 32), 1)
        pick = jnp.where(taken == (rows // 2) * 8 + lax.rem(rows, 2), 1.0, 0.0).astype(jnp.bfloat16)
        for kb in range(4):
            found = jnp.concatenate([columns_ref[me.dp((4 - ka) % 4, (4 - kb) % 4)] for ka in range(4)], axis=0)
            silu = (found / (1.0 + jnp.exp(-found))).astype(jnp.bfloat16)
            silu = dot(pick, silu).astype(jnp.bfloat16)
            partial[kb] = dot(silu, weight_ref[...])
        for k in (1, 2, 3):
            wires.push(base + 5 + k, partial.at[k], b_sums.at[k - 1], me.ring(0, 4 - k))

    def add_b():
        for k in (1, 2, 3):
            wires.got(base + 5 + k, b_sums.at[k - 1], me.sibling())
        a_sums[0] = partial[0] + b_sums[0] + b_sums[1] + b_sums[2]
        for k in (1, 2, 3):
            wires.push(base + 8 + k, a_sums.at[0], a_sums.at[k], me.ring(4 - k, 0))

    def add_a():
        for k in (1, 2, 3):
            wires.got(base + 8 + k, a_sums.at[k], me.sibling())
        total = a_sums[0, 0:2]
        for k in (1, 2, 3):
            total = total + a_sums[k, 2 * k : 2 * k + 2]
        across_sums[0] = jnp.concatenate([total, jnp.zeros((6, total.shape[1]), jnp.float32)], axis=0)
        wires.push(base + 12, across_sums.at[0], across_sums.at[1], me.flipped())

    def end():
        wires.got(base + 12, across_sums.at[1], me.sibling())
        lead = me.s == 0
        kept = jnp.where(lead, across_sums[0, 0:1], across_sums[0, 1:2])
        came = jnp.where(lead, across_sums[1, 0:1], across_sums[1, 1:2])
        zeros = jnp.zeros((2, WIDE), jnp.float32)
        for block, row in ((0, jnp.where(lead, kept, came)), (1, jnp.where(lead, came, kept))):
            mod_ref[block] = jnp.concatenate([row[:, r * WIDE : (r + 1) * WIDE] for r in range(6)] + [zeros], axis=0)

    return [swap[0], swap[1], multiply, add_b, add_a, end]


def gather_kernel(p_ref, conds_ref, weight_ref, first_ref, second_ref, columns_ref, mod_ref, shard, c_first, c_second, partial, b_sums, a_sums, across_sums, local, send, recv):
    me = Place()
    mine = p_ref.at[half_rows(me.c, 0, HALF), :]
    own = pltpu.make_async_copy(mine, shard.at[me.s], local.at[2])
    own.start()
    greet(me.grid_peers() + [me.across(), me.flipped(), me.sibling()])
    wires = Wires(send, recv)
    wires.push(0, mine, shard.at[me.s], me.across())
    small = modulation_steps(me, wires, 73, conds_ref, weight_ref, columns_ref, mod_ref, c_first, c_second, partial, b_sums, a_sums, across_sums)
    small[0]()
    small[1]()
    own.wait()
    wires.got(0, shard.at[1 - me.s], me.across())
    one = gather_steps(me, wires, 1, shard.at[0], first_ref, local.at[0])
    two = gather_steps(me, wires, 37, shard.at[1], second_ref, local.at[1])
    one[0]()
    two[0]()
    small[2]()
    one[1]()
    small[3]()
    one[2]()
    two[1]()
    small[4]()
    two[2]()
    small[5]()
    for step in one[3:7] + two[3:7] + one[7:11] + two[7:11] + [one[11], two[11]]:
        step()
    wires.finish()


def gather_weights(packed, conds, weight):
    bf, f32 = jnp.bfloat16, jnp.float32
    wide = weight.shape[1]
    whole = pl.BlockSpec(memory_space=pltpu.VMEM)
    away = pl.BlockSpec(memory_space=pl.ANY)
    return pl.pallas_call(
        gather_kernel,
        out_shape=[
            jax.ShapeDtypeStruct((16, ROWS, WIDE), bf),
            jax.ShapeDtypeStruct((16, ROWS, WIDE), bf),
            jax.ShapeDtypeStruct((16, 8, PAIR), f32),
            jax.ShapeDtypeStruct((2, 8, WIDE), f32),
        ],
        in_specs=[away, whole, whole],
        out_specs=[away, away, whole, whole],
        scratch_shapes=[
            pltpu.VMEM((2, HALF, WIDE), bf),
            pltpu.VMEM((2, 4, 4, 8, PAIR), f32),
            pltpu.VMEM((2, 4, 4, 8, PAIR), f32),
            pltpu.VMEM((4, 8, wide), f32),
            pltpu.VMEM((3, 8, wide), f32),
            pltpu.VMEM((4, 8, wide), f32),
            pltpu.VMEM((2, 8, wide), f32),
            pltpu.SemaphoreType.DMA((3,)),
            pltpu.SemaphoreType.DMA((86,)),
            pltpu.SemaphoreType.DMA((86,)),
        ],
        compiler_params=pltpu.CompilerParams(
            collective_id=0, has_side_effects=True, vmem_limit_bytes=24 * 1024 * 1024
        ),
        cost_estimate=pl.CostEstimate(flops=0, bytes_accessed=60000000, transcendentals=0),
        name="gather_weights",
    )(packed, conds, weight)


def reduce_steps(me, wires, base, source, load, buffers):
    mine, sib, r_top, r_low, r_left, r_right, a_top, a_low, a_left, a_right = buffers
    right_a, left_a = me.ring(1, 0), me.ring(3, 0)
    right_b, left_b = me.ring(0, 1), me.ring(0, 3)
    sibling = me.sibling()

    def push(index, origin, target, device):
        wires.push(base + index, origin, target, device)

    def got(index, target):
        wires.got(base + index, target, sibling)

    def block(ka, kb):
        return mine.at[me.dp(ka, kb)]

    def from_side(ka, kb):
        return sib.at[me.dp(ka, kb)]

    def fetch(ka, kb):
        dp = me.dp(ka, kb)
        return pltpu.make_async_copy(source.at[dp, half_rows(me.c, 0, HALF), :], mine.at[dp], load.at[4 * ka + kb])

    def start():
        for kb in (2, 1, 3, 0):
            for ka in (2, 1, 3, 0):
                fetch(ka, kb).start()
                dp = me.dp(kb, ka)
                push(4 * ka + kb, source.at[dp, half_rows(1 - me.c, 0, HALF), :], sib.at[dp], sibling)

    def total(target, parts, offset=0, count=HALF):
        add_rows(target, parts, offset, count)

    def ready(ka, kb):
        fetch(ka, kb).wait()
        got(4 * ka + kb, from_side(ka, kb))

    def far_b(ka):
        ready(ka, 2)
        far = block(ka, 2)
        total(far, [(from_side(ka, 2), 0)])
        push(16 + 4 * ka, far.at[pl.ds(0, TOP), :], r_top.at[ka], right_b)
        push(17 + 4 * ka, far.at[pl.ds(TOP, LOW), :], r_low.at[ka], left_b)

    def near_b(ka):
        at = 16 + 4 * ka
        ready(ka, 1)
        got(at, r_top.at[ka])
        near, side = block(ka, 1), from_side(ka, 1)
        total(near, [(side, 0), (r_top.at[ka], 0)], 0, TOP)
        total(near, [(side, 0)], TOP, LOW)
        push(at + 2, near, r_left.at[ka], right_b)
        ready(ka, 3)
        got(at + 1, r_low.at[ka])
        near, side = block(ka, 3), from_side(ka, 3)
        total(near, [(side, 0)], 0, TOP)
        total(near, [(side, 0), (r_low.at[ka], TOP)], TOP, LOW)
        push(at + 3, near, r_right.at[ka], left_b)

    def own_b(ka):
        at = 16 + 4 * ka
        ready(ka, 0)
        got(at + 2, r_left.at[ka])
        got(at + 3, r_right.at[ka])
        total(block(ka, 0), [(from_side(ka, 0), 0), (r_left.at[ka], 0), (r_right.at[ka], 0)])
        if ka == 2:
            far = block(2, 0)
            push(32, far.at[pl.ds(0, TOP), :], a_top, right_a)
            push(33, far.at[pl.ds(TOP, LOW), :], a_low, left_a)

    def near_a():
        got(32, a_top)
        total(block(1, 0), [(a_top, 0)], 0, TOP)
        push(34, block(1, 0), a_left, right_a)
        got(33, a_low)
        total(block(3, 0), [(a_low, TOP)], TOP, LOW)
        push(35, block(3, 0), a_right, left_a)

    def own_a():
        got(34, a_left)
        got(35, a_right)
        total(block(0, 0), [(a_left, 0), (a_right, 0)])

    order = (2, 1, 3, 0)
    steps = [start]
    for made in (far_b, near_b, own_b):
        steps += [functools.partial(made, ka) for ka in order]
    return steps + [near_a, own_a]


def add_rows(target, parts, offset=0, count=HALF):
    def step(i, carry):
        rows = pl.ds(pl.multiple_of(offset + 16 * i, 16), 16)
        value = target[rows, :].astype(jnp.float32)
        for part, start in parts:
            value = value + part[pl.ds(pl.multiple_of(offset - start + 16 * i, 16), 16), :].astype(jnp.float32)
        target[rows, :] = value.astype(jnp.bfloat16)
        return carry

    lax.fori_loop(0, count // 16, step, 0)


def terms_steps(me, wires, base, first_ref, second_ref, weight_ref, all_ref, conds_ref, sums, rounded, tiles, c_first, c_second):
    peers = [me.sibling(), me.beside(), me.askew()]

    def start():
        sums[me.q, 0] = first_ref[...]
        sums[me.q, 1] = second_ref[...]
        for k in range(3):
            wires.push(base + k, sums.at[me.q], sums.at[me.q], peers[k], base + k)

    def add():
        for k in range(3):
            wires.got(base + k, sums.at[peers[k][2]], peers[k])
        total = sums[0] + sums[1] + sums[2] + sums[3]
        rounded[...] = total.astype(jnp.bfloat16).astype(jnp.float32)
        all_ref[me.d, me.s] = rounded[me.s]
        wires.push(base + 3, rounded.at[1 - me.s], all_ref.at[me.d, me.s], me.flipped())

    def spread_a():
        wires.got(base + 3, all_ref.at[me.d, 1 - me.s], me.sibling())
        for k in (1, 2, 3):
            wires.push(base + 3 + k, all_ref.at[me.d], all_ref.at[me.d], me.ring(k, 0))

    def spread_b():
        for k in (1, 2, 3):
            wires.got(base + 3 + k, all_ref.at[me.dp(4 - k, 0)], me.sibling())
        for ka in range(4):
            block = all_ref.at[me.dp((4 - ka) % 4, 0)]
            for k in (1, 2, 3):
                wires.push(base + 4 + 3 * ka + 2 + k, block, block, me.ring(0, k))

    def multiply():
        for ka in range(4):
            for k in (1, 2, 3):
                wires.got(base + 4 + 3 * ka + 2 + k, all_ref.at[me.dp((4 - ka) % 4, 4 - k)], me.sibling())
        grads = all_ref[...].reshape(256, WIDE).astype(jnp.bfloat16)
        row = lax.rem(lax.broadcasted_iota(jnp.int32, (256, PAIR), 0), 8)
        total = jnp.zeros((256, PAIR), jnp.float32)
        for r in range(6):
            made = dot(grads, weight_ref[:, r * WIDE : (r + 1) * WIDE], 1, 1)
            total = total + jnp.where(row == r, made, 0.0)
        total = jnp.sum(total.reshape(16, 2, 8, PAIR), axis=2, keepdims=True)
        level = lax.broadcasted_iota(jnp.int32, (16, 8, PAIR), 1)
        tiles[0] = jnp.where(level == 0, total[:, 0], jnp.where(level == 1, total[:, 1], 0.0))
        wires.push(base + 19, tiles.at[0], tiles.at[1], me.flipped())

    def join():
        wires.got(base + 19, tiles.at[1], me.sibling())
        tiles[2] = tiles[0] + tiles[1]
        swap_two[0]()

    swap_two = swap_steps(me, wires, base + 20, tiles.at[2], c_first, c_second, conds_ref)
    return [start, add, spread_a, spread_b, multiply, join, swap_two[1], swap_two[2]]


def reduce_kernel(
    first_ref, second_ref, first_terms, second_terms, weight_ref, kept_out, sent_out, kept_grad, sent_grad,
    o_ref, all_ref, conds_ref, outs_ref, grads_ref,
    mine, sib, r_top, r_low, r_left, r_right, a_top, a_low, a_left, a_right, r_across, r_beside,
    sums, rounded, tiles, c_first, c_second, load, local, send, recv,
):
    me = Place()
    greet(me.grid_peers() + [me.across(), me.flipped(), me.beside(), me.askew(), me.sibling()])
    wires = Wires(send, recv)
    buffers = (mine, sib, r_top, r_low, r_left, r_right, a_top, a_low, a_left, a_right)
    one = reduce_steps(me, wires, 0, second_ref, load.at[1], [ref.at[1] for ref in buffers])
    two = reduce_steps(me, wires, 36, first_ref, load.at[0], [ref.at[0] for ref in buffers])
    small = terms_steps(me, wires, 77, first_terms, second_terms, weight_ref, all_ref, conds_ref, sums, rounded, tiles, c_first, c_second)
    one[0]()
    two[0]()
    small[0]()
    keeps = [
        pltpu.make_async_copy(kept_out, outs_ref.at[me.s], local.at[0]),
        pltpu.make_async_copy(kept_grad, grads_ref.at[me.s], local.at[1]),
    ]
    for item in keeps:
        item.start()
    wires.push(72, sent_out, outs_ref.at[me.s], me.flipped())
    wires.push(73, sent_grad, grads_ref.at[me.s], me.flipped())
    big = one[1:5] + two[1:5] + one[5:9] + two[5:9] + one[9:13] + two[9:13] + [one[13], two[13], one[14], two[14]]
    small = small[1:]
    for index, step in enumerate(big):
        step()
        if index % 3 == 2 and small:
            small.pop(0)()
    while small:
        small.pop(0)()
    held = mine.at[me.s, me.d]
    wires.push(74, mine.at[1 - me.s, me.d], r_across, me.across())
    wires.got(74, r_across, me.across())
    add_rows(held, [(r_across, 0)])
    beside = pltpu.make_async_remote_copy(
        src_ref=held, dst_ref=r_beside, send_sem=send.at[75], recv_sem=recv.at[75], device_id=me.beside(), device_id_type=MESH
    )
    beside.start()
    wires.got(75, r_beside, me.beside())
    beside.wait_send()
    add_rows(held, [(r_beside, 0)])
    out_rows = o_ref.at[half_rows(me.c, 0, HALF), :]
    wires.push(76, held, out_rows, me.sibling())
    own = pltpu.make_async_copy(held, out_rows, local.at[2])
    own.start()
    own.wait()
    for item in keeps:
        item.wait()
    wires.got(72, outs_ref.at[1 - me.s], me.flipped())
    wires.got(73, grads_ref.at[1 - me.s], me.flipped())
    wires.got(76, o_ref.at[half_rows(1 - me.c, 0, HALF), :], me.sibling())
    wires.finish()


def reduce_grads(*operands):
    count = 77 + 26
    bf, f32 = jnp.bfloat16, jnp.float32
    blocks = lambda *lead: pltpu.VMEM(lead + (WIDE,), bf)
    whole = pl.BlockSpec(memory_space=pltpu.VMEM)
    away = pl.BlockSpec(memory_space=pl.ANY)
    return pl.pallas_call(
        reduce_kernel,
        out_shape=[
            jax.ShapeDtypeStruct((ROWS, WIDE), bf),
            jax.ShapeDtypeStruct((16, 2, 8, WIDE), f32),
            jax.ShapeDtypeStruct((16, 8, PAIR), f32),
            jax.ShapeDtypeStruct((2, TOKENS, WIDE), bf),
            jax.ShapeDtypeStruct((2, TOKENS, WIDE), f32),
        ],
        in_specs=[away, away, whole, whole, whole, away, away, away, away],
        out_specs=[away, whole, whole, away, away],
        scratch_shapes=[
            blocks(2, 16, HALF),
            blocks(2, 16, HALF),
            blocks(2, 4, TOP),
            blocks(2, 4, LOW),
            blocks(2, 4, HALF),
            blocks(2, 4, HALF),
            blocks(2, TOP),
            blocks(2, LOW),
            blocks(2, HALF),
            blocks(2, HALF),
            blocks(HALF),
            blocks(HALF),
            pltpu.VMEM((4, 2, 8, WIDE), f32),
            pltpu.VMEM((2, 8, WIDE), f32),
            pltpu.VMEM((3, 16, 8, PAIR), f32),
            pltpu.VMEM((2, 4, 4, 8, PAIR), f32),
            pltpu.VMEM((2, 4, 4, 8, PAIR), f32),
            pltpu.SemaphoreType.DMA((2, 16)),
            pltpu.SemaphoreType.DMA((3,)),
            pltpu.SemaphoreType.DMA((count,)),
            pltpu.SemaphoreType.DMA((count,)),
        ],
        compiler_params=pltpu.CompilerParams(
            collective_id=1, has_side_effects=True, vmem_limit_bytes=57 * 1024 * 1024
        ),
        cost_estimate=pl.CostEstimate(flops=0, bytes_accessed=60000000, transcendentals=0),
        name="reduce_grads",
    )(*operands)


def seq_peers(me):
    far = [(me.s, me.d, (1 - me.xl) * 2 + core) for core in range(2)]
    return me.sibling(), far


def forward_kernel(
    part, x_ref, mod_ref, bias_ref, w_hbm,
    out_ref, mixed_one_ref, qkv_out, lse_ref, att_out, branch_one_ref, middle_ref, mixed_two_ref, expanded_out, branch_two_ref,
    w, stage, qkv, heads, att, expanded, load, save, send, recv,
):
    me = Place()
    sibling, far = seq_peers(me)
    first_load = pltpu.make_async_copy(w_hbm.at[:, pl.ds(0, 144), :], w.at[:, pl.ds(0, 144), :], load.at[0])
    rest_load = pltpu.make_async_copy(w_hbm.at[:, pl.ds(144, 464), :], w.at[:, pl.ds(144, 464), :], load.at[1])
    first_load.start()
    rest_load.start()
    greet([sibling, *far])
    wires = Wires(send, recv)

    row = lambda index: mod_ref[index : index + 1, :]
    bias = lambda index: bias_ref[index : index + 1, :]
    tokens = x_ref[...].astype(jnp.float32)
    normed_one, _ = norm_rows(tokens)
    mixed_one = (normed_one * (1.0 + row(1)) + row(0)).astype(jnp.bfloat16)
    mixed_one_ref[...] = mixed_one
    first_load.wait()

    def project(kind, weight_row, added):
        made = dot(mixed_one, square(w, weight_row))
        if added is not None:
            made = made + added
        made = made.astype(jnp.bfloat16)
        for pair in range(6):
            stage[pair, kind] = made[:, pair * PAIR : (pair + 1) * PAIR]

    project(0, 48, None)
    project(1, 96, bias(1))
    for j in range(3):
        for g in range(2):
            wires.push(2 * j + g, stage.at[3 * g + j, pl.ds(0, 2)], qkv.at[2 + me.c, j, pl.ds(0, 2)], far[g], 2 * j + me.c)
    project(2, 0, bias(0))
    for j in range(3):
        wires.push(6 + j, stage.at[3 * (1 - me.c) + j], qkv.at[me.c, j], sibling)
    for j in range(3):
        qkv[me.c, j] = stage[3 * me.c + j]

    for j in range(3):
        wires.got(6 + j, qkv.at[1 - me.c, j], sibling)
        for g in range(2):
            wires.got(2 * j + g, qkv.at[2 + g, j, pl.ds(0, 2)], far[g])

        def queries_step(g, carry):
            keys = qkv[:, j, 0].reshape(4 * TOKENS, PAIR)
            values = qkv[:, j, 1].reshape(4 * TOKENS, PAIR)
            queries = qkv[g, j, 2] * jnp.bfloat16(0.125)
            made = []
            for head in range(2):
                scores = dot(keys, only_head(queries, head), 1, 1)
                top = jnp.max(scores, axis=0, keepdims=True)
                powers = jnp.exp(scores - top)
                sums = jnp.sum(powers, axis=0, keepdims=True)
                lse_ref[(2 * j + head) * 2 + g] = top + jnp.log(sums)
                weights = (powers * (1.0 / sums)).astype(jnp.bfloat16)
                made.append(dot(values, weights, 0, 0)[head * HEAD : (head + 1) * HEAD])
            heads[g, j] = jnp.concatenate(made, axis=0).T.astype(jnp.bfloat16)
            return carry

        lax.fori_loop(0, 2, queries_step, 0)
        wires.push(9 + j, heads.at[1 - me.c, j], att.at[3 * me.c + j], sibling)
        att[3 * me.c + j] = heads[me.c, j]
    qkv_save = pltpu.make_async_copy(qkv, qkv_out, save.at[0])
    qkv_save.start()
    rest_load.wait()
    for j in range(3):
        wires.got(9 + j, att.at[3 * (1 - me.c) + j], sibling)
    att_save = pltpu.make_async_copy(att, att_out, save.at[1])
    att_save.start()
    attended = side_by_side(att)
    branch_one = dot(attended, square(w, 144)) + bias(2)
    branch_one_ref[...] = branch_one
    middle = tokens + row(2) * branch_one
    middle_ref[...] = middle
    normed_two, _ = norm_rows(middle)
    mixed_two = (normed_two * (1.0 + row(4)) + row(3)).astype(jnp.bfloat16)
    mixed_two_ref[...] = mixed_two
    total = bias(7)
    saves = []
    for k in range(4):
        u = dot(mixed_two, square(w, EXPAND_ROWS[k])) + bias(3 + k)
        expanded[k] = u
        item = pltpu.make_async_copy(expanded.at[k], expanded_out.at[k], save.at[2 + k])
        item.start()
        saves.append(item)
        activated = (0.5 * u * (1.0 + jnp.tanh(ROOT * (u + 0.044715 * (u * u * u))))).astype(jnp.bfloat16)
        total = total + dot(activated, contract_square(w, k))
    branch_two_ref[...] = total
    out_ref[...] = (middle + row(5) * total).astype(jnp.bfloat16)
    qkv_save.wait()
    att_save.wait()
    for item in saves:
        item.wait()
    wires.finish()


def block_forward(part, tokens, modulation, bias, blocks):
    shape = lambda dims, dtype: jax.ShapeDtypeStruct(dims, dtype)
    bf, f32 = jnp.bfloat16, jnp.float32
    whole = pl.BlockSpec(memory_space=pltpu.VMEM)
    away = pl.BlockSpec(memory_space=pl.ANY)
    return pl.pallas_call(
        functools.partial(forward_kernel, part),
        out_shape=[
            shape((TOKENS, WIDE), bf),
            shape((TOKENS, WIDE), bf),
            shape((4, 3, 3, TOKENS, PAIR), bf),
            shape((12, 1, TOKENS), f32),
            shape((6, TOKENS, PAIR), bf),
            shape((TOKENS, WIDE), f32),
            shape((TOKENS, WIDE), f32),
            shape((TOKENS, WIDE), bf),
            shape((4, TOKENS, WIDE), f32),
            shape((TOKENS, WIDE), f32),
        ],
        in_specs=[whole, whole, whole, away],
        out_specs=[whole, whole, away, whole, away, whole, whole, whole, away, whole],
        scratch_shapes=[
            pltpu.VMEM((16, ROWS, WIDE), bf),
            pltpu.VMEM((6, 3, TOKENS, PAIR), bf),
            pltpu.VMEM((4, 3, 3, TOKENS, PAIR), bf),
            pltpu.VMEM((2, 3, TOKENS, PAIR), bf),
            pltpu.VMEM((6, TOKENS, PAIR), bf),
            pltpu.VMEM((4, TOKENS, WIDE), f32),
            pltpu.SemaphoreType.DMA((2,)),
            pltpu.SemaphoreType.DMA((6,)),
            pltpu.SemaphoreType.DMA((12,)),
            pltpu.SemaphoreType.DMA((12,)),
        ],
        compiler_params=pltpu.CompilerParams(
            collective_id=2 + part, has_side_effects=True, vmem_limit_bytes=56 * 1024 * 1024
        ),
        cost_estimate=pl.CostEstimate(flops=5 * 10**9, bytes_accessed=25 * 10**6, transcendentals=4 * 10**6),
        name=("forward_first", "forward_second")[part],
    )(tokens, modulation, bias, blocks)


def backward_kernel(
    part, grad_ref, x_ref, mod_ref, w_hbm, mixed_one_ref, qkv_in, lse_ref, att_ref, branch_one_ref, middle_ref, mixed_two_ref, expanded_in, branch_two_ref,
    input_grad_ref, terms_ref, grads_out,
    w, made, expanded, qkv, stage, given, dkv, dq, own, far_out, far_in, side_out, side_in, joined, load, save, send, recv,
):
    me = Place()
    sibling, far = seq_peers(me)
    c, other = me.c, 1 - me.c
    back_load = pltpu.make_async_copy(w_hbm.at[:, pl.ds(192, 416), :], w.at[:, pl.ds(192, 416), :], load.at[0])
    expanded_load = pltpu.make_async_copy(expanded_in, expanded, load.at[1])
    front_load = pltpu.make_async_copy(w_hbm.at[:, pl.ds(0, 192), :], w.at[:, pl.ds(0, 192), :], load.at[2])
    qkv_load = pltpu.make_async_copy(qkv_in, qkv, load.at[3])
    back_load.start()
    expanded_load.start()
    front_load.start()
    qkv_load.start()
    greet([sibling, *far])
    wires = Wires(send, recv)
    saves = []

    def keep(index, start, count):
        rows = pl.ds(start, count)
        item = pltpu.make_async_copy(made.at[:, rows, :], grads_out.at[:, rows, :], save.at[index])
        item.start()
        saves.append(item)

    row = lambda index: mod_ref[index : index + 1, :]
    gradient = grad_ref[...].astype(jnp.float32)
    branch_two_grad = (row(5) * gradient).astype(jnp.bfloat16)
    gate_two_grad = column_sum(gradient * branch_two_ref[...])
    contract_bias_grad = column_sum(branch_two_grad)
    mixed_two = mixed_two_ref[...]
    mixed_two_grad = None
    expand_bias_grads = []
    back_load.wait()
    expanded_load.wait()
    for k in range(4):
        u = expanded[k]
        squared = u * u
        tanh = jnp.tanh(ROOT * (u + 0.044715 * (squared * u)))
        half = 0.5 * (1.0 + tanh)
        activated = (u * half).astype(jnp.bfloat16)
        slope = half + 0.5 * u * (1.0 - tanh * tanh) * (ROOT * (1.0 + (3.0 * 0.044715) * squared))
        made[4 * k : 4 * k + 4, CONTRACT_ROW : CONTRACT_ROW + 192, :] = (
            dot(activated, branch_two_grad, 0, 0).astype(jnp.bfloat16).reshape(4, 192, WIDE)
        )
        expanded_grad = (dot(branch_two_grad, contract_square(w, k), 1, 1) * slope).astype(jnp.bfloat16)
        start = EXPAND_ROWS[k]
        made[:, start : start + 48, :] = dot(mixed_two, expanded_grad, 0, 0).astype(jnp.bfloat16).reshape(16, 48, WIDE)
        expand_bias_grads.append(column_sum(expanded_grad))
        term = dot(expanded_grad, square(w, start), 1, 1)
        mixed_two_grad = term if mixed_two_grad is None else mixed_two_grad + term
    keep(0, 304, 288)
    keep(1, 192, 96)
    normed_two, inv_two = norm_rows(middle_ref[...])
    scale_two_grad = column_sum(mixed_two_grad * normed_two)
    shift_two_grad = column_sum(mixed_two_grad)
    middle_grad = gradient + norm_back(mixed_two_grad * (1.0 + row(4)), normed_two, inv_two)
    gate_one_grad = column_sum(middle_grad * branch_one_ref[...])
    branch_one_grad = (row(2) * middle_grad).astype(jnp.bfloat16)
    front_load.wait()
    attended_grad = dot(branch_one_grad, square(w, 144), 1, 1).astype(jnp.bfloat16)
    for pair in range(6):
        stage[pair] = attended_grad[:, pair * PAIR : (pair + 1) * PAIR]
    wires.push(0, stage.at[pl.ds(3 * other, 3)], given.at[c], sibling)
    given[c] = stage[pl.ds(3 * c, 3)]
    input_grad_ref[...] = middle_grad
    made[:, 144:192, :] = dot(side_by_side(att_ref), branch_one_grad, 0, 0).astype(jnp.bfloat16).reshape(16, 48, WIDE)
    keep(2, 144, 48)
    attention_bias_grad = column_sum(branch_one_grad)
    qkv_load.wait()
    wires.got(0, given.at[other], sibling)

    for j in range(3):
        dkv[...] = jnp.zeros_like(dkv)

        def queries_step(g, carry):
            keys = qkv[:, j, 0].reshape(4 * TOKENS, PAIR)
            values = qkv[:, j, 1].reshape(4 * TOKENS, PAIR)
            queries = qkv[g, j, 2] * jnp.bfloat16(0.125)
            output_grads = given[g, j]
            key_sums, value_sums, query_parts = 0.0, 0.0, []
            for head in range(2):
                head_queries = only_head(queries, head)
                head_grads = only_head(output_grads, head)
                scores = dot(keys, head_queries, 1, 1)
                probs = jnp.exp(scores - lse_ref[(2 * j + head) * 2 + g])
                weight_grads = dot(values, head_grads, 1, 1)
                centre = jnp.sum(probs * weight_grads, axis=0, keepdims=True)
                score_grads = (probs * (weight_grads - centre)).astype(jnp.bfloat16)
                key_sums = key_sums + dot(score_grads, head_queries)
                value_sums = value_sums + dot(probs.astype(jnp.bfloat16), head_grads)
                query_parts.append(dot(keys, score_grads, 0, 0)[head * HEAD : (head + 1) * HEAD])
            dq[g] = jnp.concatenate(query_parts, axis=0).T * 0.125
            dkv[0] += key_sums.reshape(4, TOKENS, PAIR)
            dkv[1] += value_sums.reshape(4, TOKENS, PAIR)
            return carry

        lax.fori_loop(0, 2, queries_step, 0)
        for g in range(2):
            far_out[j, g] = dkv[:, 2 + g].astype(jnp.bfloat16)
            wires.push(1 + 2 * j + g, far_out.at[j, g], far_in.at[j, c], far[g], 1 + 2 * j + c)
        side_out[j, 0:2] = dkv[:, other].astype(jnp.bfloat16)
        side_out[j, 2] = dq[other].astype(jnp.bfloat16)
        wires.push(7 + j, side_out.at[j], side_in.at[j], sibling)
        own[j, 0:2] = dkv[:, c]
        own[j, 2] = dq[c]

    for j in range(3):
        wires.got(7 + j, side_in.at[j], sibling)
        for g in range(2):
            wires.got(1 + 2 * j + g, far_in.at[j, g], far[g])
        for kind in range(2):
            joined[kind, 3 * c + j] = (own[j, kind] + far_in[j, c, kind].astype(jnp.float32)).astype(jnp.bfloat16)
            joined[kind, 3 * other + j] = (
                side_in[j, kind].astype(jnp.float32) + far_in[j, other, kind].astype(jnp.float32)
            ).astype(jnp.bfloat16)
        joined[2, 3 * c + j] = own[j, 2].astype(jnp.bfloat16)
        joined[2, 3 * other + j] = side_in[j, 2]
    mixed_one = mixed_one_ref[...]
    mixed_one_grad, bias_grads = None, []
    for kind, start in ((0, 48), (1, 96), (2, 0)):
        piece = side_by_side(joined, (kind,))
        bias_grads.append(column_sum(piece))
        made[:, start : start + 48, :] = dot(mixed_one, piece, 0, 0).astype(jnp.bfloat16).reshape(16, 48, WIDE)
        term = dot(piece, square(w, start), 1, 1)
        mixed_one_grad = term if mixed_one_grad is None else mixed_one_grad + term
    keep(3, 0, 144)
    small = jnp.concatenate(
        [
            bias_grads[2],
            bias_grads[1],
            attention_bias_grad,
            *expand_bias_grads,
            contract_bias_grad,
            jnp.zeros((8, WIDE), jnp.float32),
        ],
        axis=0,
    ).astype(jnp.bfloat16)
    made[:, BIAS_ROW : BIAS_ROW + 16, :] = jnp.broadcast_to(small[None], (16, 16, WIDE))
    made[:, 592:608, :] = jnp.zeros((16, 16, WIDE), jnp.bfloat16)
    keep(4, BIAS_ROW, 16)
    keep(5, 592, 16)
    normed_one, inv_one = norm_rows(x_ref[...].astype(jnp.float32))
    terms_ref[...] = jnp.concatenate(
        [
            column_sum(mixed_one_grad),
            column_sum(mixed_one_grad * normed_one),
            gate_one_grad,
            shift_two_grad,
            scale_two_grad,
            gate_two_grad,
            jnp.zeros((2, WIDE), jnp.float32),
        ],
        axis=0,
    )
    input_grad_ref[...] += norm_back(mixed_one_grad * (1.0 + row(1)), normed_one, inv_one)
    for item in saves:
        item.wait()
    wires.finish()


def block_backward(part, gradient, tokens, modulation, blocks, kept):
    shape = lambda dims, dtype: jax.ShapeDtypeStruct(dims, dtype)
    bf, f32 = jnp.bfloat16, jnp.float32
    whole = pl.BlockSpec(memory_space=pltpu.VMEM)
    away = pl.BlockSpec(memory_space=pl.ANY)
    return pl.pallas_call(
        functools.partial(backward_kernel, part),
        out_shape=[
            shape((TOKENS, WIDE), f32),
            shape((8, WIDE), f32),
            shape((16, ROWS, WIDE), bf),
        ],
        in_specs=[whole, whole, whole, away, whole, away, whole, whole, whole, whole, whole, away, whole],
        out_specs=[whole, whole, away],
        scratch_shapes=[
            pltpu.VMEM((16, ROWS, WIDE), bf),
            pltpu.VMEM((16, ROWS, WIDE), bf),
            pltpu.VMEM((4, TOKENS, WIDE), f32),
            pltpu.VMEM((4, 3, 3, TOKENS, PAIR), bf),
            pltpu.VMEM((6, TOKENS, PAIR), bf),
            pltpu.VMEM((2, 3, TOKENS, PAIR), bf),
            pltpu.VMEM((2, 4, TOKENS, PAIR), f32),
            pltpu.VMEM((2, TOKENS, PAIR), f32),
            pltpu.VMEM((3, 3, TOKENS, PAIR), f32),
            pltpu.VMEM((3, 2, 2, TOKENS, PAIR), bf),
            pltpu.VMEM((3, 2, 2, TOKENS, PAIR), bf),
            pltpu.VMEM((3, 3, TOKENS, PAIR), bf),
            pltpu.VMEM((3, 3, TOKENS, PAIR), bf),
            pltpu.VMEM((3, 6, TOKENS, PAIR), bf),
            pltpu.SemaphoreType.DMA((4,)),
            pltpu.SemaphoreType.DMA((6,)),
            pltpu.SemaphoreType.DMA((10,)),
            pltpu.SemaphoreType.DMA((10,)),
        ],
        compiler_params=pltpu.CompilerParams(
            collective_id=4 + part, has_side_effects=True, vmem_limit_bytes=58 * 1024 * 1024
        ),
        cost_estimate=pl.CostEstimate(flops=12 * 10**9, bytes_accessed=45 * 10**6, transcendentals=4 * 10**6),
        name=("backward_first", "backward_second")[part],
    )(gradient, tokens, modulation, blocks, *kept)


def pack_weights(projection, attention, expand, contract, biases):
    fill = jnp.zeros((WIDE - biases.shape[0],), jnp.bfloat16)
    columns = lambda weight: weight.reshape(48, -1, WIDE).swapaxes(0, 1).reshape(-1, WIDE)
    return jnp.concatenate(
        [
            columns(projection),
            attention,
            columns(expand[:, : 2 * WIDE]),
            jnp.concatenate([biases, fill])[None],
            jnp.zeros((15, WIDE), jnp.bfloat16),
            columns(expand[:, 2 * WIDE :]),
            contract,
            jnp.zeros((16, WIDE), jnp.bfloat16),
        ]
    )


def bias_rows(biases):
    query_value = biases[:, :, :96].reshape(2, 2, WIDE)
    attention = biases[:, :, 96:144].reshape(2, 1, WIDE)
    expand = biases[:, :, 144:336].reshape(2, 4, WIDE)
    contract = biases[:, :, 336:384].reshape(2, 1, WIDE)
    return jnp.concatenate([query_value, attention, expand, contract], axis=1)


def unpack_grads(rows, place):
    columns = lambda part: part.reshape(-1, 48, WIDE).swapaxes(0, 1).reshape(48, -1)
    own = lambda part, size: lax.dynamic_slice_in_dim(part.reshape(-1), place * size, size)
    bias = rows[BIAS_ROW : BIAS_ROW + 8]
    return [
        columns(rows[:144]),
        own(bias[0:2], 96),
        rows[144:192],
        own(bias[2:3], 48),
        columns(jnp.concatenate([rows[192:288], rows[304:400]])),
        own(bias[3:7], 192),
        rows[400:592],
        own(bias[7:8], 48),
    ]


def on_device(
    latents,
    conditions,
    output_cotangent,
    modulation_weight,
    modulation_bias,
    projection_weight,
    projection_bias,
    attention_weight,
    attention_bias,
    expand_weight,
    expand_bias,
    contract_weight,
    contract_bias,
):
    section = lax.axis_index("section")
    place = lax.axis_index("dp")
    is_first = section == 0
    biases = jnp.concatenate(
        [projection_bias[0], attention_bias[0], expand_bias[0], contract_bias[0], modulation_bias[0]]
    )
    packed = pack_weights(projection_weight[0], attention_weight[0], expand_weight[0], contract_weight[0], biases)
    pieces = jnp.pad(conditions[:, 0].reshape(2, 16, 48).swapaxes(0, 1), ((0, 0), (0, 6), (0, PAIR - 48)))
    owned_weight = jnp.pad(modulation_weight[0], ((0, PAIR - 48), (0, 0)))
    first_blocks, second_blocks, own_conds, modulations = gather_weights(packed, pieces, owned_weight)
    biases = jnp.stack([first_blocks[:, BIAS_ROW], second_blocks[:, BIAS_ROW]]).astype(jnp.float32)
    added = jnp.pad(biases[:, :, 384:672].reshape(2, 6, WIDE), ((0, 0), (0, 2), (0, 0)))
    modulations = modulations + added
    bias = bias_rows(biases)

    tokens = lax.dynamic_index_in_dim(latents, section, 0, keepdims=False)[0]
    cotangent = lax.dynamic_index_in_dim(output_cotangent, section, 0, keepdims=False)[0]
    first_output, *first_kept = block_forward(0, tokens, modulations[0], bias[0], first_blocks)
    second_output, *second_kept = block_forward(1, first_output, modulations[1], bias[1], second_blocks)
    second_grad, second_terms, second_made = block_backward(
        1, cotangent, first_output, modulations[1], second_blocks, second_kept
    )
    second_grad = second_grad.astype(jnp.bfloat16)
    first_grad, first_terms, first_made = block_backward(0, second_grad, tokens, modulations[0], first_blocks, first_kept)

    rounded_grad = second_grad.astype(jnp.float32)
    rows, terms, cond_terms, section_outputs, input_grads = reduce_grads(
        first_made,
        second_made,
        first_terms,
        second_terms,
        owned_weight,
        jnp.where(is_first, first_output, second_output),
        jnp.where(is_first, second_output, first_output),
        jnp.where(is_first, first_grad, rounded_grad),
        jnp.where(is_first, rounded_grad, first_grad),
    )
    reduced = [grad[None] for grad in unpack_grads(rows.astype(jnp.float32), place)]
    section_outputs = section_outputs[None, :, None]
    input_grads = input_grads[None, :, None]
    terms = terms[:, :, :6].reshape(16, 2, -1)
    own_silu = jax.nn.silu(own_conds[:, :2, :48]).astype(jnp.bfloat16)
    modulation_weight_grad = jnp.einsum(
        "imk,ime->ke", own_silu, terms.astype(jnp.bfloat16), preferred_element_type=jnp.float32
    )
    modulation_bias_grad = lax.dynamic_slice_in_dim(jnp.sum(terms, axis=(0, 1)), place * 288, 288)
    cond_terms = cond_terms[:, :2, :48].swapaxes(0, 1).reshape(2, 1, WIDE)
    condition_grads = jax.vjp(jax.nn.silu, conditions)[1](cond_terms)[0]
    return (
        section_outputs,
        input_grads,
        condition_grads,
        modulation_weight_grad[None],
        modulation_bias_grad[None],
        *reduced,
    )


def solution(mesh):
    return jax.shard_map(
        on_device,
        mesh=mesh,
        in_specs=(
            P(None, "dp", "seq", None),
            P(None, "dp", None),
            P(None, "dp", "seq", None),
            P("section", "dp", None),
            P("section", "dp"),
            P("section", "dp", None),
            P("section", "dp"),
            P("section", "dp", None),
            P("section", "dp"),
            P("section", "dp", None),
            P("section", "dp"),
            P("section", "dp", None),
            P("section", "dp"),
        ),
        out_specs=(
            P("section", None, "dp", "seq", None),
            P("section", None, "dp", "seq", None),
            P(None, "dp", None),
            P("section", "dp", None),
            P("section", "dp"),
            P("section", "dp", None),
            P("section", "dp"),
            P("section", "dp", None),
            P("section", "dp"),
            P("section", "dp", None),
            P("section", "dp"),
            P("section", "dp", None),
            P("section", "dp"),
        ),
        check_vma=False,
    )
```

```python
import functools

import jax
import jax.numpy as jnp
from jax import lax
from jax.experimental import pallas as pl
from jax.experimental.pallas import tpu as pltpu
from jax.sharding import PartitionSpec as P

HEAD = 64


MESH = pl.DeviceIdType.MESH
ROWS = 608
HALF = ROWS // 2
TOP = 160
LOW = HALF - TOP
WIDE = 768
OFFSETS = (0, 3, 1, 2)


class Place:
    def __init__(self):
        self.s = lax.axis_index("section")
        self.d = lax.axis_index("dp")
        self.q = lax.axis_index("seq")
        y, z = self.d // 4, lax.rem(self.d, 4)
        self.xl, self.c = self.q // 2, lax.rem(self.q, 2)
        self.a = (1 - self.c) * z + self.c * y
        self.b = (1 - self.c) * y + self.c * z

    def dp(self, ka, kb):
        aa = lax.rem(self.a + ka, 4)
        bb = lax.rem(self.b + kb, 4)
        return aa * (1 + 3 * self.c) + bb * (4 - 3 * self.c)

    def ring(self, ka, kb):
        return (self.s, self.dp(ka, kb), self.q)

    def sibling(self):
        return (self.s, self.d, self.xl * 2 + 1 - self.c)

    def across(self):
        return (1 - self.s, self.d, (1 - self.xl) * 2 + self.c)

    def beside(self):
        return (self.s, self.d, (1 - self.xl) * 2 + self.c)

    def askew(self):
        return (self.s, self.d, (1 - self.xl) * 2 + 1 - self.c)

    def flipped(self):
        return (1 - self.s, self.d, self.q)

    def grid_peers(self):
        return [self.ring(k, 0) for k in (1, 3, 2)] + [self.ring(0, k) for k in (1, 3, 2)]


def greet(devices):
    barrier = pltpu.get_barrier_semaphore()
    for device in devices:
        pl.semaphore_signal(barrier, inc=1, device_id=device, device_id_type=MESH)
    pl.semaphore_wait(barrier, len(devices))


def half_rows(core, offset, count):
    return pl.ds(pl.multiple_of(core * HALF + offset, 16), count)


class Wires:
    def __init__(self, send, recv):
        self.send, self.recv, self.started = send, recv, []

    def push(self, index, source, target, device, landing=None):
        item = pltpu.make_async_remote_copy(
            src_ref=source,
            dst_ref=target,
            send_sem=self.send.at[index],
            recv_sem=self.recv.at[index if landing is None else landing],
            device_id=device,
            device_id_type=MESH,
        )
        item.start()
        self.started.append(item)

    def got(self, index, target, device):
        pltpu.make_async_remote_copy(
            src_ref=target,
            dst_ref=target,
            send_sem=self.send.at[0],
            recv_sem=self.recv.at[index],
            device_id=device,
            device_id_type=MESH,
        ).wait_recv()

    def finish(self):
        for item in self.started:
            item.wait_send()


TOKENS = 256
PAIR = 128
EXPAND_ROWS = (192, 240, 304, 352)
CONTRACT_ROW = 400
BIAS_ROW = 288
ROOT = (2.0 / 3.141592653589793) ** 0.5


def norm_rows(values):
    row_mean = jnp.mean(values, axis=-1, keepdims=True)
    centered = values - row_mean
    variance = jnp.mean(centered * centered, axis=-1, keepdims=True)
    inv_std = lax.rsqrt(variance + 1e-06)
    return (centered * inv_std, inv_std)


def norm_back(gradient, normed, inv_std):
    row_mean = jnp.mean(gradient, axis=-1, keepdims=True)
    along = jnp.mean(gradient * normed, axis=-1, keepdims=True)
    return inv_std * (gradient - row_mean - normed * along)


def dot(left, right, left_dim=1, right_dim=0):
    return lax.dot_general(
        left, right, (((left_dim,), (right_dim,)), ((), ())), preferred_element_type=jnp.float32
    )


def column_sum(values):
    return jnp.sum(values.astype(jnp.float32), axis=0, keepdims=True)


def square(w, row):
    return w[:, row : row + 48, :].reshape(WIDE, WIDE)


def contract_square(w, part):
    return w[4 * part : 4 * part + 4, CONTRACT_ROW : CONTRACT_ROW + 192, :].reshape(WIDE, WIDE)


def side_by_side(ref, lead=()):
    return jnp.concatenate([ref[(*lead, pair)] for pair in range(6)], axis=1)


def head_lanes(head):
    lane = lax.broadcasted_iota(jnp.int32, (1, PAIR), 1)
    return (lane // HEAD) == head


def only_head(values, head):
    return jnp.where(head_lanes(head), values, jnp.zeros_like(values))


def gather_steps(me, wires, base, source, w_ref, local):
    right_a, left_a = me.ring(1, 0), me.ring(3, 0)
    right_b, left_b = me.ring(0, 1), me.ring(0, 3)
    sibling = me.sibling()

    def slot(ka, kb, offset=0, count=HALF):
        return w_ref.at[me.dp(ka, kb), half_rows(me.c, offset, count), :]

    def got(index, target):
        wires.got(base + index, target, sibling)

    def push(index, origin, target, device):
        wires.push(base + index, origin, target, device)

    def to_side(ka, kb, origin=None):
        block = slot(ka, kb)
        push(20 + 4 * ka + kb, block if origin is None else origin, block, sibling)

    def spread_b(ka, origin=None):
        block = slot(ka, 0)
        origin = block if origin is None else origin
        push(4 + 4 * ka, origin, block, right_b)
        push(5 + 4 * ka, origin, block, left_b)

    own = pltpu.make_async_copy(source, slot(0, 0), local)

    def start():
        own.start()
        push(0, source, slot(0, 0), right_a)
        push(1, source, slot(0, 0), left_a)
        spread_b(0, source)
        to_side(0, 0, source)

    def forward_a():
        got(0, slot(3, 0))
        push(2, slot(3, 0, 0, TOP), slot(3, 0, 0, TOP), right_a)
        spread_b(3)
        to_side(3, 0)
        got(1, slot(1, 0))
        push(3, slot(1, 0, TOP, LOW), slot(1, 0, TOP, LOW), left_a)
        spread_b(1)
        to_side(1, 0)

    def end_a():
        got(2, slot(2, 0, 0, TOP))
        got(3, slot(2, 0, TOP, LOW))
        spread_b(2)
        to_side(2, 0)

    def forward_b(ka):
        at = 4 + 4 * ka
        got(at, slot(ka, 3))
        push(at + 2, slot(ka, 3, 0, TOP), slot(ka, 3, 0, TOP), right_b)
        to_side(ka, 3)
        got(at + 1, slot(ka, 1))
        push(at + 3, slot(ka, 1, TOP, LOW), slot(ka, 1, TOP, LOW), left_b)
        to_side(ka, 1)

    def end_b(ka):
        at = 4 + 4 * ka
        got(at + 2, slot(ka, 2, 0, TOP))
        got(at + 3, slot(ka, 2, TOP, LOW))
        to_side(ka, 2)

    def finish():
        own.wait()
        for ka in range(4):
            for kb in range(4):
                got(20 + 4 * ka + kb, w_ref.at[me.dp(kb, ka), half_rows(1 - me.c, 0, HALF), :])

    steps = [start, forward_a, end_a]
    steps += [functools.partial(forward_b, ka) for ka in OFFSETS]
    steps += [functools.partial(end_b, ka) for ka in OFFSETS]
    return steps + [finish]


def swap_steps(me, wires, base, pieces, first, second, result):
    def start():
        for ka in range(4):
            for kb in range(4):
                first[0, ka, kb] = pieces[me.dp(ka, kb)]
        for k in (1, 2, 3):
            wires.push(base + k - 1, first.at[0, k], first.at[1, k], me.ring(k, 0))

    def middle():
        for kb in range(4):
            second[0, kb, 0] = first[0, 0, kb]
        for k in (1, 2, 3):
            wires.got(base + k - 1, first.at[1, k], me.sibling())
            for kb in range(4):
                second[0, kb, k] = first[1, k, kb]
        for k in (1, 2, 3):
            wires.push(base + 2 + k, second.at[0, k], second.at[1, k], me.ring(0, k))

    def end():
        for ka in range(4):
            result[me.dp((4 - ka) % 4, 0)] = second[0, 0, ka]
        for k in (1, 2, 3):
            wires.got(base + 2 + k, second.at[1, k], me.sibling())
            for ka in range(4):
                result[me.dp((4 - ka) % 4, 4 - k)] = second[1, k, ka]

    return [start, middle, end]


def modulation_steps(me, wires, base, conds_ref, weight_ref, columns_ref, mod_ref, first, second, partial, b_sums, a_sums, across_sums):
    swap = swap_steps(me, wires, base, conds_ref, first, second, columns_ref)

    def multiply():
        swap[2]()
        rows = lax.broadcasted_iota(jnp.int32, (8, 32), 0)
        taken = lax.broadcasted_iota(jnp.int32, (8, 32), 1)
        pick = jnp.where(taken == (rows // 2) * 8 + lax.rem(rows, 2), 1.0, 0.0).astype(jnp.bfloat16)
        for kb in range(4):
            found = jnp.concatenate([columns_ref[me.dp((4 - ka) % 4, (4 - kb) % 4)] for ka in range(4)], axis=0)
            silu = (found / (1.0 + jnp.exp(-found))).astype(jnp.bfloat16)
            silu = dot(pick, silu).astype(jnp.bfloat16)
            partial[kb] = dot(silu, weight_ref[...])
        for k in (1, 2, 3):
            wires.push(base + 5 + k, partial.at[k], b_sums.at[k - 1], me.ring(0, 4 - k))

    def add_b():
        for k in (1, 2, 3):
            wires.got(base + 5 + k, b_sums.at[k - 1], me.sibling())
        a_sums[0] = partial[0] + b_sums[0] + b_sums[1] + b_sums[2]
        for k in (1, 2, 3):
            wires.push(base + 8 + k, a_sums.at[0], a_sums.at[k], me.ring(4 - k, 0))

    def add_a():
        for k in (1, 2, 3):
            wires.got(base + 8 + k, a_sums.at[k], me.sibling())
        total = a_sums[0, 0:2]
        for k in (1, 2, 3):
            total = total + a_sums[k, 2 * k : 2 * k + 2]
        across_sums[0] = jnp.concatenate([total, jnp.zeros((6, total.shape[1]), jnp.float32)], axis=0)
        wires.push(base + 12, across_sums.at[0], across_sums.at[1], me.flipped())

    def end():
        wires.got(base + 12, across_sums.at[1], me.sibling())
        lead = me.s == 0
        kept = jnp.where(lead, across_sums[0, 0:1], across_sums[0, 1:2])
        came = jnp.where(lead, across_sums[1, 0:1], across_sums[1, 1:2])
        zeros = jnp.zeros((2, WIDE), jnp.float32)
        for block, row in ((0, jnp.where(lead, kept, came)), (1, jnp.where(lead, came, kept))):
            mod_ref[block] = jnp.concatenate([row[:, r * WIDE : (r + 1) * WIDE] for r in range(6)] + [zeros], axis=0)

    return [swap[0], swap[1], multiply, add_b, add_a, end]


def gather_kernel(p_ref, conds_ref, weight_ref, first_ref, shard_out, columns_ref, mod_ref, shard, c_first, c_second, partial, b_sums, a_sums, across_sums, local, send, recv):
    me = Place()
    mine = p_ref.at[half_rows(me.c, 0, HALF), :]
    own = pltpu.make_async_copy(mine, shard.at[me.s], local.at[2])
    own.start()
    greet(me.grid_peers() + [me.across(), me.flipped(), me.sibling()])
    wires = Wires(send, recv)
    wires.push(0, mine, shard.at[me.s], me.across())
    small = modulation_steps(me, wires, 37, conds_ref, weight_ref, columns_ref, mod_ref, c_first, c_second, partial, b_sums, a_sums, across_sums)
    small[0]()
    small[1]()
    own.wait()
    wires.got(0, shard.at[1 - me.s], me.across())
    handed = pltpu.make_async_copy(shard.at[1], shard_out, local.at[1])
    handed.start()
    one = gather_steps(me, wires, 1, shard.at[0], first_ref, local.at[0])
    one[0]()
    small[2]()
    one[1]()
    one[2]()
    small[3]()
    one[3]()
    one[4]()
    small[4]()
    one[5]()
    one[6]()
    small[5]()
    for step in one[7:]:
        step()
    handed.wait()
    wires.finish()


def gather_weights(packed, conds, weight):
    bf, f32 = jnp.bfloat16, jnp.float32
    wide = weight.shape[1]
    whole = pl.BlockSpec(memory_space=pltpu.VMEM)
    away = pl.BlockSpec(memory_space=pl.ANY)
    return pl.pallas_call(
        gather_kernel,
        out_shape=[
            jax.ShapeDtypeStruct((16, ROWS, WIDE), bf),
            jax.ShapeDtypeStruct((HALF, WIDE), bf),
            jax.ShapeDtypeStruct((16, 8, PAIR), f32),
            jax.ShapeDtypeStruct((2, 8, WIDE), f32),
        ],
        in_specs=[away, whole, whole],
        out_specs=[away, away, whole, whole],
        scratch_shapes=[
            pltpu.VMEM((2, HALF, WIDE), bf),
            pltpu.VMEM((2, 4, 4, 8, PAIR), f32),
            pltpu.VMEM((2, 4, 4, 8, PAIR), f32),
            pltpu.VMEM((4, 8, wide), f32),
            pltpu.VMEM((3, 8, wide), f32),
            pltpu.VMEM((4, 8, wide), f32),
            pltpu.VMEM((2, 8, wide), f32),
            pltpu.SemaphoreType.DMA((3,)),
            pltpu.SemaphoreType.DMA((50,)),
            pltpu.SemaphoreType.DMA((50,)),
        ],
        compiler_params=pltpu.CompilerParams(
            collective_id=0, has_side_effects=True, vmem_limit_bytes=24 * 1024 * 1024
        ),
        cost_estimate=pl.CostEstimate(flops=0, bytes_accessed=60000000, transcendentals=0),
        name="gather_weights",
    )(packed, conds, weight)


def reduce_steps(me, wires, base, source, load, buffers):
    mine, sib, r_top, r_low, r_left, r_right, a_top, a_low, a_left, a_right = buffers
    right_a, left_a = me.ring(1, 0), me.ring(3, 0)
    right_b, left_b = me.ring(0, 1), me.ring(0, 3)
    sibling = me.sibling()

    def push(index, origin, target, device):
        wires.push(base + index, origin, target, device)

    def got(index, target):
        wires.got(base + index, target, sibling)

    def block(ka, kb):
        return mine.at[me.dp(ka, kb)]

    def from_side(ka, kb):
        return sib.at[me.dp(ka, kb)]

    def fetch(ka, kb):
        dp = me.dp(ka, kb)
        return pltpu.make_async_copy(source.at[dp, half_rows(me.c, 0, HALF), :], mine.at[dp], load.at[4 * ka + kb])

    def start():
        for kb in (2, 1, 3, 0):
            for ka in (2, 1, 3, 0):
                fetch(ka, kb).start()
                dp = me.dp(kb, ka)
                push(4 * ka + kb, source.at[dp, half_rows(1 - me.c, 0, HALF), :], sib.at[dp], sibling)

    def total(target, parts, offset=0, count=HALF):
        add_rows(target, parts, offset, count)

    def ready(ka, kb):
        fetch(ka, kb).wait()
        got(4 * ka + kb, from_side(ka, kb))

    def far_b(ka):
        ready(ka, 2)
        far = block(ka, 2)
        total(far, [(from_side(ka, 2), 0)])
        push(16 + 4 * ka, far.at[pl.ds(0, TOP), :], r_top.at[ka], right_b)
        push(17 + 4 * ka, far.at[pl.ds(TOP, LOW), :], r_low.at[ka], left_b)

    def near_b(ka):
        at = 16 + 4 * ka
        ready(ka, 1)
        got(at, r_top.at[ka])
        near, side = block(ka, 1), from_side(ka, 1)
        total(near, [(side, 0), (r_top.at[ka], 0)], 0, TOP)
        total(near, [(side, 0)], TOP, LOW)
        push(at + 2, near, r_left.at[ka], right_b)
        ready(ka, 3)
        got(at + 1, r_low.at[ka])
        near, side = block(ka, 3), from_side(ka, 3)
        total(near, [(side, 0)], 0, TOP)
        total(near, [(side, 0), (r_low.at[ka], TOP)], TOP, LOW)
        push(at + 3, near, r_right.at[ka], left_b)

    def own_b(ka):
        at = 16 + 4 * ka
        ready(ka, 0)
        got(at + 2, r_left.at[ka])
        got(at + 3, r_right.at[ka])
        total(block(ka, 0), [(from_side(ka, 0), 0), (r_left.at[ka], 0), (r_right.at[ka], 0)])
        if ka == 2:
            far = block(2, 0)
            push(32, far.at[pl.ds(0, TOP), :], a_top, right_a)
            push(33, far.at[pl.ds(TOP, LOW), :], a_low, left_a)

    def near_a():
        got(32, a_top)
        total(block(1, 0), [(a_top, 0)], 0, TOP)
        push(34, block(1, 0), a_left, right_a)
        got(33, a_low)
        total(block(3, 0), [(a_low, TOP)], TOP, LOW)
        push(35, block(3, 0), a_right, left_a)

    def own_a():
        got(34, a_left)
        got(35, a_right)
        total(block(0, 0), [(a_left, 0), (a_right, 0)])

    order = (2, 1, 3, 0)
    steps = [start]
    for made in (far_b, near_b, own_b):
        steps += [functools.partial(made, ka) for ka in order]
    return steps + [near_a, own_a]


def add_rows(target, parts, offset=0, count=HALF):
    def step(i, carry):
        rows = pl.ds(pl.multiple_of(offset + 16 * i, 16), 16)
        value = target[rows, :].astype(jnp.float32)
        for part, start in parts:
            value = value + part[pl.ds(pl.multiple_of(offset - start + 16 * i, 16), 16), :].astype(jnp.float32)
        target[rows, :] = value.astype(jnp.bfloat16)
        return carry

    lax.fori_loop(0, count // 16, step, 0)


def terms_steps(me, wires, base, first_ref, second_ref, weight_ref, all_ref, conds_ref, sums, rounded, tiles, c_first, c_second):
    peers = [me.sibling(), me.beside(), me.askew()]

    def start():
        sums[me.q, 0] = first_ref[...]
        sums[me.q, 1] = second_ref[...]
        for k in range(3):
            wires.push(base + k, sums.at[me.q], sums.at[me.q], peers[k], base + k)

    def add():
        for k in range(3):
            wires.got(base + k, sums.at[peers[k][2]], peers[k])
        total = sums[0] + sums[1] + sums[2] + sums[3]
        rounded[...] = total.astype(jnp.bfloat16).astype(jnp.float32)
        all_ref[me.d, me.s] = rounded[me.s]
        wires.push(base + 3, rounded.at[1 - me.s], all_ref.at[me.d, me.s], me.flipped())

    def spread_a():
        wires.got(base + 3, all_ref.at[me.d, 1 - me.s], me.sibling())
        for k in (1, 2, 3):
            wires.push(base + 3 + k, all_ref.at[me.d], all_ref.at[me.d], me.ring(k, 0))

    def spread_b():
        for k in (1, 2, 3):
            wires.got(base + 3 + k, all_ref.at[me.dp(4 - k, 0)], me.sibling())
        for ka in range(4):
            block = all_ref.at[me.dp((4 - ka) % 4, 0)]
            for k in (1, 2, 3):
                wires.push(base + 4 + 3 * ka + 2 + k, block, block, me.ring(0, k))

    def multiply():
        for ka in range(4):
            for k in (1, 2, 3):
                wires.got(base + 4 + 3 * ka + 2 + k, all_ref.at[me.dp((4 - ka) % 4, 4 - k)], me.sibling())
        grads = all_ref[...].reshape(256, WIDE).astype(jnp.bfloat16)
        row = lax.rem(lax.broadcasted_iota(jnp.int32, (256, PAIR), 0), 8)
        total = jnp.zeros((256, PAIR), jnp.float32)
        for r in range(6):
            made = dot(grads, weight_ref[:, r * WIDE : (r + 1) * WIDE], 1, 1)
            total = total + jnp.where(row == r, made, 0.0)
        total = jnp.sum(total.reshape(16, 2, 8, PAIR), axis=2, keepdims=True)
        level = lax.broadcasted_iota(jnp.int32, (16, 8, PAIR), 1)
        tiles[0] = jnp.where(level == 0, total[:, 0], jnp.where(level == 1, total[:, 1], 0.0))
        wires.push(base + 19, tiles.at[0], tiles.at[1], me.flipped())

    def join():
        wires.got(base + 19, tiles.at[1], me.sibling())
        tiles[2] = tiles[0] + tiles[1]
        swap_two[0]()

    swap_two = swap_steps(me, wires, base + 20, tiles.at[2], c_first, c_second, conds_ref)
    return [start, add, spread_a, spread_b, multiply, join, swap_two[1], swap_two[2]]


def reduce_kernel(
    first_ref, second_rows, first_terms, second_terms, weight_ref, kept_out, sent_out, kept_grad, sent_grad,
    o_ref, all_ref, conds_ref, outs_ref, grads_ref,
    mine, sib, r_top, r_low, r_left, r_right, a_top, a_low, a_left, a_right, final, r_across, r_beside,
    sums, rounded, tiles, c_first, c_second, load, local, send, recv,
):
    me = Place()
    greet(me.grid_peers() + [me.across(), me.flipped(), me.beside(), me.askew(), me.sibling()])
    wires = Wires(send, recv)
    buffers = (mine, sib, r_top, r_low, r_left, r_right, a_top, a_low, a_left, a_right)
    two = reduce_steps(me, wires, 36, first_ref, load, buffers)
    small = terms_steps(me, wires, 77, first_terms, second_terms, weight_ref, all_ref, conds_ref, sums, rounded, tiles, c_first, c_second)
    two[0]()
    small[0]()
    keeps = [
        pltpu.make_async_copy(second_rows, final.at[1], local.at[3]),
        pltpu.make_async_copy(kept_out, outs_ref.at[me.s], local.at[0]),
        pltpu.make_async_copy(kept_grad, grads_ref.at[me.s], local.at[1]),
    ]
    for item in keeps:
        item.start()
    wires.push(72, sent_out, outs_ref.at[me.s], me.flipped())
    wires.push(73, sent_grad, grads_ref.at[me.s], me.flipped())
    big = two[1:]
    small = small[1:]
    for index, step in enumerate(big):
        step()
        if index % 2 == 1 and small:
            small.pop(0)()
    while small:
        small.pop(0)()
    final[0] = mine[me.d]
    for item in keeps:
        item.wait()
    held = final.at[me.s]
    wires.push(74, final.at[1 - me.s], r_across, me.across())
    wires.got(74, r_across, me.across())
    add_rows(held, [(r_across, 0)])
    beside = pltpu.make_async_remote_copy(
        src_ref=held, dst_ref=r_beside, send_sem=send.at[75], recv_sem=recv.at[75], device_id=me.beside(), device_id_type=MESH
    )
    beside.start()
    wires.got(75, r_beside, me.beside())
    beside.wait_send()
    add_rows(held, [(r_beside, 0)])
    out_rows = o_ref.at[half_rows(me.c, 0, HALF), :]
    wires.push(76, held, out_rows, me.sibling())
    own = pltpu.make_async_copy(held, out_rows, local.at[2])
    own.start()
    own.wait()
    wires.got(72, outs_ref.at[1 - me.s], me.flipped())
    wires.got(73, grads_ref.at[1 - me.s], me.flipped())
    wires.got(76, o_ref.at[half_rows(1 - me.c, 0, HALF), :], me.sibling())
    wires.finish()


def reduce_buffers():
    blocks = lambda *lead: pltpu.VMEM(lead + (WIDE,), jnp.bfloat16)
    return [
        blocks(16, HALF),
        blocks(16, HALF),
        blocks(4, TOP),
        blocks(4, LOW),
        blocks(4, HALF),
        blocks(4, HALF),
        blocks(TOP),
        blocks(LOW),
        blocks(HALF),
        blocks(HALF),
    ]


def reduce_grads(*operands):
    count = 77 + 26
    bf, f32 = jnp.bfloat16, jnp.float32
    blocks = lambda *lead: pltpu.VMEM(lead + (WIDE,), bf)
    whole = pl.BlockSpec(memory_space=pltpu.VMEM)
    away = pl.BlockSpec(memory_space=pl.ANY)
    return pl.pallas_call(
        reduce_kernel,
        out_shape=[
            jax.ShapeDtypeStruct((ROWS, WIDE), bf),
            jax.ShapeDtypeStruct((16, 2, 8, WIDE), f32),
            jax.ShapeDtypeStruct((16, 8, PAIR), f32),
            jax.ShapeDtypeStruct((2, TOKENS, WIDE), bf),
            jax.ShapeDtypeStruct((2, TOKENS, WIDE), f32),
        ],
        in_specs=[away, away, whole, whole, whole, away, away, away, away],
        out_specs=[away, whole, whole, away, away],
        scratch_shapes=[
            *reduce_buffers(),
            blocks(2, HALF),
            blocks(HALF),
            blocks(HALF),
            pltpu.VMEM((4, 2, 8, WIDE), f32),
            pltpu.VMEM((2, 8, WIDE), f32),
            pltpu.VMEM((3, 16, 8, PAIR), f32),
            pltpu.VMEM((2, 4, 4, 8, PAIR), f32),
            pltpu.VMEM((2, 4, 4, 8, PAIR), f32),
            pltpu.SemaphoreType.DMA((16,)),
            pltpu.SemaphoreType.DMA((4,)),
            pltpu.SemaphoreType.DMA((count,)),
            pltpu.SemaphoreType.DMA((count,)),
        ],
        compiler_params=pltpu.CompilerParams(
            collective_id=1, has_side_effects=True, vmem_limit_bytes=48 * 1024 * 1024
        ),
        cost_estimate=pl.CostEstimate(flops=0, bytes_accessed=60000000, transcendentals=0),
        name="reduce_grads",
    )(*operands)


def seq_peers(me):
    far = [(me.s, me.d, (1 - me.xl) * 2 + core) for core in range(2)]
    return me.sibling(), far


def forward_kernel(
    part, x_ref, mod_ref, bias_ref, w_hbm, *refs
):
    shard_ref, refs = (refs[0], refs[1:]) if part == 0 else (None, refs)
    out_ref, mixed_one_ref, qkv_out, lse_ref, att_out, branch_one_ref, middle_ref, mixed_two_ref, expanded_out, branch_two_ref, *refs = refs
    next_ref, refs = (refs[0], refs[1:]) if part == 0 else (None, refs)
    w, stage, qkv, heads, att, expanded, load, save, send, recv = refs
    me = Place()
    sibling, far = seq_peers(me)
    first_load = pltpu.make_async_copy(w_hbm.at[:, pl.ds(0, 144), :], w.at[:, pl.ds(0, 144), :], load.at[0])
    rest_load = pltpu.make_async_copy(w_hbm.at[:, pl.ds(144, 464), :], w.at[:, pl.ds(144, 464), :], load.at[1])
    first_load.start()
    rest_load.start()
    around = [me.ring(1, 0), me.ring(3, 0), me.ring(0, 1), me.ring(0, 3)] if part == 0 else []
    greet([sibling, *far, *around])
    wires = Wires(send, recv)
    beside = gather_steps(me, wires, 12, shard_ref, next_ref, load.at[2]) if part == 0 else []

    def advance(count):
        for _ in range(min(count, len(beside))):
            beside.pop(0)()

    advance(1)

    row = lambda index: mod_ref[index : index + 1, :]
    bias = lambda index: bias_ref[index : index + 1, :]
    tokens = x_ref[...].astype(jnp.float32)
    normed_one, _ = norm_rows(tokens)
    mixed_one = (normed_one * (1.0 + row(1)) + row(0)).astype(jnp.bfloat16)
    mixed_one_ref[...] = mixed_one
    first_load.wait()

    def project(kind, weight_row, added):
        made = dot(mixed_one, square(w, weight_row))
        if added is not None:
            made = made + added
        made = made.astype(jnp.bfloat16)
        for pair in range(6):
            stage[pair, kind] = made[:, pair * PAIR : (pair + 1) * PAIR]

    project(0, 48, None)
    project(1, 96, bias(1))
    for j in range(3):
        for g in range(2):
            wires.push(2 * j + g, stage.at[3 * g + j, pl.ds(0, 2)], qkv.at[2 + me.c, j, pl.ds(0, 2)], far[g], 2 * j + me.c)
    project(2, 0, bias(0))
    advance(1)
    for j in range(3):
        wires.push(6 + j, stage.at[3 * (1 - me.c) + j], qkv.at[me.c, j], sibling)
    for j in range(3):
        qkv[me.c, j] = stage[3 * me.c + j]

    advance(1)
    for j in range(3):
        wires.got(6 + j, qkv.at[1 - me.c, j], sibling)
        for g in range(2):
            wires.got(2 * j + g, qkv.at[2 + g, j, pl.ds(0, 2)], far[g])

        def queries_step(g, carry):
            keys = qkv[:, j, 0].reshape(4 * TOKENS, PAIR)
            values = qkv[:, j, 1].reshape(4 * TOKENS, PAIR)
            queries = qkv[g, j, 2] * jnp.bfloat16(0.125)
            made = []
            for head in range(2):
                scores = dot(keys, only_head(queries, head), 1, 1)
                top = jnp.max(scores, axis=0, keepdims=True)
                powers = jnp.exp(scores - top)
                sums = jnp.sum(powers, axis=0, keepdims=True)
                lse_ref[(2 * j + head) * 2 + g] = top + jnp.log(sums)
                weights = (powers * (1.0 / sums)).astype(jnp.bfloat16)
                made.append(dot(values, weights, 0, 0)[head * HEAD : (head + 1) * HEAD])
            heads[g, j] = jnp.concatenate(made, axis=0).T.astype(jnp.bfloat16)
            return carry

        lax.fori_loop(0, 2, queries_step, 0)
        wires.push(9 + j, heads.at[1 - me.c, j], att.at[3 * me.c + j], sibling)
        att[3 * me.c + j] = heads[me.c, j]
        advance(1)
    qkv_save = pltpu.make_async_copy(qkv, qkv_out, save.at[0])
    qkv_save.start()
    rest_load.wait()
    for j in range(3):
        wires.got(9 + j, att.at[3 * (1 - me.c) + j], sibling)
    att_save = pltpu.make_async_copy(att, att_out, save.at[1])
    att_save.start()
    attended = side_by_side(att)
    branch_one = dot(attended, square(w, 144)) + bias(2)
    branch_one_ref[...] = branch_one
    advance(1)
    middle = tokens + row(2) * branch_one
    middle_ref[...] = middle
    normed_two, _ = norm_rows(middle)
    mixed_two = (normed_two * (1.0 + row(4)) + row(3)).astype(jnp.bfloat16)
    mixed_two_ref[...] = mixed_two
    total = bias(7)
    saves = []
    for k in range(4):
        u = dot(mixed_two, square(w, EXPAND_ROWS[k])) + bias(3 + k)
        expanded[k] = u
        item = pltpu.make_async_copy(expanded.at[k], expanded_out.at[k], save.at[2 + k])
        item.start()
        saves.append(item)
        activated = (0.5 * u * (1.0 + jnp.tanh(ROOT * (u + 0.044715 * (u * u * u))))).astype(jnp.bfloat16)
        total = total + dot(activated, contract_square(w, k))
        advance(1)
    branch_two_ref[...] = total
    out_ref[...] = (middle + row(5) * total).astype(jnp.bfloat16)
    advance(12)
    qkv_save.wait()
    att_save.wait()
    for item in saves:
        item.wait()
    wires.finish()


def block_forward(part, tokens, modulation, bias, blocks, *shard):
    shape = lambda dims, dtype: jax.ShapeDtypeStruct(dims, dtype)
    bf, f32 = jnp.bfloat16, jnp.float32
    whole = pl.BlockSpec(memory_space=pltpu.VMEM)
    away = pl.BlockSpec(memory_space=pl.ANY)
    return pl.pallas_call(
        functools.partial(forward_kernel, part),
        out_shape=[
            shape((TOKENS, WIDE), bf),
            shape((TOKENS, WIDE), bf),
            shape((4, 3, 3, TOKENS, PAIR), bf),
            shape((12, 1, TOKENS), f32),
            shape((6, TOKENS, PAIR), bf),
            shape((TOKENS, WIDE), f32),
            shape((TOKENS, WIDE), f32),
            shape((TOKENS, WIDE), bf),
            shape((4, TOKENS, WIDE), f32),
            shape((TOKENS, WIDE), f32),
        ]
        + [shape((16, ROWS, WIDE), bf) for _ in shard],
        in_specs=[whole, whole, whole, away] + [away for _ in shard],
        out_specs=[whole, whole, away, whole, away, whole, whole, whole, away, whole] + [away for _ in shard],
        scratch_shapes=[
            pltpu.VMEM((16, ROWS, WIDE), bf),
            pltpu.VMEM((6, 3, TOKENS, PAIR), bf),
            pltpu.VMEM((4, 3, 3, TOKENS, PAIR), bf),
            pltpu.VMEM((2, 3, TOKENS, PAIR), bf),
            pltpu.VMEM((6, TOKENS, PAIR), bf),
            pltpu.VMEM((4, TOKENS, WIDE), f32),
            pltpu.SemaphoreType.DMA((3,)),
            pltpu.SemaphoreType.DMA((6,)),
            pltpu.SemaphoreType.DMA((48,)),
            pltpu.SemaphoreType.DMA((48,)),
        ],
        compiler_params=pltpu.CompilerParams(
            collective_id=2 + part, has_side_effects=True, vmem_limit_bytes=56 * 1024 * 1024
        ),
        cost_estimate=pl.CostEstimate(flops=5 * 10**9, bytes_accessed=25 * 10**6, transcendentals=4 * 10**6),
        name=("forward_first", "forward_second")[part],
    )(tokens, modulation, bias, blocks, *shard)


def backward_kernel(
    part, grad_ref, x_ref, mod_ref, w_hbm, mixed_one_ref, qkv_in, lse_ref, att_ref, branch_one_ref, middle_ref, mixed_two_ref, expanded_in, branch_two_ref, *refs
):
    later_ref, refs = (refs[0], refs[1:]) if part == 0 else (None, refs)
    input_grad_ref, terms_ref, grads_out, *refs = refs
    rows_out, refs = (refs[0], refs[1:]) if part == 0 else (None, refs)
    w, expanded, qkv, stage, given, dkv, dq, own, far_out, far_in, side_out, side_in, joined, load, save, send, recv, *refs = refs
    me = Place()
    sibling, far = seq_peers(me)
    c, other = me.c, 1 - me.c
    back_load = pltpu.make_async_copy(w_hbm.at[:, pl.ds(192, 416), :], w.at[:, pl.ds(192, 416), :], load.at[0])
    expanded_load = pltpu.make_async_copy(expanded_in, expanded, load.at[1])
    front_load = pltpu.make_async_copy(w_hbm.at[:, pl.ds(0, 192), :], w.at[:, pl.ds(0, 192), :], load.at[2])
    qkv_load = pltpu.make_async_copy(qkv_in, qkv, load.at[3])
    back_load.start()
    expanded_load.start()
    front_load.start()
    qkv_load.start()
    around = [me.ring(1, 0), me.ring(3, 0), me.ring(0, 1), me.ring(0, 3)] if part == 0 else []
    greet([sibling, *far, *around])
    wires = Wires(send, recv)
    beside = reduce_steps(me, wires, 10, later_ref, refs[-1], refs[:-1]) if part == 0 else []

    def advance(count):
        for _ in range(min(count, len(beside))):
            beside.pop(0)()

    advance(1)
    saves = []

    def keep(index, start, count):
        rows = pl.ds(start, count)
        item = pltpu.make_async_copy(w.at[:, rows, :], grads_out.at[:, rows, :], save.at[index])
        item.start()
        saves.append(item)

    row = lambda index: mod_ref[index : index + 1, :]
    gradient = grad_ref[...].astype(jnp.float32)
    branch_two_grad = (row(5) * gradient).astype(jnp.bfloat16)
    gate_two_grad = column_sum(gradient * branch_two_ref[...])
    contract_bias_grad = column_sum(branch_two_grad)
    mixed_two = mixed_two_ref[...]
    mixed_two_grad = None
    expand_bias_grads = []
    back_load.wait()
    expanded_load.wait()
    for k in range(4):
        u = expanded[k]
        squared = u * u
        tanh = jnp.tanh(ROOT * (u + 0.044715 * (squared * u)))
        half = 0.5 * (1.0 + tanh)
        activated = (u * half).astype(jnp.bfloat16)
        slope = half + 0.5 * u * (1.0 - tanh * tanh) * (ROOT * (1.0 + (3.0 * 0.044715) * squared))
        expanded_grad = (dot(branch_two_grad, contract_square(w, k), 1, 1) * slope).astype(jnp.bfloat16)
        start = EXPAND_ROWS[k]
        expand_bias_grads.append(column_sum(expanded_grad))
        term = dot(expanded_grad, square(w, start), 1, 1)
        mixed_two_grad = term if mixed_two_grad is None else mixed_two_grad + term
        w[4 * k : 4 * k + 4, CONTRACT_ROW : CONTRACT_ROW + 192, :] = (
            dot(activated, branch_two_grad, 0, 0).astype(jnp.bfloat16).reshape(4, 192, WIDE)
        )
        w[:, start : start + 48, :] = dot(mixed_two, expanded_grad, 0, 0).astype(jnp.bfloat16).reshape(16, 48, WIDE)
        advance(1)
    keep(0, 304, 288)
    keep(1, 192, 96)
    normed_two, inv_two = norm_rows(middle_ref[...])
    scale_two_grad = column_sum(mixed_two_grad * normed_two)
    shift_two_grad = column_sum(mixed_two_grad)
    middle_grad = gradient + norm_back(mixed_two_grad * (1.0 + row(4)), normed_two, inv_two)
    gate_one_grad = column_sum(middle_grad * branch_one_ref[...])
    branch_one_grad = (row(2) * middle_grad).astype(jnp.bfloat16)
    front_load.wait()
    attended_grad = dot(branch_one_grad, square(w, 144), 1, 1).astype(jnp.bfloat16)
    for pair in range(6):
        stage[pair] = attended_grad[:, pair * PAIR : (pair + 1) * PAIR]
    wires.push(0, stage.at[pl.ds(3 * other, 3)], given.at[c], sibling)
    advance(1)
    given[c] = stage[pl.ds(3 * c, 3)]
    input_grad_ref[...] = middle_grad
    w[:, 144:192, :] = dot(side_by_side(att_ref), branch_one_grad, 0, 0).astype(jnp.bfloat16).reshape(16, 48, WIDE)
    keep(2, 144, 48)
    attention_bias_grad = column_sum(branch_one_grad)
    advance(1)
    qkv_load.wait()
    wires.got(0, given.at[other], sibling)

    for j in range(3):
        dkv[...] = jnp.zeros_like(dkv)

        def queries_step(g, carry):
            keys = qkv[:, j, 0].reshape(4 * TOKENS, PAIR)
            values = qkv[:, j, 1].reshape(4 * TOKENS, PAIR)
            queries = qkv[g, j, 2] * jnp.bfloat16(0.125)
            output_grads = given[g, j]
            key_sums, value_sums, query_parts = 0.0, 0.0, []
            for head in range(2):
                head_queries = only_head(queries, head)
                head_grads = only_head(output_grads, head)
                scores = dot(keys, head_queries, 1, 1)
                probs = jnp.exp(scores - lse_ref[(2 * j + head) * 2 + g])
                weight_grads = dot(values, head_grads, 1, 1)
                centre = jnp.sum(probs * weight_grads, axis=0, keepdims=True)
                score_grads = (probs * (weight_grads - centre)).astype(jnp.bfloat16)
                key_sums = key_sums + dot(score_grads, head_queries)
                value_sums = value_sums + dot(probs.astype(jnp.bfloat16), head_grads)
                query_parts.append(dot(keys, score_grads, 0, 0)[head * HEAD : (head + 1) * HEAD])
            dq[g] = jnp.concatenate(query_parts, axis=0).T * 0.125
            dkv[0] += key_sums.reshape(4, TOKENS, PAIR)
            dkv[1] += value_sums.reshape(4, TOKENS, PAIR)
            return carry

        lax.fori_loop(0, 2, queries_step, 0)
        for g in range(2):
            far_out[j, g] = dkv[:, 2 + g].astype(jnp.bfloat16)
            wires.push(1 + 2 * j + g, far_out.at[j, g], far_in.at[j, c], far[g], 1 + 2 * j + c)
        side_out[j, 0:2] = dkv[:, other].astype(jnp.bfloat16)
        side_out[j, 2] = dq[other].astype(jnp.bfloat16)
        wires.push(7 + j, side_out.at[j], side_in.at[j], sibling)
        own[j, 0:2] = dkv[:, c]
        own[j, 2] = dq[c]
        advance(1 if j == 0 else 2)

    for j in range(3):
        wires.got(7 + j, side_in.at[j], sibling)
        for g in range(2):
            wires.got(1 + 2 * j + g, far_in.at[j, g], far[g])
        for kind in range(2):
            joined[kind, 3 * c + j] = (own[j, kind] + far_in[j, c, kind].astype(jnp.float32)).astype(jnp.bfloat16)
            joined[kind, 3 * other + j] = (
                side_in[j, kind].astype(jnp.float32) + far_in[j, other, kind].astype(jnp.float32)
            ).astype(jnp.bfloat16)
        joined[2, 3 * c + j] = own[j, 2].astype(jnp.bfloat16)
        joined[2, 3 * other + j] = side_in[j, 2]
    mixed_one = mixed_one_ref[...]
    mixed_one_grad, bias_grads = None, []
    for kind, start in ((0, 48), (1, 96), (2, 0)):
        piece = side_by_side(joined, (kind,))
        bias_grads.append(column_sum(piece))
        term = dot(piece, square(w, start), 1, 1)
        mixed_one_grad = term if mixed_one_grad is None else mixed_one_grad + term
        w[:, start : start + 48, :] = dot(mixed_one, piece, 0, 0).astype(jnp.bfloat16).reshape(16, 48, WIDE)
        advance(1)
    keep(3, 0, 144)
    small = jnp.concatenate(
        [
            bias_grads[2],
            bias_grads[1],
            attention_bias_grad,
            *expand_bias_grads,
            contract_bias_grad,
            jnp.zeros((8, WIDE), jnp.float32),
        ],
        axis=0,
    ).astype(jnp.bfloat16)
    w[:, BIAS_ROW : BIAS_ROW + 16, :] = jnp.broadcast_to(small[None], (16, 16, WIDE))
    w[:, 592:608, :] = jnp.zeros((16, 16, WIDE), jnp.bfloat16)
    keep(4, BIAS_ROW, 16)
    keep(5, 592, 16)
    normed_one, inv_one = norm_rows(x_ref[...].astype(jnp.float32))
    terms_ref[...] = jnp.concatenate(
        [
            column_sum(mixed_one_grad),
            column_sum(mixed_one_grad * normed_one),
            gate_one_grad,
            shift_two_grad,
            scale_two_grad,
            gate_two_grad,
            jnp.zeros((2, WIDE), jnp.float32),
        ],
        axis=0,
    )
    input_grad_ref[...] += norm_back(mixed_one_grad * (1.0 + row(1)), normed_one, inv_one)
    advance(16)
    if part == 0:
        rows_save = pltpu.make_async_copy(refs[0].at[me.d], rows_out, load.at[0])
        rows_save.start()
        rows_save.wait()
    for item in saves:
        item.wait()
    wires.finish()


def block_backward(part, gradient, tokens, modulation, blocks, kept, *later):
    shape = lambda dims, dtype: jax.ShapeDtypeStruct(dims, dtype)
    bf, f32 = jnp.bfloat16, jnp.float32
    whole = pl.BlockSpec(memory_space=pltpu.VMEM)
    away = pl.BlockSpec(memory_space=pl.ANY)
    return pl.pallas_call(
        functools.partial(backward_kernel, part),
        out_shape=[
            shape((TOKENS, WIDE), f32),
            shape((8, WIDE), f32),
            shape((16, ROWS, WIDE), bf),
        ]
        + [shape((HALF, WIDE), bf) for _ in later],
        in_specs=[whole, whole, whole, away, whole, away, whole, whole, whole, whole, whole, away, whole] + [away for _ in later],
        out_specs=[whole, whole, away] + [away for _ in later],
        scratch_shapes=[
            pltpu.VMEM((16, ROWS, WIDE), bf),
            pltpu.VMEM((4, TOKENS, WIDE), f32),
            pltpu.VMEM((4, 3, 3, TOKENS, PAIR), bf),
            pltpu.VMEM((6, TOKENS, PAIR), bf),
            pltpu.VMEM((2, 3, TOKENS, PAIR), bf),
            pltpu.VMEM((2, 4, TOKENS, PAIR), f32),
            pltpu.VMEM((2, TOKENS, PAIR), f32),
            pltpu.VMEM((3, 3, TOKENS, PAIR), f32),
            pltpu.VMEM((3, 2, 2, TOKENS, PAIR), bf),
            pltpu.VMEM((3, 2, 2, TOKENS, PAIR), bf),
            pltpu.VMEM((3, 3, TOKENS, PAIR), bf),
            pltpu.VMEM((3, 3, TOKENS, PAIR), bf),
            pltpu.VMEM((3, 6, TOKENS, PAIR), bf),
            pltpu.SemaphoreType.DMA((4,)),
            pltpu.SemaphoreType.DMA((6,)),
            pltpu.SemaphoreType.DMA((46,)),
            pltpu.SemaphoreType.DMA((46,)),
        ]
        + ([*reduce_buffers(), pltpu.SemaphoreType.DMA((16,))] if later else []),
        compiler_params=pltpu.CompilerParams(
            collective_id=4 + part, has_side_effects=True, vmem_limit_bytes=60 * 1024 * 1024
        ),
        cost_estimate=pl.CostEstimate(flops=12 * 10**9, bytes_accessed=45 * 10**6, transcendentals=4 * 10**6),
        name=("backward_first", "backward_second")[part],
    )(gradient, tokens, modulation, blocks, *kept, *later)


def pack_weights(projection, attention, expand, contract, biases):
    fill = jnp.zeros((WIDE - biases.shape[0],), jnp.bfloat16)
    columns = lambda weight: weight.reshape(48, -1, WIDE).swapaxes(0, 1).reshape(-1, WIDE)
    return jnp.concatenate(
        [
            columns(projection),
            attention,
            columns(expand[:, : 2 * WIDE]),
            jnp.concatenate([biases, fill])[None],
            jnp.zeros((15, WIDE), jnp.bfloat16),
            columns(expand[:, 2 * WIDE :]),
            contract,
            jnp.zeros((16, WIDE), jnp.bfloat16),
        ]
    )


def bias_rows(biases):
    parts = [
        biases[:, :96].reshape(2, WIDE),
        biases[:, 96:144].reshape(1, WIDE),
        biases[:, 144:336].reshape(4, WIDE),
        biases[:, 336:384].reshape(1, WIDE),
    ]
    added = jnp.pad(biases[:, 384:672].reshape(6, WIDE), ((0, 2), (0, 0)))
    return jnp.concatenate(parts), added


def unpack_grads(rows, place):
    columns = lambda part: part.reshape(-1, 48, WIDE).swapaxes(0, 1).reshape(48, -1)
    own = lambda part, size: lax.dynamic_slice_in_dim(part.reshape(-1), place * size, size)
    bias = rows[BIAS_ROW : BIAS_ROW + 8]
    return [
        columns(rows[:144]),
        own(bias[0:2], 96),
        rows[144:192],
        own(bias[2:3], 48),
        columns(jnp.concatenate([rows[192:288], rows[304:400]])),
        own(bias[3:7], 192),
        rows[400:592],
        own(bias[7:8], 48),
    ]


def on_device(
    latents,
    conditions,
    output_cotangent,
    modulation_weight,
    modulation_bias,
    projection_weight,
    projection_bias,
    attention_weight,
    attention_bias,
    expand_weight,
    expand_bias,
    contract_weight,
    contract_bias,
):
    section = lax.axis_index("section")
    place = lax.axis_index("dp")
    is_first = section == 0
    biases = jnp.concatenate(
        [projection_bias[0], attention_bias[0], expand_bias[0], contract_bias[0], modulation_bias[0]]
    )
    packed = pack_weights(projection_weight[0], attention_weight[0], expand_weight[0], contract_weight[0], biases)
    pieces = jnp.pad(conditions[:, 0].reshape(2, 16, 48).swapaxes(0, 1), ((0, 0), (0, 6), (0, PAIR - 48)))
    owned_weight = jnp.pad(modulation_weight[0], ((0, PAIR - 48), (0, 0)))
    first_blocks, shard, own_conds, modulations = gather_weights(packed, pieces, owned_weight)
    first_bias, first_added = bias_rows(first_blocks[:, BIAS_ROW].astype(jnp.float32))
    first_modulation = modulations[0] + first_added

    tokens = lax.dynamic_index_in_dim(latents, section, 0, keepdims=False)[0]
    cotangent = lax.dynamic_index_in_dim(output_cotangent, section, 0, keepdims=False)[0]
    first_output, *first_kept, second_blocks = block_forward(0, tokens, first_modulation, first_bias, first_blocks, shard)
    second_bias, second_added = bias_rows(second_blocks[:, BIAS_ROW].astype(jnp.float32))
    second_modulation = modulations[1] + second_added
    second_output, *second_kept = block_forward(1, first_output, second_modulation, second_bias, second_blocks)
    second_grad, second_terms, second_made = block_backward(
        1, cotangent, first_output, second_modulation, second_blocks, second_kept
    )
    second_grad = second_grad.astype(jnp.bfloat16)
    first_grad, first_terms, first_made, second_rows = block_backward(
        0, second_grad, tokens, first_modulation, first_blocks, first_kept, second_made
    )

    rounded_grad = second_grad.astype(jnp.float32)
    rows, terms, cond_terms, section_outputs, input_grads = reduce_grads(
        first_made,
        second_rows,
        first_terms,
        second_terms,
        owned_weight,
        jnp.where(is_first, first_output, second_output),
        jnp.where(is_first, second_output, first_output),
        jnp.where(is_first, first_grad, rounded_grad),
        jnp.where(is_first, rounded_grad, first_grad),
    )
    reduced = [grad[None] for grad in unpack_grads(rows.astype(jnp.float32), place)]
    section_outputs = section_outputs[None, :, None]
    input_grads = input_grads[None, :, None]
    terms = terms[:, :, :6].reshape(16, 2, -1)
    own_silu = jax.nn.silu(own_conds[:, :2, :48]).astype(jnp.bfloat16)
    modulation_weight_grad = jnp.einsum(
        "imk,ime->ke", own_silu, terms.astype(jnp.bfloat16), preferred_element_type=jnp.float32
    )
    modulation_bias_grad = lax.dynamic_slice_in_dim(jnp.sum(terms, axis=(0, 1)), place * 288, 288)
    cond_terms = cond_terms[:, :2, :48].swapaxes(0, 1).reshape(2, 1, WIDE)
    condition_grads = jax.vjp(jax.nn.silu, conditions)[1](cond_terms)[0]
    return (
        section_outputs,
        input_grads,
        condition_grads,
        modulation_weight_grad[None],
        modulation_bias_grad[None],
        *reduced,
    )


def solution(mesh):
    return jax.shard_map(
        on_device,
        mesh=mesh,
        in_specs=(
            P(None, "dp", "seq", None),
            P(None, "dp", None),
            P(None, "dp", "seq", None),
            P("section", "dp", None),
            P("section", "dp"),
            P("section", "dp", None),
            P("section", "dp"),
            P("section", "dp", None),
            P("section", "dp"),
            P("section", "dp", None),
            P("section", "dp"),
            P("section", "dp", None),
            P("section", "dp"),
        ),
        out_specs=(
            P("section", None, "dp", "seq", None),
            P("section", None, "dp", "seq", None),
            P(None, "dp", None),
            P("section", "dp", None),
            P("section", "dp"),
            P("section", "dp", None),
            P("section", "dp"),
            P("section", "dp", None),
            P("section", "dp"),
            P("section", "dp", None),
            P("section", "dp"),
            P("section", "dp", None),
            P("section", "dp"),
        ),
        check_vma=False,
    )
```

```python
import functools

import jax
import jax.numpy as jnp
from jax import lax
from jax.experimental import pallas as pl
from jax.experimental.pallas import tpu as pltpu
from jax.sharding import PartitionSpec as P

HEAD = 64


MESH = pl.DeviceIdType.MESH
ROWS = 608
HALF = ROWS // 2
TOP = 160
LOW = HALF - TOP
WIDE = 768
OFFSETS = (0, 3, 1, 2)


class Place:
    def __init__(self):
        self.s = lax.axis_index("section")
        self.d = lax.axis_index("dp")
        self.q = lax.axis_index("seq")
        y, z = self.d // 4, lax.rem(self.d, 4)
        self.xl, self.c = self.q // 2, lax.rem(self.q, 2)
        self.a = (1 - self.c) * z + self.c * y
        self.b = (1 - self.c) * y + self.c * z

    def dp(self, ka, kb):
        aa = lax.rem(self.a + ka, 4)
        bb = lax.rem(self.b + kb, 4)
        return aa * (1 + 3 * self.c) + bb * (4 - 3 * self.c)

    def ring(self, ka, kb):
        return (self.s, self.dp(ka, kb), self.q)

    def sibling(self):
        return (self.s, self.d, self.xl * 2 + 1 - self.c)

    def across(self):
        return (1 - self.s, self.d, (1 - self.xl) * 2 + self.c)

    def beside(self):
        return (self.s, self.d, (1 - self.xl) * 2 + self.c)

    def askew(self):
        return (self.s, self.d, (1 - self.xl) * 2 + 1 - self.c)

    def flipped(self):
        return (1 - self.s, self.d, self.q)

    def grid_peers(self):
        return [self.ring(k, 0) for k in (1, 3, 2)] + [self.ring(0, k) for k in (1, 3, 2)]


def greet(devices):
    barrier = pltpu.get_barrier_semaphore()
    for device in devices:
        pl.semaphore_signal(barrier, inc=1, device_id=device, device_id_type=MESH)
    pl.semaphore_wait(barrier, len(devices))


def half_rows(core, offset, count):
    return pl.ds(pl.multiple_of(core * HALF + offset, 16), count)


class Wires:
    def __init__(self, send, recv):
        self.send, self.recv, self.started = send, recv, []

    def push(self, index, source, target, device, landing=None):
        item = pltpu.make_async_remote_copy(
            src_ref=source,
            dst_ref=target,
            send_sem=self.send.at[index],
            recv_sem=self.recv.at[index if landing is None else landing],
            device_id=device,
            device_id_type=MESH,
        )
        item.start()
        self.started.append(item)

    def got(self, index, target, device):
        pltpu.make_async_remote_copy(
            src_ref=target,
            dst_ref=target,
            send_sem=self.send.at[0],
            recv_sem=self.recv.at[index],
            device_id=device,
            device_id_type=MESH,
        ).wait_recv()

    def finish(self):
        for item in self.started:
            item.wait_send()


TOKENS = 256
PAIR = 128
EXPAND_ROWS = (192, 240, 304, 352)
CONTRACT_ROW = 400
BIAS_ROW = 288
ROOT = (2.0 / 3.141592653589793) ** 0.5


def norm_rows(values):
    row_mean = jnp.mean(values, axis=-1, keepdims=True)
    centered = values - row_mean
    variance = jnp.mean(centered * centered, axis=-1, keepdims=True)
    inv_std = lax.rsqrt(variance + 1e-06)
    return (centered * inv_std, inv_std)


def norm_back(gradient, normed, inv_std):
    row_mean = jnp.mean(gradient, axis=-1, keepdims=True)
    along = jnp.mean(gradient * normed, axis=-1, keepdims=True)
    return inv_std * (gradient - row_mean - normed * along)


def dot(left, right, left_dim=1, right_dim=0):
    return lax.dot_general(
        left, right, (((left_dim,), (right_dim,)), ((), ())), preferred_element_type=jnp.float32
    )


def column_sum(values):
    return jnp.sum(values.astype(jnp.float32), axis=0, keepdims=True)


def square(w, row):
    return w[:, row : row + 48, :].reshape(WIDE, WIDE)


def contract_square(w, part):
    return w[4 * part : 4 * part + 4, CONTRACT_ROW : CONTRACT_ROW + 192, :].reshape(WIDE, WIDE)


def side_by_side(ref, lead=()):
    return jnp.concatenate([ref[(*lead, pair)] for pair in range(6)], axis=1)


def head_lanes(head):
    lane = lax.broadcasted_iota(jnp.int32, (1, PAIR), 1)
    return (lane // HEAD) == head


def only_head(values, head):
    return jnp.where(head_lanes(head), values, jnp.zeros_like(values))


def gather_steps(me, wires, base, source, w_ref, local):
    right_a, left_a = me.ring(1, 0), me.ring(3, 0)
    right_b, left_b = me.ring(0, 1), me.ring(0, 3)
    sibling = me.sibling()

    def slot(ka, kb, offset=0, count=HALF):
        return w_ref.at[me.dp(ka, kb), half_rows(me.c, offset, count), :]

    def got(index, target):
        wires.got(base + index, target, sibling)

    def push(index, origin, target, device):
        wires.push(base + index, origin, target, device)

    def to_side(ka, kb, origin=None):
        block = slot(ka, kb)
        push(20 + 4 * ka + kb, block if origin is None else origin, block, sibling)

    def spread_b(ka, origin=None):
        block = slot(ka, 0)
        origin = block if origin is None else origin
        push(4 + 4 * ka, origin, block, right_b)
        push(5 + 4 * ka, origin, block, left_b)

    own = pltpu.make_async_copy(source, slot(0, 0), local)

    def start():
        own.start()
        push(0, source, slot(0, 0), right_a)
        push(1, source, slot(0, 0), left_a)
        spread_b(0, source)
        to_side(0, 0, source)

    def forward_a():
        got(0, slot(3, 0))
        push(2, slot(3, 0, 0, TOP), slot(3, 0, 0, TOP), right_a)
        spread_b(3)
        to_side(3, 0)
        got(1, slot(1, 0))
        push(3, slot(1, 0, TOP, LOW), slot(1, 0, TOP, LOW), left_a)
        spread_b(1)
        to_side(1, 0)

    def end_a():
        got(2, slot(2, 0, 0, TOP))
        got(3, slot(2, 0, TOP, LOW))
        spread_b(2)
        to_side(2, 0)

    def forward_b(ka):
        at = 4 + 4 * ka
        got(at, slot(ka, 3))
        push(at + 2, slot(ka, 3, 0, TOP), slot(ka, 3, 0, TOP), right_b)
        to_side(ka, 3)
        got(at + 1, slot(ka, 1))
        push(at + 3, slot(ka, 1, TOP, LOW), slot(ka, 1, TOP, LOW), left_b)
        to_side(ka, 1)

    def end_b(ka):
        at = 4 + 4 * ka
        got(at + 2, slot(ka, 2, 0, TOP))
        got(at + 3, slot(ka, 2, TOP, LOW))
        to_side(ka, 2)

    def finish():
        own.wait()
        for ka in range(4):
            for kb in range(4):
                got(20 + 4 * ka + kb, w_ref.at[me.dp(kb, ka), half_rows(1 - me.c, 0, HALF), :])

    steps = [start, forward_a, end_a]
    steps += [functools.partial(forward_b, ka) for ka in OFFSETS]
    steps += [functools.partial(end_b, ka) for ka in OFFSETS]
    return steps + [finish]


def swap_steps(me, wires, base, pieces, first, second, result):
    def start():
        for ka in range(4):
            for kb in range(4):
                first[0, ka, kb] = pieces[me.dp(ka, kb)]
        for k in (1, 2, 3):
            wires.push(base + k - 1, first.at[0, k], first.at[1, k], me.ring(k, 0))

    def middle():
        for kb in range(4):
            second[0, kb, 0] = first[0, 0, kb]
        for k in (1, 2, 3):
            wires.got(base + k - 1, first.at[1, k], me.sibling())
            for kb in range(4):
                second[0, kb, k] = first[1, k, kb]
        for k in (1, 2, 3):
            wires.push(base + 2 + k, second.at[0, k], second.at[1, k], me.ring(0, k))

    def end():
        for ka in range(4):
            result[me.dp((4 - ka) % 4, 0)] = second[0, 0, ka]
        for k in (1, 2, 3):
            wires.got(base + 2 + k, second.at[1, k], me.sibling())
            for ka in range(4):
                result[me.dp((4 - ka) % 4, 4 - k)] = second[1, k, ka]

    return [start, middle, end]


def modulation_steps(me, wires, base, conds_ref, weight_ref, columns_ref, mod_ref, first, second, partial, b_sums, a_sums, across_sums):
    swap = swap_steps(me, wires, base, conds_ref, first, second, columns_ref)

    def multiply():
        swap[2]()
        rows = lax.broadcasted_iota(jnp.int32, (8, 32), 0)
        taken = lax.broadcasted_iota(jnp.int32, (8, 32), 1)
        pick = jnp.where(taken == (rows // 2) * 8 + lax.rem(rows, 2), 1.0, 0.0).astype(jnp.bfloat16)
        for kb in range(4):
            found = jnp.concatenate([columns_ref[me.dp((4 - ka) % 4, (4 - kb) % 4)] for ka in range(4)], axis=0)
            silu = (found / (1.0 + jnp.exp(-found))).astype(jnp.bfloat16)
            silu = dot(pick, silu).astype(jnp.bfloat16)
            partial[kb] = dot(silu, weight_ref[...])
        for k in (1, 2, 3):
            wires.push(base + 5 + k, partial.at[k], b_sums.at[k - 1], me.ring(0, 4 - k))

    def add_b():
        for k in (1, 2, 3):
            wires.got(base + 5 + k, b_sums.at[k - 1], me.sibling())
        a_sums[0] = partial[0] + b_sums[0] + b_sums[1] + b_sums[2]
        for k in (1, 2, 3):
            wires.push(base + 8 + k, a_sums.at[0], a_sums.at[k], me.ring(4 - k, 0))

    def add_a():
        for k in (1, 2, 3):
            wires.got(base + 8 + k, a_sums.at[k], me.sibling())
        total = a_sums[0, 0:2]
        for k in (1, 2, 3):
            total = total + a_sums[k, 2 * k : 2 * k + 2]
        across_sums[0] = jnp.concatenate([total, jnp.zeros((6, total.shape[1]), jnp.float32)], axis=0)
        wires.push(base + 12, across_sums.at[0], across_sums.at[1], me.flipped())

    def end():
        wires.got(base + 12, across_sums.at[1], me.sibling())
        lead = me.s == 0
        kept = jnp.where(lead, across_sums[0, 0:1], across_sums[0, 1:2])
        came = jnp.where(lead, across_sums[1, 0:1], across_sums[1, 1:2])
        zeros = jnp.zeros((2, WIDE), jnp.float32)
        for block, row in ((0, jnp.where(lead, kept, came)), (1, jnp.where(lead, came, kept))):
            mod_ref[block] = jnp.concatenate([row[:, r * WIDE : (r + 1) * WIDE] for r in range(6)] + [zeros], axis=0)

    return [swap[0], swap[1], multiply, add_b, add_a, end]


def gather_kernel(projection_ref, attention_ref, expand_ref, contract_ref, extra_ref, conds_ref, weight_ref, first_ref, shard_out, columns_ref, mod_ref, shard, c_first, c_second, partial, b_sums, a_sums, across_sums, local, send, recv):
    me = Place()
    columns = lambda ref, k: ref.at[:, pl.ds(k * WIDE, WIDE)]
    halves = (
        [columns(projection_ref, k) for k in range(3)] + [attention_ref, columns(expand_ref, 0), columns(expand_ref, 1), extra_ref],
        [columns(expand_ref, 2), columns(expand_ref, 3), contract_ref, extra_ref],
    )

    def pack(core):
        items, start = [], 0
        for part in halves[core]:
            count = part.shape[0]
            items.append(pltpu.make_async_copy(part, shard.at[me.s, pl.ds(start, count), :], local.at[2 + len(items)]))
            start += count
        for item in items:
            item.start()
        for item in items:
            item.wait()

    for core in range(2):
        pl.when(me.c == core)(functools.partial(pack, core))
    mine = shard.at[me.s]
    greet(me.grid_peers() + [me.across(), me.flipped(), me.sibling()])
    wires = Wires(send, recv)
    wires.push(0, mine, shard.at[me.s], me.across())
    small = modulation_steps(me, wires, 37, conds_ref, weight_ref, columns_ref, mod_ref, c_first, c_second, partial, b_sums, a_sums, across_sums)
    small[0]()
    small[1]()
    wires.got(0, shard.at[1 - me.s], me.across())
    handed = pltpu.make_async_copy(shard.at[1], shard_out, local.at[1])
    handed.start()
    one = gather_steps(me, wires, 1, shard.at[0], first_ref, local.at[0])
    one[0]()
    small[2]()
    for step in one[1:5]:
        step()
    small[3]()
    for step in one[5:8]:
        step()
    small[4]()
    for step in one[8:11]:
        step()
    small[5]()
    one[11]()
    handed.wait()
    wires.finish()


def gather_weights(*operands):
    bf, f32 = jnp.bfloat16, jnp.float32
    wide = operands[-1].shape[1]
    whole = pl.BlockSpec(memory_space=pltpu.VMEM)
    away = pl.BlockSpec(memory_space=pl.ANY)
    return pl.pallas_call(
        gather_kernel,
        out_shape=[
            jax.ShapeDtypeStruct((16, ROWS, WIDE), bf),
            jax.ShapeDtypeStruct((HALF, WIDE), bf),
            jax.ShapeDtypeStruct((16, 8, PAIR), f32),
            jax.ShapeDtypeStruct((2, 8, WIDE), f32),
        ],
        in_specs=[away] * 5 + [whole, whole],
        out_specs=[away, away, whole, whole],
        scratch_shapes=[
            pltpu.VMEM((2, HALF, WIDE), bf),
            pltpu.VMEM((2, 4, 4, 8, PAIR), f32),
            pltpu.VMEM((2, 4, 4, 8, PAIR), f32),
            pltpu.VMEM((4, 8, wide), f32),
            pltpu.VMEM((3, 8, wide), f32),
            pltpu.VMEM((4, 8, wide), f32),
            pltpu.VMEM((2, 8, wide), f32),
            pltpu.SemaphoreType.DMA((9,)),
            pltpu.SemaphoreType.DMA((50,)),
            pltpu.SemaphoreType.DMA((50,)),
        ],
        compiler_params=pltpu.CompilerParams(
            collective_id=0, has_side_effects=True, vmem_limit_bytes=60 * 1024 * 1024
        ),
        cost_estimate=pl.CostEstimate(flops=0, bytes_accessed=60000000, transcendentals=0),
        name="gather_weights",
    )(*operands)


def reduce_steps(me, wires, base, source, load, buffers):
    mine, sib, r_top, r_low, r_left, r_right, a_top, a_low, a_left, a_right = buffers
    right_a, left_a = me.ring(1, 0), me.ring(3, 0)
    right_b, left_b = me.ring(0, 1), me.ring(0, 3)
    sibling = me.sibling()

    def push(index, origin, target, device):
        wires.push(base + index, origin, target, device)

    def got(index, target):
        wires.got(base + index, target, sibling)

    def block(ka, kb):
        return mine.at[me.dp(ka, kb)]

    def from_side(ka, kb):
        return sib.at[me.dp(ka, kb)]

    def fetch(ka, kb):
        dp = me.dp(ka, kb)
        return pltpu.make_async_copy(source.at[dp, half_rows(me.c, 0, HALF), :], mine.at[dp], load.at[4 * ka + kb])

    def start():
        for kb in (2, 1, 3, 0):
            for ka in (2, 1, 3, 0):
                fetch(ka, kb).start()
                dp = me.dp(kb, ka)
                push(4 * ka + kb, source.at[dp, half_rows(1 - me.c, 0, HALF), :], sib.at[dp], sibling)

    def total(target, parts, offset=0, count=HALF):
        add_rows(target, parts, offset, count)

    def ready(ka, kb):
        fetch(ka, kb).wait()
        got(4 * ka + kb, from_side(ka, kb))

    def far_b(ka):
        ready(ka, 2)
        far = block(ka, 2)
        total(far, [(from_side(ka, 2), 0)])
        push(16 + 4 * ka, far.at[pl.ds(0, TOP), :], r_top.at[ka], right_b)
        push(17 + 4 * ka, far.at[pl.ds(TOP, LOW), :], r_low.at[ka], left_b)

    def near_b(ka):
        at = 16 + 4 * ka
        ready(ka, 1)
        got(at, r_top.at[ka])
        near, side = block(ka, 1), from_side(ka, 1)
        total(near, [(side, 0), (r_top.at[ka], 0)], 0, TOP)
        total(near, [(side, 0)], TOP, LOW)
        push(at + 2, near, r_left.at[ka], right_b)
        ready(ka, 3)
        got(at + 1, r_low.at[ka])
        near, side = block(ka, 3), from_side(ka, 3)
        total(near, [(side, 0)], 0, TOP)
        total(near, [(side, 0), (r_low.at[ka], TOP)], TOP, LOW)
        push(at + 3, near, r_right.at[ka], left_b)

    def own_b(ka):
        at = 16 + 4 * ka
        ready(ka, 0)
        got(at + 2, r_left.at[ka])
        got(at + 3, r_right.at[ka])
        total(block(ka, 0), [(from_side(ka, 0), 0), (r_left.at[ka], 0), (r_right.at[ka], 0)])
        if ka == 2:
            far = block(2, 0)
            push(32, far.at[pl.ds(0, TOP), :], a_top, right_a)
            push(33, far.at[pl.ds(TOP, LOW), :], a_low, left_a)

    def near_a():
        got(32, a_top)
        total(block(1, 0), [(a_top, 0)], 0, TOP)
        push(34, block(1, 0), a_left, right_a)
        got(33, a_low)
        total(block(3, 0), [(a_low, TOP)], TOP, LOW)
        push(35, block(3, 0), a_right, left_a)

    def own_a():
        got(34, a_left)
        got(35, a_right)
        total(block(0, 0), [(a_left, 0), (a_right, 0)])

    order = (2, 1, 3, 0)
    steps = [start]
    for made in (far_b, near_b, own_b):
        steps += [functools.partial(made, ka) for ka in order]
    return steps + [near_a, own_a]


def add_rows(target, parts, offset=0, count=HALF):
    def step(i, carry):
        rows = pl.ds(pl.multiple_of(offset + 16 * i, 16), 16)
        value = target[rows, :].astype(jnp.float32)
        for part, start in parts:
            value = value + part[pl.ds(pl.multiple_of(offset - start + 16 * i, 16), 16), :].astype(jnp.float32)
        target[rows, :] = value.astype(jnp.bfloat16)
        return carry

    lax.fori_loop(0, count // 16, step, 0)


def terms_steps(me, wires, base, first_ref, second_ref, weight_ref, all_ref, conds_ref, sums, rounded, tiles, c_first, c_second):
    peers = [me.sibling(), me.beside(), me.askew()]

    def start():
        sums[me.q, 0] = first_ref[...]
        sums[me.q, 1] = second_ref[...]
        for k in range(3):
            wires.push(base + k, sums.at[me.q], sums.at[me.q], peers[k], base + k)

    def add():
        for k in range(3):
            wires.got(base + k, sums.at[peers[k][2]], peers[k])
        total = sums[0] + sums[1] + sums[2] + sums[3]
        rounded[...] = total.astype(jnp.bfloat16).astype(jnp.float32)
        all_ref[me.d, me.s] = rounded[me.s]
        wires.push(base + 3, rounded.at[1 - me.s], all_ref.at[me.d, me.s], me.flipped())

    def spread_a():
        wires.got(base + 3, all_ref.at[me.d, 1 - me.s], me.sibling())
        for k in (1, 2, 3):
            wires.push(base + 3 + k, all_ref.at[me.d], all_ref.at[me.d], me.ring(k, 0))

    def spread_b():
        for k in (1, 2, 3):
            wires.got(base + 3 + k, all_ref.at[me.dp(4 - k, 0)], me.sibling())
        for ka in range(4):
            block = all_ref.at[me.dp((4 - ka) % 4, 0)]
            for k in (1, 2, 3):
                wires.push(base + 4 + 3 * ka + 2 + k, block, block, me.ring(0, k))

    def multiply():
        for ka in range(4):
            for k in (1, 2, 3):
                wires.got(base + 4 + 3 * ka + 2 + k, all_ref.at[me.dp((4 - ka) % 4, 4 - k)], me.sibling())
        grads = all_ref[...].reshape(256, WIDE).astype(jnp.bfloat16)
        row = lax.rem(lax.broadcasted_iota(jnp.int32, (256, PAIR), 0), 8)
        total = jnp.zeros((256, PAIR), jnp.float32)
        for r in range(6):
            made = dot(grads, weight_ref[:, r * WIDE : (r + 1) * WIDE], 1, 1)
            total = total + jnp.where(row == r, made, 0.0)
        total = jnp.sum(total.reshape(16, 2, 8, PAIR), axis=2, keepdims=True)
        level = lax.broadcasted_iota(jnp.int32, (16, 8, PAIR), 1)
        tiles[0] = jnp.where(level == 0, total[:, 0], jnp.where(level == 1, total[:, 1], 0.0))
        wires.push(base + 19, tiles.at[0], tiles.at[1], me.flipped())

    def join():
        wires.got(base + 19, tiles.at[1], me.sibling())
        tiles[2] = tiles[0] + tiles[1]
        swap_two[0]()

    swap_two = swap_steps(me, wires, base + 20, tiles.at[2], c_first, c_second, conds_ref)
    return [start, add, spread_a, spread_b, multiply, join, swap_two[1], swap_two[2]]


def reduce_kernel(
    first_ref, second_rows, first_terms, second_terms, weight_ref, kept_grad, sent_grad,
    projection_ref, attention_ref, expand_ref, contract_ref, bias_ref, all_ref, conds_ref, grads_ref,
    mine, sib, r_top, r_low, r_left, r_right, a_top, a_low, a_left, a_right, final, r_across, r_beside, rows, r_grad, wide_grad,
    sums, rounded, tiles, c_first, c_second, load, local, send, recv,
):
    me = Place()
    greet(me.grid_peers() + [me.across(), me.flipped(), me.beside(), me.askew(), me.sibling()])
    wires = Wires(send, recv)
    buffers = (mine, sib, r_top, r_low, r_left, r_right, a_top, a_low, a_left, a_right)
    two = reduce_steps(me, wires, 36, first_ref, load, buffers)
    small = terms_steps(me, wires, 86, first_terms, second_terms, weight_ref, all_ref, conds_ref, sums, rounded, tiles, c_first, c_second)
    two[0]()
    small[0]()
    keeps = [
        pltpu.make_async_copy(second_rows, final.at[1], local.at[3]),
        pltpu.make_async_copy(kept_grad, grads_ref.at[me.s], local.at[1]),
    ]
    for item in keeps:
        item.start()
    big = two[1:]
    small = small[1:]
    for index, step in enumerate(big):
        step()
        if index % 2 == 1 and small:
            small.pop(0)()
        if index == 2:
            wires.push(73, sent_grad, r_grad, me.flipped())
    while small:
        small.pop(0)()
    final[0] = mine[me.d]
    for item in keeps:
        item.wait()
    wires.got(73, r_grad, me.flipped())
    wide_grad[...] = r_grad[...].astype(jnp.float32)
    came = pltpu.make_async_copy(wide_grad, grads_ref.at[1 - me.s], local.at[0])
    came.start()
    held = final.at[me.s]
    cuts = ((0, 80), (80, 80), (160, 80), (240, 64))
    for n, (start, count) in enumerate(cuts):
        part = pl.ds(start, count)
        wires.push(74 + n, final.at[1 - me.s, part, :], r_across.at[part, :], me.across())
    for n, (start, count) in enumerate(cuts):
        part = pl.ds(start, count)
        wires.got(74 + n, r_across.at[part, :], me.across())
        add_rows(held, [(r_across, 0)], start, count)
        wires.push(78 + n, held.at[part, :], r_beside.at[part, :], me.beside())
    for n, (start, count) in enumerate(cuts):
        part = pl.ds(start, count)
        wires.got(78 + n, r_beside.at[part, :], me.beside())
        total = held[part, :].astype(jnp.float32) + r_beside[part, :].astype(jnp.float32)
        rows[half_rows(me.c, start, count), :] = total.astype(jnp.bfloat16)
        block = rows.at[half_rows(me.c, start, count), :]
        wires.push(82 + n, block, block, me.sibling())
    for n, (start, count) in enumerate(cuts):
        wires.got(82 + n, rows.at[half_rows(1 - me.c, start, count), :], me.sibling())
    for ref, starts in ((projection_ref, (0, 48, 96)), (attention_ref, (144,)), (expand_ref, EXPAND_ROWS)):
        for k, start in enumerate(starts):
            ref[:, k * WIDE : (k + 1) * WIDE] = rows[start : start + 48, :].astype(jnp.float32)
    contract_ref[...] = rows[CONTRACT_ROW : CONTRACT_ROW + 192, :].astype(jnp.float32)
    bias_ref[...] = rows[BIAS_ROW : BIAS_ROW + 16, :].astype(jnp.float32)
    came.wait()
    wires.finish()


def reduce_buffers():
    blocks = lambda *lead: pltpu.VMEM(lead + (WIDE,), jnp.bfloat16)
    return [
        blocks(16, HALF),
        blocks(16, HALF),
        blocks(4, TOP),
        blocks(4, LOW),
        blocks(4, HALF),
        blocks(4, HALF),
        blocks(TOP),
        blocks(LOW),
        blocks(HALF),
        blocks(HALF),
    ]


def reduce_grads(*operands):
    count = 86 + 26
    bf, f32 = jnp.bfloat16, jnp.float32
    blocks = lambda *lead: pltpu.VMEM(lead + (WIDE,), bf)
    whole = pl.BlockSpec(memory_space=pltpu.VMEM)
    away = pl.BlockSpec(memory_space=pl.ANY)
    return pl.pallas_call(
        reduce_kernel,
        out_shape=[
            jax.ShapeDtypeStruct((48, 3 * WIDE), f32),
            jax.ShapeDtypeStruct((48, WIDE), f32),
            jax.ShapeDtypeStruct((48, 4 * WIDE), f32),
            jax.ShapeDtypeStruct((192, WIDE), f32),
            jax.ShapeDtypeStruct((16, WIDE), f32),
            jax.ShapeDtypeStruct((16, 2, 8, WIDE), f32),
            jax.ShapeDtypeStruct((16, 8, PAIR), f32),
            jax.ShapeDtypeStruct((2, TOKENS, WIDE), f32),
        ],
        in_specs=[away, away, whole, whole, whole, away, away],
        out_specs=[whole] * 7 + [away],
        scratch_shapes=[
            *reduce_buffers(),
            blocks(2, HALF),
            blocks(HALF),
            blocks(HALF),
            blocks(ROWS),
            blocks(TOKENS),
            pltpu.VMEM((TOKENS, WIDE), f32),
            pltpu.VMEM((4, 2, 8, WIDE), f32),
            pltpu.VMEM((2, 8, WIDE), f32),
            pltpu.VMEM((3, 16, 8, PAIR), f32),
            pltpu.VMEM((2, 4, 4, 8, PAIR), f32),
            pltpu.VMEM((2, 4, 4, 8, PAIR), f32),
            pltpu.SemaphoreType.DMA((16,)),
            pltpu.SemaphoreType.DMA((4,)),
            pltpu.SemaphoreType.DMA((count,)),
            pltpu.SemaphoreType.DMA((count,)),
        ],
        compiler_params=pltpu.CompilerParams(
            collective_id=1, has_side_effects=True, vmem_limit_bytes=48 * 1024 * 1024
        ),
        cost_estimate=pl.CostEstimate(flops=0, bytes_accessed=60000000, transcendentals=0),
        name="reduce_grads",
    )(*operands)


def seq_peers(me):
    far = [(me.s, me.d, (1 - me.xl) * 2 + core) for core in range(2)]
    return me.sibling(), far


def forward_kernel(
    part, x_ref, mod_ref, bias_ref, w_hbm, *refs
):
    shard_ref, refs = (refs[0], refs[1:]) if part == 0 else (None, refs)
    out_ref, mixed_one_ref, qkv_out, lse_ref, att_out, branch_one_ref, middle_ref, mixed_two_ref, expanded_out, branch_two_ref, *refs = refs
    next_ref, refs = (refs[0], refs[1:]) if part == 0 else (None, refs)
    w, stage, qkv, heads, att, expanded, load, save, send, recv = refs
    me = Place()
    sibling, far = seq_peers(me)
    first_load = pltpu.make_async_copy(w_hbm.at[:, pl.ds(0, 144), :], w.at[:, pl.ds(0, 144), :], load.at[0])
    rest_load = pltpu.make_async_copy(w_hbm.at[:, pl.ds(144, 464), :], w.at[:, pl.ds(144, 464), :], load.at[1])
    first_load.start()
    rest_load.start()
    around = [me.ring(1, 0), me.ring(3, 0), me.ring(0, 1), me.ring(0, 3)] if part == 0 else []
    greet([sibling, *far, *around])
    wires = Wires(send, recv)
    beside = gather_steps(me, wires, 12, shard_ref, next_ref, load.at[2]) if part == 0 else []

    def advance(count):
        for _ in range(min(count, len(beside))):
            beside.pop(0)()

    advance(1)

    row = lambda index: mod_ref[index : index + 1, :]
    bias = lambda index: bias_ref[index : index + 1, :]
    tokens = x_ref[...].astype(jnp.float32)
    normed_one, _ = norm_rows(tokens)
    mixed_one = (normed_one * (1.0 + row(1)) + row(0)).astype(jnp.bfloat16)
    mixed_one_ref[...] = mixed_one
    first_load.wait()

    def project(kind, weight_row, added):
        made = dot(mixed_one, square(w, weight_row))
        if added is not None:
            made = made + added
        made = made.astype(jnp.bfloat16)
        for pair in range(6):
            stage[pair, kind] = made[:, pair * PAIR : (pair + 1) * PAIR]

    project(0, 48, None)
    project(1, 96, bias(1))
    for j in range(3):
        for g in range(2):
            wires.push(2 * j + g, stage.at[3 * g + j, pl.ds(0, 2)], qkv.at[2 + me.c, j, pl.ds(0, 2)], far[g], 2 * j + me.c)
    project(2, 0, bias(0))
    advance(1)
    for j in range(3):
        wires.push(6 + j, stage.at[3 * (1 - me.c) + j], qkv.at[me.c, j], sibling)
    for j in range(3):
        qkv[me.c, j] = stage[3 * me.c + j]

    advance(1)
    for j in range(3):
        wires.got(6 + j, qkv.at[1 - me.c, j], sibling)
        for g in range(2):
            wires.got(2 * j + g, qkv.at[2 + g, j, pl.ds(0, 2)], far[g])

        def queries_step(g, carry):
            keys = qkv[:, j, 0].reshape(4 * TOKENS, PAIR)
            values = qkv[:, j, 1].reshape(4 * TOKENS, PAIR)
            queries = qkv[g, j, 2] * jnp.bfloat16(0.125)
            made = []
            for head in range(2):
                scores = dot(keys, only_head(queries, head), 1, 1)
                top = jnp.max(scores, axis=0, keepdims=True)
                powers = jnp.exp(scores - top)
                sums = jnp.sum(powers, axis=0, keepdims=True)
                lse_ref[(2 * j + head) * 2 + g] = top + jnp.log(sums)
                weights = powers.astype(jnp.bfloat16)
                made.append(dot(values, weights, 0, 0)[head * HEAD : (head + 1) * HEAD] * (1.0 / sums))
            heads[g, j] = jnp.concatenate(made, axis=0).T.astype(jnp.bfloat16)
            return carry

        lax.fori_loop(0, 2, queries_step, 0)
        wires.push(9 + j, heads.at[1 - me.c, j], att.at[3 * me.c + j], sibling)
        att[3 * me.c + j] = heads[me.c, j]
        advance(1)
    qkv_save = pltpu.make_async_copy(qkv, qkv_out, save.at[0])
    qkv_save.start()
    rest_load.wait()
    for j in range(3):
        wires.got(9 + j, att.at[3 * (1 - me.c) + j], sibling)
    att_save = pltpu.make_async_copy(att, att_out, save.at[1])
    att_save.start()
    attended = side_by_side(att)
    branch_one = dot(attended, square(w, 144)) + bias(2)
    branch_one_ref[...] = branch_one
    advance(1)
    middle = tokens + row(2) * branch_one
    middle_ref[...] = middle
    normed_two, _ = norm_rows(middle)
    mixed_two = (normed_two * (1.0 + row(4)) + row(3)).astype(jnp.bfloat16)
    mixed_two_ref[...] = mixed_two
    total = bias(7)
    saves = []
    for k in range(4):
        u = dot(mixed_two, square(w, EXPAND_ROWS[k])) + bias(3 + k)
        expanded[k] = u
        item = pltpu.make_async_copy(expanded.at[k], expanded_out.at[k], save.at[2 + k])
        item.start()
        saves.append(item)
        activated = (0.5 * u * (1.0 + jnp.tanh(ROOT * (u + 0.044715 * (u * u * u))))).astype(jnp.bfloat16)
        total = total + dot(activated, contract_square(w, k))
        advance(1)
    branch_two_ref[...] = total
    out_ref[...] = (middle + row(5) * total).astype(jnp.bfloat16)
    advance(12)
    qkv_save.wait()
    att_save.wait()
    for item in saves:
        item.wait()
    wires.finish()


def block_forward(part, tokens, modulation, bias, blocks, *shard):
    shape = lambda dims, dtype: jax.ShapeDtypeStruct(dims, dtype)
    bf, f32 = jnp.bfloat16, jnp.float32
    whole = pl.BlockSpec(memory_space=pltpu.VMEM)
    away = pl.BlockSpec(memory_space=pl.ANY)
    return pl.pallas_call(
        functools.partial(forward_kernel, part),
        out_shape=[
            shape((TOKENS, WIDE), bf),
            shape((TOKENS, WIDE), bf),
            shape((4, 3, 3, TOKENS, PAIR), bf),
            shape((12, 1, TOKENS), f32),
            shape((6, TOKENS, PAIR), bf),
            shape((TOKENS, WIDE), f32),
            shape((TOKENS, WIDE), f32),
            shape((TOKENS, WIDE), bf),
            shape((4, TOKENS, WIDE), f32),
            shape((TOKENS, WIDE), f32),
        ]
        + [shape((16, ROWS, WIDE), bf) for _ in shard],
        in_specs=[whole, whole, whole, away] + [away for _ in shard],
        out_specs=[whole, whole, away, whole, away, whole, whole, whole, away, whole] + [away for _ in shard],
        scratch_shapes=[
            pltpu.VMEM((16, ROWS, WIDE), bf),
            pltpu.VMEM((6, 3, TOKENS, PAIR), bf),
            pltpu.VMEM((4, 3, 3, TOKENS, PAIR), bf),
            pltpu.VMEM((2, 3, TOKENS, PAIR), bf),
            pltpu.VMEM((6, TOKENS, PAIR), bf),
            pltpu.VMEM((4, TOKENS, WIDE), f32),
            pltpu.SemaphoreType.DMA((3,)),
            pltpu.SemaphoreType.DMA((6,)),
            pltpu.SemaphoreType.DMA((48,)),
            pltpu.SemaphoreType.DMA((48,)),
        ],
        compiler_params=pltpu.CompilerParams(
            collective_id=2 + part, has_side_effects=True, vmem_limit_bytes=56 * 1024 * 1024
        ),
        cost_estimate=pl.CostEstimate(flops=5 * 10**9, bytes_accessed=25 * 10**6, transcendentals=4 * 10**6),
        name=("forward_first", "forward_second")[part],
    )(tokens, modulation, bias, blocks, *shard)


def backward_kernel(
    part, grad_ref, x_ref, mod_ref, w_hbm, mixed_one_ref, qkv_in, lse_ref, att_ref, branch_one_ref, middle_ref, mixed_two_ref, expanded_in, branch_two_ref, *refs
):
    if part == 0:
        later_ref, *refs = refs
    else:
        kept_out, sent_out, *refs = refs
    input_grad_ref, terms_ref, grads_out, *refs = refs
    extra_out, *refs = refs
    carried, refs = (input_grad_ref, refs) if part == 0 else (refs[0], refs[1:])
    w, expanded, qkv, stage, given, dkv, dq, own, far_out, far_in, side_out, side_in, joined, load, save, send, recv, *refs = refs
    me = Place()
    sibling, far = seq_peers(me)
    c, other = me.c, 1 - me.c
    back_load = pltpu.make_async_copy(w_hbm.at[:, pl.ds(192, 416), :], w.at[:, pl.ds(192, 416), :], load.at[0])
    expanded_load = pltpu.make_async_copy(expanded_in, expanded, load.at[1])
    front_load = pltpu.make_async_copy(w_hbm.at[:, pl.ds(0, 192), :], w.at[:, pl.ds(0, 192), :], load.at[2])
    qkv_load = pltpu.make_async_copy(qkv_in, qkv, load.at[3])
    back_load.start()
    expanded_load.start()
    front_load.start()
    qkv_load.start()
    around = [me.ring(1, 0), me.ring(3, 0), me.ring(0, 1), me.ring(0, 3)] if part == 0 else [me.flipped()]
    greet([sibling, *far, *around])
    wires = Wires(send, recv)
    beside = reduce_steps(me, wires, 10, later_ref, refs[-1], refs[:-1]) if part == 0 else []

    def advance(count):
        for _ in range(min(count, len(beside))):
            beside.pop(0)()

    advance(1)
    if part == 1:
        keep_out = pltpu.make_async_copy(kept_out, extra_out.at[me.s], load.at[4])
        keep_out.start()
        wires.push(10, sent_out, extra_out.at[me.s], me.flipped())
    saves = []

    def keep(index, start, count):
        rows = pl.ds(start, count)
        item = pltpu.make_async_copy(w.at[:, rows, :], grads_out.at[:, rows, :], save.at[index])
        item.start()
        saves.append(item)

    row = lambda index: mod_ref[index : index + 1, :]
    gradient = grad_ref[...].astype(jnp.float32)
    branch_two_grad = (row(5) * gradient).astype(jnp.bfloat16)
    gate_two_grad = column_sum(gradient * branch_two_ref[...])
    contract_bias_grad = column_sum(branch_two_grad)
    mixed_two = mixed_two_ref[...]
    mixed_two_grad = None
    expand_bias_grads = []
    back_load.wait()
    expanded_load.wait()
    for k in range(4):
        u = expanded[k]
        squared = u * u
        tanh = jnp.tanh(ROOT * (u + 0.044715 * (squared * u)))
        half = 0.5 * (1.0 + tanh)
        activated = (u * half).astype(jnp.bfloat16)
        slope = half + 0.5 * u * (1.0 - tanh * tanh) * (ROOT * (1.0 + (3.0 * 0.044715) * squared))
        expanded_grad = (dot(branch_two_grad, contract_square(w, k), 1, 1) * slope).astype(jnp.bfloat16)
        start = EXPAND_ROWS[k]
        expand_bias_grads.append(column_sum(expanded_grad))
        term = dot(expanded_grad, square(w, start), 1, 1)
        mixed_two_grad = term if mixed_two_grad is None else mixed_two_grad + term
        w[4 * k : 4 * k + 4, CONTRACT_ROW : CONTRACT_ROW + 192, :] = (
            dot(activated, branch_two_grad, 0, 0).astype(jnp.bfloat16).reshape(4, 192, WIDE)
        )
        w[:, start : start + 48, :] = dot(mixed_two, expanded_grad, 0, 0).astype(jnp.bfloat16).reshape(16, 48, WIDE)
        advance(1)
    keep(0, 304, 288)
    keep(1, 192, 96)
    normed_two, inv_two = norm_rows(middle_ref[...])
    scale_two_grad = column_sum(mixed_two_grad * normed_two)
    shift_two_grad = column_sum(mixed_two_grad)
    middle_grad = gradient + norm_back(mixed_two_grad * (1.0 + row(4)), normed_two, inv_two)
    gate_one_grad = column_sum(middle_grad * branch_one_ref[...])
    branch_one_grad = (row(2) * middle_grad).astype(jnp.bfloat16)
    front_load.wait()
    attended_grad = dot(branch_one_grad, square(w, 144), 1, 1).astype(jnp.bfloat16)
    for pair in range(6):
        stage[pair] = attended_grad[:, pair * PAIR : (pair + 1) * PAIR]
    wires.push(0, stage.at[pl.ds(3 * other, 3)], given.at[c], sibling)
    advance(1)
    given[c] = stage[pl.ds(3 * c, 3)]
    carried[...] = middle_grad
    w[:, 144:192, :] = dot(side_by_side(att_ref), branch_one_grad, 0, 0).astype(jnp.bfloat16).reshape(16, 48, WIDE)
    keep(2, 144, 48)
    attention_bias_grad = column_sum(branch_one_grad)
    advance(1)
    qkv_load.wait()
    wires.got(0, given.at[other], sibling)

    for j in range(3):
        dkv[...] = jnp.zeros_like(dkv)

        def queries_step(g, carry):
            keys = qkv[:, j, 0].reshape(4 * TOKENS, PAIR)
            values = qkv[:, j, 1].reshape(4 * TOKENS, PAIR)
            queries = qkv[g, j, 2] * jnp.bfloat16(0.125)
            output_grads = given[g, j]
            key_sums, value_sums, query_parts = 0.0, 0.0, []
            for head in range(2):
                head_queries = only_head(queries, head)
                head_grads = only_head(output_grads, head)
                scores = dot(keys, head_queries, 1, 1)
                probs = jnp.exp(scores - lse_ref[(2 * j + head) * 2 + g])
                weight_grads = dot(values, head_grads, 1, 1)
                centre = jnp.sum(probs * weight_grads, axis=0, keepdims=True)
                score_grads = (probs * (weight_grads - centre)).astype(jnp.bfloat16)
                key_sums = key_sums + dot(score_grads, head_queries)
                value_sums = value_sums + dot(probs.astype(jnp.bfloat16), head_grads)
                query_parts.append(dot(keys, score_grads, 0, 0)[head * HEAD : (head + 1) * HEAD])
            dq[g] = jnp.concatenate(query_parts, axis=0).T * 0.125
            dkv[0] += key_sums.reshape(4, TOKENS, PAIR)
            dkv[1] += value_sums.reshape(4, TOKENS, PAIR)
            return carry

        lax.fori_loop(0, 2, queries_step, 0)
        for g in range(2):
            far_out[j, g] = dkv[:, 2 + g].astype(jnp.bfloat16)
            wires.push(1 + 2 * j + g, far_out.at[j, g], far_in.at[j, c], far[g], 1 + 2 * j + c)
        side_out[j, 0:2] = dkv[:, other].astype(jnp.bfloat16)
        side_out[j, 2] = dq[other].astype(jnp.bfloat16)
        wires.push(7 + j, side_out.at[j], side_in.at[j], sibling)
        own[j, 0:2] = dkv[:, c]
        own[j, 2] = dq[c]
        advance(1 if j == 0 else 2)

    for j in range(3):
        wires.got(7 + j, side_in.at[j], sibling)
        for g in range(2):
            wires.got(1 + 2 * j + g, far_in.at[j, g], far[g])
        for kind in range(2):
            joined[kind, 3 * c + j] = (own[j, kind] + far_in[j, c, kind].astype(jnp.float32)).astype(jnp.bfloat16)
            joined[kind, 3 * other + j] = (
                side_in[j, kind].astype(jnp.float32) + far_in[j, other, kind].astype(jnp.float32)
            ).astype(jnp.bfloat16)
        joined[2, 3 * c + j] = own[j, 2].astype(jnp.bfloat16)
        joined[2, 3 * other + j] = side_in[j, 2]
    mixed_one = mixed_one_ref[...]
    mixed_one_grad, bias_grads = None, []
    for kind, start in ((0, 48), (1, 96), (2, 0)):
        piece = side_by_side(joined, (kind,))
        bias_grads.append(column_sum(piece))
        term = dot(piece, square(w, start), 1, 1)
        mixed_one_grad = term if mixed_one_grad is None else mixed_one_grad + term
        w[:, start : start + 48, :] = dot(mixed_one, piece, 0, 0).astype(jnp.bfloat16).reshape(16, 48, WIDE)
        advance(1)
    keep(3, 0, 144)
    small = jnp.concatenate(
        [
            bias_grads[2],
            bias_grads[1],
            attention_bias_grad,
            *expand_bias_grads,
            contract_bias_grad,
            jnp.zeros((8, WIDE), jnp.float32),
        ],
        axis=0,
    ).astype(jnp.bfloat16)
    w[:, BIAS_ROW : BIAS_ROW + 16, :] = jnp.broadcast_to(small[None], (16, 16, WIDE))
    w[:, 592:608, :] = jnp.zeros((16, 16, WIDE), jnp.bfloat16)
    keep(4, BIAS_ROW, 16)
    keep(5, 592, 16)
    normed_one, inv_one = norm_rows(x_ref[...].astype(jnp.float32))
    terms_ref[...] = jnp.concatenate(
        [
            column_sum(mixed_one_grad),
            column_sum(mixed_one_grad * normed_one),
            gate_one_grad,
            shift_two_grad,
            scale_two_grad,
            gate_two_grad,
            jnp.zeros((2, WIDE), jnp.float32),
        ],
        axis=0,
    )
    result = carried[...] + norm_back(mixed_one_grad * (1.0 + row(1)), normed_one, inv_one)
    input_grad_ref[...] = result.astype(input_grad_ref.dtype)
    advance(16)
    if part == 0:
        rows_save = pltpu.make_async_copy(refs[0].at[me.d], extra_out, load.at[0])
        rows_save.start()
        rows_save.wait()
    else:
        keep_out.wait()
        wires.got(10, extra_out.at[1 - me.s], me.flipped())
    for item in saves:
        item.wait()
    wires.finish()


def block_backward(part, gradient, tokens, modulation, blocks, kept, *later):
    shape = lambda dims, dtype: jax.ShapeDtypeStruct(dims, dtype)
    bf, f32 = jnp.bfloat16, jnp.float32
    whole = pl.BlockSpec(memory_space=pltpu.VMEM)
    away = pl.BlockSpec(memory_space=pl.ANY)
    return pl.pallas_call(
        functools.partial(backward_kernel, part),
        out_shape=[
            shape((TOKENS, WIDE), f32 if part == 0 else bf),
            shape((8, WIDE), f32),
            shape((16, ROWS, WIDE), bf),
        ]
        + [shape((HALF, WIDE), bf) if part == 0 else shape((2, TOKENS, WIDE), bf)],
        in_specs=[whole, whole, whole, away, whole, away, whole, whole, whole, whole, whole, away, whole] + [away for _ in later],
        out_specs=[whole, whole, away, away],
        scratch_shapes=([] if part == 0 else [pltpu.VMEM((TOKENS, WIDE), f32)])
        + [
            pltpu.VMEM((16, ROWS, WIDE), bf),
            pltpu.VMEM((4, TOKENS, WIDE), f32),
            pltpu.VMEM((4, 3, 3, TOKENS, PAIR), bf),
            pltpu.VMEM((6, TOKENS, PAIR), bf),
            pltpu.VMEM((2, 3, TOKENS, PAIR), bf),
            pltpu.VMEM((2, 4, TOKENS, PAIR), f32),
            pltpu.VMEM((2, TOKENS, PAIR), f32),
            pltpu.VMEM((3, 3, TOKENS, PAIR), f32),
            pltpu.VMEM((3, 2, 2, TOKENS, PAIR), bf),
            pltpu.VMEM((3, 2, 2, TOKENS, PAIR), bf),
            pltpu.VMEM((3, 3, TOKENS, PAIR), bf),
            pltpu.VMEM((3, 3, TOKENS, PAIR), bf),
            pltpu.VMEM((3, 6, TOKENS, PAIR), bf),
            pltpu.SemaphoreType.DMA((5,)),
            pltpu.SemaphoreType.DMA((6,)),
            pltpu.SemaphoreType.DMA((46,)),
            pltpu.SemaphoreType.DMA((46,)),
        ]
        + ([*reduce_buffers(), pltpu.SemaphoreType.DMA((16,))] if part == 0 else []),
        compiler_params=pltpu.CompilerParams(
            collective_id=4 + part, has_side_effects=True, vmem_limit_bytes=60 * 1024 * 1024
        ),
        cost_estimate=pl.CostEstimate(flops=12 * 10**9, bytes_accessed=45 * 10**6, transcendentals=4 * 10**6),
        name=("backward_first", "backward_second")[part],
    )(gradient, tokens, modulation, blocks, *kept, *later)


def bias_rows(biases):
    parts = [
        biases[:, :96].reshape(2, WIDE),
        biases[:, 96:144].reshape(1, WIDE),
        biases[:, 144:336].reshape(4, WIDE),
        biases[:, 336:384].reshape(1, WIDE),
    ]
    added = jnp.pad(biases[:, 384:672].reshape(6, WIDE), ((0, 2), (0, 0)))
    return jnp.concatenate(parts), added


def with_biases(made, bias, place):
    own = lambda part, size: lax.dynamic_slice_in_dim(part.reshape(-1), place * size, size)
    projection, attention, expand, contract = made
    return [
        projection,
        own(bias[0:2], 96),
        attention,
        own(bias[2:3], 48),
        expand,
        own(bias[3:7], 192),
        contract,
        own(bias[7:8], 48),
    ]


def on_device(
    latents,
    conditions,
    output_cotangent,
    modulation_weight,
    modulation_bias,
    projection_weight,
    projection_bias,
    attention_weight,
    attention_bias,
    expand_weight,
    expand_bias,
    contract_weight,
    contract_bias,
):
    section = lax.axis_index("section")
    place = lax.axis_index("dp")
    is_first = section == 0
    biases = jnp.concatenate(
        [projection_bias[0], attention_bias[0], expand_bias[0], contract_bias[0], modulation_bias[0]]
    )
    extra = jnp.pad(biases[None], ((0, 15), (0, WIDE - biases.shape[0])))
    pieces = jnp.pad(conditions[:, 0].reshape(2, 16, 48).swapaxes(0, 1), ((0, 0), (0, 6), (0, PAIR - 48)))
    owned_weight = jnp.pad(modulation_weight[0], ((0, PAIR - 48), (0, 0)))
    first_blocks, shard, own_conds, modulations = gather_weights(
        projection_weight[0], attention_weight[0], expand_weight[0], contract_weight[0], extra, pieces, owned_weight
    )
    first_bias, first_added = bias_rows(first_blocks[:, BIAS_ROW].astype(jnp.float32))
    first_modulation = modulations[0] + first_added

    tokens = lax.dynamic_index_in_dim(latents, section, 0, keepdims=False)[0]
    cotangent = lax.dynamic_index_in_dim(output_cotangent, section, 0, keepdims=False)[0]
    first_output, *first_kept, second_blocks = block_forward(0, tokens, first_modulation, first_bias, first_blocks, shard)
    second_bias, second_added = bias_rows(second_blocks[:, BIAS_ROW].astype(jnp.float32))
    second_modulation = modulations[1] + second_added
    second_output, *second_kept = block_forward(1, first_output, second_modulation, second_bias, second_blocks)
    second_grad, second_terms, second_made, section_outputs = block_backward(
        1,
        cotangent,
        first_output,
        second_modulation,
        second_blocks,
        second_kept,
        jnp.where(is_first, first_output, second_output),
        jnp.where(is_first, second_output, first_output),
    )
    first_grad, first_terms, first_made, second_rows = block_backward(
        0, second_grad, tokens, first_modulation, first_blocks, first_kept, second_made
    )

    rounded_grad = second_grad.astype(jnp.float32)
    *made, bias, terms, cond_terms, input_grads = reduce_grads(
        first_made,
        second_rows,
        first_terms,
        second_terms,
        owned_weight,
        jnp.where(is_first, first_grad, rounded_grad),
        jnp.where(is_first, second_grad, first_grad.astype(jnp.bfloat16)),
    )
    reduced = [grad[None] for grad in with_biases(made, bias, place)]
    section_outputs = section_outputs[None, :, None]
    input_grads = input_grads[None, :, None]
    terms = terms[:, :, :6].reshape(16, 2, -1)
    own_silu = jax.nn.silu(own_conds[:, :2, :48]).astype(jnp.bfloat16)
    modulation_weight_grad = jnp.einsum(
        "imk,ime->ke", own_silu, terms.astype(jnp.bfloat16), preferred_element_type=jnp.float32
    )
    modulation_bias_grad = lax.dynamic_slice_in_dim(jnp.sum(terms, axis=(0, 1)), place * 288, 288)
    cond_terms = cond_terms[:, :2, :48].swapaxes(0, 1).reshape(2, 1, WIDE)
    condition_grads = jax.vjp(jax.nn.silu, conditions)[1](cond_terms)[0]
    return (
        section_outputs,
        input_grads,
        condition_grads,
        modulation_weight_grad[None],
        modulation_bias_grad[None],
        *reduced,
    )


def solution(mesh):
    return jax.shard_map(
        on_device,
        mesh=mesh,
        in_specs=(
            P(None, "dp", "seq", None),
            P(None, "dp", None),
            P(None, "dp", "seq", None),
            P("section", "dp", None),
            P("section", "dp"),
            P("section", "dp", None),
            P("section", "dp"),
            P("section", "dp", None),
            P("section", "dp"),
            P("section", "dp", None),
            P("section", "dp"),
            P("section", "dp", None),
            P("section", "dp"),
        ),
        out_specs=(
            P("section", None, "dp", "seq", None),
            P("section", None, "dp", "seq", None),
            P(None, "dp", None),
            P("section", "dp", None),
            P("section", "dp"),
            P("section", "dp", None),
            P("section", "dp"),
            P("section", "dp", None),
            P("section", "dp"),
            P("section", "dp", None),
            P("section", "dp"),
            P("section", "dp", None),
            P("section", "dp"),
        ),
        check_vma=False,
    )
```

```python
import functools

import jax
import jax.numpy as jnp
from jax import lax
from jax.experimental import pallas as pl
from jax.experimental.pallas import tpu as pltpu
from jax.sharding import PartitionSpec as P

HEAD = 64


MESH = pl.DeviceIdType.MESH
ROWS = 608
HALF = ROWS // 2
TOP = 160
LOW = HALF - TOP
WIDE = 768
OFFSETS = (0, 3, 1, 2)


class Place:
    def __init__(self):
        self.s = lax.axis_index("section")
        self.d = lax.axis_index("dp")
        self.q = lax.axis_index("seq")
        y, z = self.d // 4, lax.rem(self.d, 4)
        self.xl, self.c = self.q // 2, lax.rem(self.q, 2)
        self.a = (1 - self.c) * z + self.c * y
        self.b = (1 - self.c) * y + self.c * z

    def dp(self, ka, kb):
        aa = lax.rem(self.a + ka, 4)
        bb = lax.rem(self.b + kb, 4)
        return aa * (1 + 3 * self.c) + bb * (4 - 3 * self.c)

    def ring(self, ka, kb):
        return (self.s, self.dp(ka, kb), self.q)

    def sibling(self):
        return (self.s, self.d, self.xl * 2 + 1 - self.c)

    def across(self):
        return (1 - self.s, self.d, (1 - self.xl) * 2 + self.c)

    def beside(self):
        return (self.s, self.d, (1 - self.xl) * 2 + self.c)

    def askew(self):
        return (self.s, self.d, (1 - self.xl) * 2 + 1 - self.c)

    def flipped(self):
        return (1 - self.s, self.d, self.q)

    def grid_peers(self):
        return [self.ring(k, 0) for k in (1, 3, 2)] + [self.ring(0, k) for k in (1, 3, 2)]


def greet(devices):
    barrier = pltpu.get_barrier_semaphore()
    for device in devices:
        pl.semaphore_signal(barrier, inc=1, device_id=device, device_id_type=MESH)
    pl.semaphore_wait(barrier, len(devices))


def half_rows(core, offset, count):
    return pl.ds(pl.multiple_of(core * HALF + offset, 16), count)


class Wires:
    def __init__(self, send, recv):
        self.send, self.recv, self.started = send, recv, []

    def push(self, index, source, target, device, landing=None):
        item = pltpu.make_async_remote_copy(
            src_ref=source,
            dst_ref=target,
            send_sem=self.send.at[index],
            recv_sem=self.recv.at[index if landing is None else landing],
            device_id=device,
            device_id_type=MESH,
        )
        item.start()
        self.started.append(item)

    def got(self, index, target, device):
        pltpu.make_async_remote_copy(
            src_ref=target,
            dst_ref=target,
            send_sem=self.send.at[0],
            recv_sem=self.recv.at[index],
            device_id=device,
            device_id_type=MESH,
        ).wait_recv()

    def finish(self):
        for item in self.started:
            item.wait_send()


TOKENS = 256
PAIR = 128
EXPAND_ROWS = (192, 240, 304, 352)
CONTRACT_ROW = 400
BIAS_ROW = 288
ROOT = (2.0 / 3.141592653589793) ** 0.5


def norm_rows(values):
    row_mean = jnp.mean(values, axis=-1, keepdims=True)
    centered = values - row_mean
    variance = jnp.mean(centered * centered, axis=-1, keepdims=True)
    inv_std = lax.rsqrt(variance + 1e-06)
    return (centered * inv_std, inv_std)


def norm_back(gradient, normed, inv_std):
    row_mean = jnp.mean(gradient, axis=-1, keepdims=True)
    along = jnp.mean(gradient * normed, axis=-1, keepdims=True)
    return inv_std * (gradient - row_mean - normed * along)


def dot(left, right, left_dim=1, right_dim=0):
    return lax.dot_general(
        left, right, (((left_dim,), (right_dim,)), ((), ())), preferred_element_type=jnp.float32
    )


def column_sum(values):
    return jnp.sum(values.astype(jnp.float32), axis=0, keepdims=True)


def square(w, row):
    return w[:, row : row + 48, :].reshape(WIDE, WIDE)


def contract_square(w, part):
    return w[4 * part : 4 * part + 4, CONTRACT_ROW : CONTRACT_ROW + 192, :].reshape(WIDE, WIDE)


def side_by_side(ref, lead=()):
    return jnp.concatenate([ref[(*lead, pair)] for pair in range(6)], axis=1)


def head_lanes(head):
    lane = lax.broadcasted_iota(jnp.int32, (1, PAIR), 1)
    return (lane // HEAD) == head


def only_head(values, head):
    return jnp.where(head_lanes(head), values, jnp.zeros_like(values))


def gather_steps(me, wires, base, source, w_ref, local):
    right_a, left_a = me.ring(1, 0), me.ring(3, 0)
    right_b, left_b = me.ring(0, 1), me.ring(0, 3)
    sibling = me.sibling()

    def slot(ka, kb, offset=0, count=HALF):
        return w_ref.at[me.dp(ka, kb), half_rows(me.c, offset, count), :]

    def got(index, target):
        wires.got(base + index, target, sibling)

    def push(index, origin, target, device):
        wires.push(base + index, origin, target, device)

    def to_side(ka, kb, origin=None):
        block = slot(ka, kb)
        push(20 + 4 * ka + kb, block if origin is None else origin, block, sibling)

    def spread_b(ka, origin=None):
        block = slot(ka, 0)
        origin = block if origin is None else origin
        push(4 + 4 * ka, origin, block, right_b)
        push(5 + 4 * ka, origin, block, left_b)

    own = pltpu.make_async_copy(source, slot(0, 0), local)

    def start():
        own.start()
        push(0, source, slot(0, 0), right_a)
        push(1, source, slot(0, 0), left_a)
        spread_b(0, source)
        to_side(0, 0, source)

    def forward_a():
        got(0, slot(3, 0))
        push(2, slot(3, 0, 0, TOP), slot(3, 0, 0, TOP), right_a)
        spread_b(3)
        to_side(3, 0)
        got(1, slot(1, 0))
        push(3, slot(1, 0, TOP, LOW), slot(1, 0, TOP, LOW), left_a)
        spread_b(1)
        to_side(1, 0)

    def end_a():
        got(2, slot(2, 0, 0, TOP))
        got(3, slot(2, 0, TOP, LOW))
        spread_b(2)
        to_side(2, 0)

    def forward_b(ka):
        at = 4 + 4 * ka
        got(at, slot(ka, 3))
        push(at + 2, slot(ka, 3, 0, TOP), slot(ka, 3, 0, TOP), right_b)
        to_side(ka, 3)
        got(at + 1, slot(ka, 1))
        push(at + 3, slot(ka, 1, TOP, LOW), slot(ka, 1, TOP, LOW), left_b)
        to_side(ka, 1)

    def end_b(ka):
        at = 4 + 4 * ka
        got(at + 2, slot(ka, 2, 0, TOP))
        got(at + 3, slot(ka, 2, TOP, LOW))
        to_side(ka, 2)

    def finish():
        own.wait()
        for ka in range(4):
            for kb in range(4):
                got(20 + 4 * ka + kb, w_ref.at[me.dp(kb, ka), half_rows(1 - me.c, 0, HALF), :])

    steps = [start, forward_a, end_a]
    steps += [functools.partial(forward_b, ka) for ka in OFFSETS]
    steps += [functools.partial(end_b, ka) for ka in OFFSETS]
    return steps + [finish]


def swap_steps(me, wires, base, pieces, first, second, result):
    def start():
        for ka in range(4):
            for kb in range(4):
                first[0, ka, kb] = pieces[me.dp(ka, kb)]
        for k in (1, 2, 3):
            wires.push(base + k - 1, first.at[0, k], first.at[1, k], me.ring(k, 0))

    def middle():
        for kb in range(4):
            second[0, kb, 0] = first[0, 0, kb]
        for k in (1, 2, 3):
            wires.got(base + k - 1, first.at[1, k], me.sibling())
            for kb in range(4):
                second[0, kb, k] = first[1, k, kb]
        for k in (1, 2, 3):
            wires.push(base + 2 + k, second.at[0, k], second.at[1, k], me.ring(0, k))

    def end():
        for ka in range(4):
            result[me.dp((4 - ka) % 4, 0)] = second[0, 0, ka]
        for k in (1, 2, 3):
            wires.got(base + 2 + k, second.at[1, k], me.sibling())
            for ka in range(4):
                result[me.dp((4 - ka) % 4, 4 - k)] = second[1, k, ka]

    return [start, middle, end]


def modulation_steps(me, wires, base, conds_ref, weight_ref, columns_ref, mod_ref, first, second, partial, b_sums, a_sums, across_sums):
    swap = swap_steps(me, wires, base, conds_ref, first, second, columns_ref)

    def multiply():
        swap[2]()
        rows = lax.broadcasted_iota(jnp.int32, (8, 32), 0)
        taken = lax.broadcasted_iota(jnp.int32, (8, 32), 1)
        pick = jnp.where(taken == (rows // 2) * 8 + lax.rem(rows, 2), 1.0, 0.0).astype(jnp.bfloat16)
        for kb in range(4):
            found = jnp.concatenate([columns_ref[me.dp((4 - ka) % 4, (4 - kb) % 4)] for ka in range(4)], axis=0)
            silu = (found / (1.0 + jnp.exp(-found))).astype(jnp.bfloat16)
            silu = dot(pick, silu).astype(jnp.bfloat16)
            partial[kb] = dot(silu, weight_ref[...])
        for k in (1, 2, 3):
            wires.push(base + 5 + k, partial.at[k], b_sums.at[k - 1], me.ring(0, 4 - k))

    def add_b():
        for k in (1, 2, 3):
            wires.got(base + 5 + k, b_sums.at[k - 1], me.sibling())
        a_sums[0] = partial[0] + b_sums[0] + b_sums[1] + b_sums[2]
        for k in (1, 2, 3):
            wires.push(base + 8 + k, a_sums.at[0], a_sums.at[k], me.ring(4 - k, 0))

    def add_a():
        for k in (1, 2, 3):
            wires.got(base + 8 + k, a_sums.at[k], me.sibling())
        total = a_sums[0, 0:2]
        for k in (1, 2, 3):
            total = total + a_sums[k, 2 * k : 2 * k + 2]
        across_sums[0] = jnp.concatenate([total, jnp.zeros((6, total.shape[1]), jnp.float32)], axis=0)
        wires.push(base + 12, across_sums.at[0], across_sums.at[1], me.flipped())

    def end():
        wires.got(base + 12, across_sums.at[1], me.sibling())
        lead = me.s == 0
        kept = jnp.where(lead, across_sums[0, 0:1], across_sums[0, 1:2])
        came = jnp.where(lead, across_sums[1, 0:1], across_sums[1, 1:2])
        zeros = jnp.zeros((2, WIDE), jnp.float32)
        for block, row in ((0, jnp.where(lead, kept, came)), (1, jnp.where(lead, came, kept))):
            mod_ref[block] = jnp.concatenate([row[:, r * WIDE : (r + 1) * WIDE] for r in range(6)] + [zeros], axis=0)

    return [swap[0], swap[1], multiply, add_b, add_a, end]


def gather_kernel(projection_ref, attention_ref, expand_ref, contract_ref, extra_ref, conds_ref, weight_ref, first_ref, shard_out, columns_ref, mod_ref, shard, c_first, c_second, partial, b_sums, a_sums, across_sums, local, send, recv):
    me = Place()
    columns = lambda ref, k: ref.at[:, pl.ds(k * WIDE, WIDE)]
    halves = (
        [columns(projection_ref, k) for k in range(3)] + [attention_ref, columns(expand_ref, 0), columns(expand_ref, 1), extra_ref],
        [columns(expand_ref, 2), columns(expand_ref, 3), contract_ref, extra_ref],
    )

    def pack(core):
        items, start = [], 0
        for part in halves[core]:
            count = part.shape[0]
            items.append(pltpu.make_async_copy(part, shard.at[me.s, pl.ds(start, count), :], local.at[2 + len(items)]))
            start += count
        for item in items:
            item.start()
        for item in items:
            item.wait()

    for core in range(2):
        pl.when(me.c == core)(functools.partial(pack, core))
    mine = shard.at[me.s]
    greet(me.grid_peers() + [me.across(), me.flipped(), me.sibling()])
    wires = Wires(send, recv)
    wires.push(0, mine, shard.at[me.s], me.across())
    small = modulation_steps(me, wires, 37, conds_ref, weight_ref, columns_ref, mod_ref, c_first, c_second, partial, b_sums, a_sums, across_sums)
    small[0]()
    small[1]()
    wires.got(0, shard.at[1 - me.s], me.across())
    handed = pltpu.make_async_copy(shard.at[1], shard_out, local.at[1])
    handed.start()
    one = gather_steps(me, wires, 1, shard.at[0], first_ref, local.at[0])
    one[0]()
    small[2]()
    for step in one[1:5]:
        step()
    small[3]()
    for step in one[5:8]:
        step()
    small[4]()
    for step in one[8:11]:
        step()
    small[5]()
    one[11]()
    handed.wait()
    wires.finish()


def gather_weights(*operands):
    bf, f32 = jnp.bfloat16, jnp.float32
    wide = operands[-1].shape[1]
    whole = pl.BlockSpec(memory_space=pltpu.VMEM)
    away = pl.BlockSpec(memory_space=pl.ANY)
    return pl.pallas_call(
        gather_kernel,
        out_shape=[
            jax.ShapeDtypeStruct((16, ROWS, WIDE), bf),
            jax.ShapeDtypeStruct((HALF, WIDE), bf),
            jax.ShapeDtypeStruct((16, 8, PAIR), f32),
            jax.ShapeDtypeStruct((2, 8, WIDE), f32),
        ],
        in_specs=[away] * 5 + [whole, whole],
        out_specs=[away, away, whole, whole],
        scratch_shapes=[
            pltpu.VMEM((2, HALF, WIDE), bf),
            pltpu.VMEM((2, 4, 4, 8, PAIR), f32),
            pltpu.VMEM((2, 4, 4, 8, PAIR), f32),
            pltpu.VMEM((4, 8, wide), f32),
            pltpu.VMEM((3, 8, wide), f32),
            pltpu.VMEM((4, 8, wide), f32),
            pltpu.VMEM((2, 8, wide), f32),
            pltpu.SemaphoreType.DMA((9,)),
            pltpu.SemaphoreType.DMA((50,)),
            pltpu.SemaphoreType.DMA((50,)),
        ],
        compiler_params=pltpu.CompilerParams(
            collective_id=0, has_side_effects=True, vmem_limit_bytes=60 * 1024 * 1024
        ),
        cost_estimate=pl.CostEstimate(flops=0, bytes_accessed=60000000, transcendentals=0),
        name="gather_weights",
    )(*operands)


def reduce_steps(me, wires, base, source, load, buffers):
    mine, sib, r_top, r_low, r_left, r_right, a_top, a_low, a_left, a_right = buffers
    right_a, left_a = me.ring(1, 0), me.ring(3, 0)
    right_b, left_b = me.ring(0, 1), me.ring(0, 3)
    sibling = me.sibling()

    def push(index, origin, target, device):
        wires.push(base + index, origin, target, device)

    def got(index, target):
        wires.got(base + index, target, sibling)

    def block(ka, kb):
        return mine.at[me.dp(ka, kb)]

    def from_side(ka, kb):
        return sib.at[me.dp(ka, kb)]

    def fetch(ka, kb):
        dp = me.dp(ka, kb)
        return pltpu.make_async_copy(source.at[dp, half_rows(me.c, 0, HALF), :], mine.at[dp], load.at[4 * ka + kb])

    def start():
        for kb in (2, 1, 3, 0):
            for ka in (2, 1, 3, 0):
                fetch(ka, kb).start()
                dp = me.dp(kb, ka)
                push(4 * ka + kb, source.at[dp, half_rows(1 - me.c, 0, HALF), :], sib.at[dp], sibling)

    def total(target, parts, offset=0, count=HALF):
        add_rows(target, parts, offset, count)

    def ready(ka, kb):
        fetch(ka, kb).wait()
        got(4 * ka + kb, from_side(ka, kb))

    def far_b(ka):
        ready(ka, 2)
        far = block(ka, 2)
        total(far, [(from_side(ka, 2), 0)])
        push(16 + 4 * ka, far.at[pl.ds(0, TOP), :], r_top.at[ka], right_b)
        push(17 + 4 * ka, far.at[pl.ds(TOP, LOW), :], r_low.at[ka], left_b)

    def near_b(ka):
        at = 16 + 4 * ka
        ready(ka, 1)
        got(at, r_top.at[ka])
        near, side = block(ka, 1), from_side(ka, 1)
        total(near, [(side, 0), (r_top.at[ka], 0)], 0, TOP)
        total(near, [(side, 0)], TOP, LOW)
        push(at + 2, near, r_left.at[ka], right_b)
        ready(ka, 3)
        got(at + 1, r_low.at[ka])
        near, side = block(ka, 3), from_side(ka, 3)
        total(near, [(side, 0)], 0, TOP)
        total(near, [(side, 0), (r_low.at[ka], TOP)], TOP, LOW)
        push(at + 3, near, r_right.at[ka], left_b)

    def own_b(ka):
        at = 16 + 4 * ka
        ready(ka, 0)
        got(at + 2, r_left.at[ka])
        got(at + 3, r_right.at[ka])
        total(block(ka, 0), [(from_side(ka, 0), 0), (r_left.at[ka], 0), (r_right.at[ka], 0)])
        if ka == 2:
            far = block(2, 0)
            push(32, far.at[pl.ds(0, TOP), :], a_top, right_a)
            push(33, far.at[pl.ds(TOP, LOW), :], a_low, left_a)

    def near_a():
        got(32, a_top)
        total(block(1, 0), [(a_top, 0)], 0, TOP)
        push(34, block(1, 0), a_left, right_a)
        got(33, a_low)
        total(block(3, 0), [(a_low, TOP)], TOP, LOW)
        push(35, block(3, 0), a_right, left_a)

    def own_a():
        got(34, a_left)
        got(35, a_right)
        total(block(0, 0), [(a_left, 0), (a_right, 0)])

    order = (2, 1, 3, 0)
    steps = [start]
    for made in (far_b, near_b, own_b):
        steps += [functools.partial(made, ka) for ka in order]
    return steps + [near_a, own_a]


def add_rows(target, parts, offset=0, count=HALF):
    def step(i, carry):
        rows = pl.ds(pl.multiple_of(offset + 16 * i, 16), 16)
        value = target[rows, :].astype(jnp.float32)
        for part, start in parts:
            value = value + part[pl.ds(pl.multiple_of(offset - start + 16 * i, 16), 16), :].astype(jnp.float32)
        target[rows, :] = value.astype(jnp.bfloat16)
        return carry

    lax.fori_loop(0, count // 16, step, 0, unroll=True)


def terms_steps(me, wires, base, first_ref, second_ref, weight_ref, all_ref, conds_ref, sums, rounded, tiles, c_first, c_second):
    peers = [me.sibling(), me.beside(), me.askew()]

    def start():
        sums[me.q, 0] = first_ref[...]
        sums[me.q, 1] = second_ref[...]
        for k in range(3):
            wires.push(base + k, sums.at[me.q], sums.at[me.q], peers[k], base + k)

    def add():
        for k in range(3):
            wires.got(base + k, sums.at[peers[k][2]], peers[k])
        total = sums[0] + sums[1] + sums[2] + sums[3]
        rounded[...] = total.astype(jnp.bfloat16).astype(jnp.float32)
        all_ref[me.d, me.s] = rounded[me.s]
        wires.push(base + 3, rounded.at[1 - me.s], all_ref.at[me.d, me.s], me.flipped())

    def spread_a():
        wires.got(base + 3, all_ref.at[me.d, 1 - me.s], me.sibling())
        for k in (1, 2, 3):
            wires.push(base + 3 + k, all_ref.at[me.d], all_ref.at[me.d], me.ring(k, 0))

    def spread_b():
        for k in (1, 2, 3):
            wires.got(base + 3 + k, all_ref.at[me.dp(4 - k, 0)], me.sibling())
        for ka in range(4):
            block = all_ref.at[me.dp((4 - ka) % 4, 0)]
            for k in (1, 2, 3):
                wires.push(base + 4 + 3 * ka + 2 + k, block, block, me.ring(0, k))

    def multiply():
        for ka in range(4):
            for k in (1, 2, 3):
                wires.got(base + 4 + 3 * ka + 2 + k, all_ref.at[me.dp((4 - ka) % 4, 4 - k)], me.sibling())
        grads = all_ref[...].reshape(256, WIDE).astype(jnp.bfloat16)
        row = lax.rem(lax.broadcasted_iota(jnp.int32, (256, PAIR), 0), 8)
        total = jnp.zeros((256, PAIR), jnp.float32)
        for r in range(6):
            made = dot(grads, weight_ref[:, r * WIDE : (r + 1) * WIDE], 1, 1)
            total = total + jnp.where(row == r, made, 0.0)
        total = jnp.sum(total.reshape(16, 2, 8, PAIR), axis=2, keepdims=True)
        level = lax.broadcasted_iota(jnp.int32, (16, 8, PAIR), 1)
        tiles[0] = jnp.where(level == 0, total[:, 0], jnp.where(level == 1, total[:, 1], 0.0))
        wires.push(base + 19, tiles.at[0], tiles.at[1], me.flipped())

    def join():
        wires.got(base + 19, tiles.at[1], me.sibling())
        tiles[2] = tiles[0] + tiles[1]
        swap_two[0]()

    swap_two = swap_steps(me, wires, base + 20, tiles.at[2], c_first, c_second, conds_ref)
    return [start, add, spread_a, spread_b, multiply, join, swap_two[1], swap_two[2]]


def reduce_kernel(
    first_ref, second_rows, first_terms, second_terms, weight_ref, kept_grad, sent_grad,
    projection_ref, attention_ref, expand_ref, contract_ref, bias_ref, all_ref, conds_ref, grads_ref,
    mine, sib, r_top, r_low, r_left, r_right, a_top, a_low, a_left, a_right, final, r_across, r_beside, rows, r_grad, wide_grad,
    sums, rounded, tiles, c_first, c_second, load, local, send, recv,
):
    me = Place()
    greet(me.grid_peers() + [me.across(), me.flipped(), me.beside(), me.askew(), me.sibling()])
    wires = Wires(send, recv)
    buffers = (mine, sib, r_top, r_low, r_left, r_right, a_top, a_low, a_left, a_right)
    two = reduce_steps(me, wires, 36, first_ref, load, buffers)
    small = terms_steps(me, wires, 86, first_terms, second_terms, weight_ref, all_ref, conds_ref, sums, rounded, tiles, c_first, c_second)
    two[0]()
    small[0]()
    keeps = [
        pltpu.make_async_copy(second_rows, final.at[1], local.at[3]),
        pltpu.make_async_copy(kept_grad, grads_ref.at[me.s], local.at[1]),
    ]
    for item in keeps:
        item.start()
    big = two[1:]
    small = small[1:]
    for index, step in enumerate(big):
        step()
        if index % 2 == 1 and small:
            small.pop(0)()
        if index == 2:
            wires.push(73, sent_grad, r_grad, me.flipped())
    while small:
        small.pop(0)()
    final[0] = mine[me.d]
    for item in keeps:
        item.wait()
    wires.got(73, r_grad, me.flipped())
    wide_grad[...] = r_grad[...].astype(jnp.float32)
    came = pltpu.make_async_copy(wide_grad, grads_ref.at[1 - me.s], local.at[0])
    came.start()
    held = final.at[me.s]
    cuts = ((0, 80), (80, 80), (160, 80), (240, 64))
    for n, (start, count) in enumerate(cuts):
        part = pl.ds(start, count)
        wires.push(74 + n, final.at[1 - me.s, part, :], r_across.at[part, :], me.across())
    for n, (start, count) in enumerate(cuts):
        part = pl.ds(start, count)
        wires.got(74 + n, r_across.at[part, :], me.across())
        add_rows(held, [(r_across, 0)], start, count)
        wires.push(78 + n, held.at[part, :], r_beside.at[part, :], me.beside())
    for n, (start, count) in enumerate(cuts):
        part = pl.ds(start, count)
        wires.got(78 + n, r_beside.at[part, :], me.beside())
        total = held[part, :].astype(jnp.float32) + r_beside[part, :].astype(jnp.float32)
        rows[half_rows(me.c, start, count), :] = total.astype(jnp.bfloat16)
        block = rows.at[half_rows(me.c, start, count), :]
        wires.push(82 + n, block, block, me.sibling())
    for n, (start, count) in enumerate(cuts):
        wires.got(82 + n, rows.at[half_rows(1 - me.c, start, count), :], me.sibling())
    for ref, starts in ((projection_ref, (0, 48, 96)), (attention_ref, (144,)), (expand_ref, EXPAND_ROWS)):
        for k, start in enumerate(starts):
            ref[:, k * WIDE : (k + 1) * WIDE] = rows[start : start + 48, :].astype(jnp.float32)
    contract_ref[...] = rows[CONTRACT_ROW : CONTRACT_ROW + 192, :].astype(jnp.float32)
    bias_ref[...] = rows[BIAS_ROW : BIAS_ROW + 16, :].astype(jnp.float32)
    came.wait()
    wires.finish()


def reduce_buffers():
    blocks = lambda *lead: pltpu.VMEM(lead + (WIDE,), jnp.bfloat16)
    return [
        blocks(16, HALF),
        blocks(16, HALF),
        blocks(4, TOP),
        blocks(4, LOW),
        blocks(4, HALF),
        blocks(4, HALF),
        blocks(TOP),
        blocks(LOW),
        blocks(HALF),
        blocks(HALF),
    ]


def reduce_grads(*operands):
    count = 86 + 26
    bf, f32 = jnp.bfloat16, jnp.float32
    blocks = lambda *lead: pltpu.VMEM(lead + (WIDE,), bf)
    whole = pl.BlockSpec(memory_space=pltpu.VMEM)
    away = pl.BlockSpec(memory_space=pl.ANY)
    return pl.pallas_call(
        reduce_kernel,
        out_shape=[
            jax.ShapeDtypeStruct((48, 3 * WIDE), f32),
            jax.ShapeDtypeStruct((48, WIDE), f32),
            jax.ShapeDtypeStruct((48, 4 * WIDE), f32),
            jax.ShapeDtypeStruct((192, WIDE), f32),
            jax.ShapeDtypeStruct((16, WIDE), f32),
            jax.ShapeDtypeStruct((16, 2, 8, WIDE), f32),
            jax.ShapeDtypeStruct((16, 8, PAIR), f32),
            jax.ShapeDtypeStruct((2, TOKENS, WIDE), f32),
        ],
        in_specs=[away, away, whole, whole, whole, away, away],
        out_specs=[whole] * 7 + [away],
        scratch_shapes=[
            *reduce_buffers(),
            blocks(2, HALF),
            blocks(HALF),
            blocks(HALF),
            blocks(ROWS),
            blocks(TOKENS),
            pltpu.VMEM((TOKENS, WIDE), f32),
            pltpu.VMEM((4, 2, 8, WIDE), f32),
            pltpu.VMEM((2, 8, WIDE), f32),
            pltpu.VMEM((3, 16, 8, PAIR), f32),
            pltpu.VMEM((2, 4, 4, 8, PAIR), f32),
            pltpu.VMEM((2, 4, 4, 8, PAIR), f32),
            pltpu.SemaphoreType.DMA((16,)),
            pltpu.SemaphoreType.DMA((4,)),
            pltpu.SemaphoreType.DMA((count,)),
            pltpu.SemaphoreType.DMA((count,)),
        ],
        compiler_params=pltpu.CompilerParams(
            collective_id=1, has_side_effects=True, vmem_limit_bytes=48 * 1024 * 1024
        ),
        cost_estimate=pl.CostEstimate(flops=0, bytes_accessed=60000000, transcendentals=0),
        name="reduce_grads",
    )(*operands)


def seq_peers(me):
    far = [(me.s, me.d, (1 - me.xl) * 2 + core) for core in range(2)]
    return me.sibling(), far


def forward_kernel(
    part, x_ref, mod_ref, bias_ref, w_hbm, *refs
):
    shard_ref, refs = (refs[0], refs[1:]) if part == 0 else (None, refs)
    out_ref, mixed_one_ref, qkv_out, lse_ref, att_out, branch_one_ref, middle_ref, mixed_two_ref, expanded_out, branch_two_ref, *refs = refs
    next_ref, refs = (refs[0], refs[1:]) if part == 0 else (None, refs)
    w, stage, qkv, heads, att, expanded, load, save, send, recv = refs
    me = Place()
    sibling, far = seq_peers(me)
    first_load = pltpu.make_async_copy(w_hbm.at[:, pl.ds(0, 144), :], w.at[:, pl.ds(0, 144), :], load.at[0])
    rest_load = pltpu.make_async_copy(w_hbm.at[:, pl.ds(144, 464), :], w.at[:, pl.ds(144, 464), :], load.at[1])
    first_load.start()
    rest_load.start()
    around = [me.ring(1, 0), me.ring(3, 0), me.ring(0, 1), me.ring(0, 3)] if part == 0 else []
    greet([sibling, *far, *around])
    wires = Wires(send, recv)
    beside = gather_steps(me, wires, 12, shard_ref, next_ref, load.at[2]) if part == 0 else []

    def advance(count):
        for _ in range(min(count, len(beside))):
            beside.pop(0)()

    advance(1)

    row = lambda index: mod_ref[index : index + 1, :]
    bias = lambda index: bias_ref[index : index + 1, :]
    tokens = x_ref[...].astype(jnp.float32)
    normed_one, _ = norm_rows(tokens)
    mixed_one = (normed_one * (1.0 + row(1)) + row(0)).astype(jnp.bfloat16)
    mixed_one_ref[...] = mixed_one
    first_load.wait()

    def project(kind, weight_row, added):
        made = dot(mixed_one, square(w, weight_row))
        if added is not None:
            made = made + added
        made = made.astype(jnp.bfloat16)
        for pair in range(6):
            stage[pair, kind] = made[:, pair * PAIR : (pair + 1) * PAIR]

    project(0, 48, None)
    project(1, 96, bias(1))
    for j in range(3):
        for g in range(2):
            wires.push(2 * j + g, stage.at[3 * g + j, pl.ds(0, 2)], qkv.at[2 + me.c, j, pl.ds(0, 2)], far[g], 2 * j + me.c)
    project(2, 0, bias(0))
    advance(1)
    for j in range(3):
        wires.push(6 + j, stage.at[3 * (1 - me.c) + j], qkv.at[me.c, j], sibling)
    for j in range(3):
        qkv[me.c, j] = stage[3 * me.c + j]

    advance(1)
    for j in range(3):
        wires.got(6 + j, qkv.at[1 - me.c, j], sibling)
        for g in range(2):
            wires.got(2 * j + g, qkv.at[2 + g, j, pl.ds(0, 2)], far[g])

        def queries_step(g, carry):
            keys = qkv[:, j, 0].reshape(4 * TOKENS, PAIR)
            values = qkv[:, j, 1].reshape(4 * TOKENS, PAIR)
            queries = qkv[g, j, 2] * jnp.bfloat16(0.125)
            made = []
            for head in range(2):
                scores = dot(keys, only_head(queries, head), 1, 1)
                top = jnp.max(scores, axis=0, keepdims=True)
                powers = jnp.exp(scores - top)
                sums = jnp.sum(powers, axis=0, keepdims=True)
                lse_ref[(2 * j + head) * 2 + g] = top + jnp.log(sums)
                weights = powers.astype(jnp.bfloat16)
                made.append(dot(values, weights, 0, 0)[head * HEAD : (head + 1) * HEAD] * (1.0 / sums))
            heads[g, j] = jnp.concatenate(made, axis=0).T.astype(jnp.bfloat16)
            return carry

        lax.fori_loop(0, 2, queries_step, 0)
        wires.push(9 + j, heads.at[1 - me.c, j], att.at[3 * me.c + j], sibling)
        att[3 * me.c + j] = heads[me.c, j]
        advance(1)
    qkv_save = pltpu.make_async_copy(qkv, qkv_out, save.at[0])
    qkv_save.start()
    rest_load.wait()
    for j in range(3):
        wires.got(9 + j, att.at[3 * (1 - me.c) + j], sibling)
    att_save = pltpu.make_async_copy(att, att_out, save.at[1])
    att_save.start()
    attended = side_by_side(att)
    branch_one = dot(attended, square(w, 144)) + bias(2)
    branch_one_ref[...] = branch_one
    advance(1)
    middle = tokens + row(2) * branch_one
    middle_ref[...] = middle
    normed_two, _ = norm_rows(middle)
    mixed_two = (normed_two * (1.0 + row(4)) + row(3)).astype(jnp.bfloat16)
    mixed_two_ref[...] = mixed_two
    total = bias(7)
    saves = []
    for k in range(4):
        u = dot(mixed_two, square(w, EXPAND_ROWS[k])) + bias(3 + k)
        expanded[k] = u
        item = pltpu.make_async_copy(expanded.at[k], expanded_out.at[k], save.at[2 + k])
        item.start()
        saves.append(item)
        activated = (0.5 * u * (1.0 + jnp.tanh(ROOT * (u + 0.044715 * (u * u * u))))).astype(jnp.bfloat16)
        total = total + dot(activated, contract_square(w, k))
        advance(1)
    branch_two_ref[...] = total
    out_ref[...] = (middle + row(5) * total).astype(jnp.bfloat16)
    advance(12)
    qkv_save.wait()
    att_save.wait()
    for item in saves:
        item.wait()
    wires.finish()


def block_forward(part, tokens, modulation, bias, blocks, *shard):
    shape = lambda dims, dtype: jax.ShapeDtypeStruct(dims, dtype)
    bf, f32 = jnp.bfloat16, jnp.float32
    whole = pl.BlockSpec(memory_space=pltpu.VMEM)
    away = pl.BlockSpec(memory_space=pl.ANY)
    return pl.pallas_call(
        functools.partial(forward_kernel, part),
        out_shape=[
            shape((TOKENS, WIDE), bf),
            shape((TOKENS, WIDE), bf),
            shape((4, 3, 3, TOKENS, PAIR), bf),
            shape((12, 1, TOKENS), f32),
            shape((6, TOKENS, PAIR), bf),
            shape((TOKENS, WIDE), f32),
            shape((TOKENS, WIDE), f32),
            shape((TOKENS, WIDE), bf),
            shape((4, TOKENS, WIDE), f32),
            shape((TOKENS, WIDE), f32),
        ]
        + [shape((16, ROWS, WIDE), bf) for _ in shard],
        in_specs=[whole, whole, whole, away] + [away for _ in shard],
        out_specs=[whole, whole, away, whole, away, whole, whole, whole, away, whole] + [away for _ in shard],
        scratch_shapes=[
            pltpu.VMEM((16, ROWS, WIDE), bf),
            pltpu.VMEM((6, 3, TOKENS, PAIR), bf),
            pltpu.VMEM((4, 3, 3, TOKENS, PAIR), bf),
            pltpu.VMEM((2, 3, TOKENS, PAIR), bf),
            pltpu.VMEM((6, TOKENS, PAIR), bf),
            pltpu.VMEM((4, TOKENS, WIDE), f32),
            pltpu.SemaphoreType.DMA((3,)),
            pltpu.SemaphoreType.DMA((6,)),
            pltpu.SemaphoreType.DMA((48,)),
            pltpu.SemaphoreType.DMA((48,)),
        ],
        compiler_params=pltpu.CompilerParams(
            collective_id=2 + part, has_side_effects=True, vmem_limit_bytes=56 * 1024 * 1024
        ),
        cost_estimate=pl.CostEstimate(flops=5 * 10**9, bytes_accessed=25 * 10**6, transcendentals=4 * 10**6),
        name=("forward_first", "forward_second")[part],
    )(tokens, modulation, bias, blocks, *shard)


def backward_kernel(
    part, grad_ref, x_ref, mod_ref, w_hbm, mixed_one_ref, qkv_in, lse_ref, att_ref, branch_one_ref, middle_ref, mixed_two_ref, expanded_in, branch_two_ref, *refs
):
    if part == 0:
        later_ref, *refs = refs
    else:
        kept_out, sent_out, *refs = refs
    input_grad_ref, terms_ref, grads_out, *refs = refs
    extra_out, *refs = refs
    carried, refs = (input_grad_ref, refs) if part == 0 else (refs[0], refs[1:])
    w, expanded, qkv, stage, given, dkv, dq, own, far_out, far_in, side_out, side_in, joined, load, save, send, recv, *refs = refs
    me = Place()
    sibling, far = seq_peers(me)
    c, other = me.c, 1 - me.c
    back_load = pltpu.make_async_copy(w_hbm.at[:, pl.ds(192, 416), :], w.at[:, pl.ds(192, 416), :], load.at[0])
    expanded_load = pltpu.make_async_copy(expanded_in, expanded, load.at[1])
    front_load = pltpu.make_async_copy(w_hbm.at[:, pl.ds(0, 192), :], w.at[:, pl.ds(0, 192), :], load.at[2])
    qkv_load = pltpu.make_async_copy(qkv_in, qkv, load.at[3])
    back_load.start()
    expanded_load.start()
    front_load.start()
    qkv_load.start()
    around = [me.ring(1, 0), me.ring(3, 0), me.ring(0, 1), me.ring(0, 3)] if part == 0 else [me.flipped()]
    greet([sibling, *far, *around])
    wires = Wires(send, recv)
    beside = reduce_steps(me, wires, 10, later_ref, refs[-1], refs[:-1]) if part == 0 else []

    def advance(count):
        for _ in range(min(count, len(beside))):
            beside.pop(0)()

    advance(1)
    if part == 1:
        keep_out = pltpu.make_async_copy(kept_out, extra_out.at[me.s], load.at[4])
        keep_out.start()
        wires.push(10, sent_out, extra_out.at[me.s], me.flipped())
    saves = []

    def keep(index, start, count):
        rows = pl.ds(start, count)
        item = pltpu.make_async_copy(w.at[:, rows, :], grads_out.at[:, rows, :], save.at[index])
        item.start()
        saves.append(item)

    row = lambda index: mod_ref[index : index + 1, :]
    gradient = grad_ref[...].astype(jnp.float32)
    branch_two_grad = (row(5) * gradient).astype(jnp.bfloat16)
    gate_two_grad = column_sum(gradient * branch_two_ref[...])
    contract_bias_grad = column_sum(branch_two_grad)
    mixed_two = mixed_two_ref[...]
    mixed_two_grad = None
    expand_bias_grads = []
    back_load.wait()
    expanded_load.wait()
    for k in range(4):
        u = expanded[k]
        squared = u * u
        tanh = jnp.tanh(ROOT * (u + 0.044715 * (squared * u)))
        half = 0.5 * (1.0 + tanh)
        activated = (u * half).astype(jnp.bfloat16)
        slope = half + 0.5 * u * (1.0 - tanh * tanh) * (ROOT * (1.0 + (3.0 * 0.044715) * squared))
        expanded_grad = (dot(branch_two_grad, contract_square(w, k), 1, 1) * slope).astype(jnp.bfloat16)
        start = EXPAND_ROWS[k]
        expand_bias_grads.append(column_sum(expanded_grad))
        term = dot(expanded_grad, square(w, start), 1, 1)
        mixed_two_grad = term if mixed_two_grad is None else mixed_two_grad + term
        w[4 * k : 4 * k + 4, CONTRACT_ROW : CONTRACT_ROW + 192, :] = (
            dot(activated, branch_two_grad, 0, 0).astype(jnp.bfloat16).reshape(4, 192, WIDE)
        )
        w[:, start : start + 48, :] = dot(mixed_two, expanded_grad, 0, 0).astype(jnp.bfloat16).reshape(16, 48, WIDE)
        advance(1)
    keep(0, 304, 288)
    keep(1, 192, 96)
    normed_two, inv_two = norm_rows(middle_ref[...])
    scale_two_grad = column_sum(mixed_two_grad * normed_two)
    shift_two_grad = column_sum(mixed_two_grad)
    middle_grad = gradient + norm_back(mixed_two_grad * (1.0 + row(4)), normed_two, inv_two)
    gate_one_grad = column_sum(middle_grad * branch_one_ref[...])
    branch_one_grad = (row(2) * middle_grad).astype(jnp.bfloat16)
    front_load.wait()
    attended_grad = dot(branch_one_grad, square(w, 144), 1, 1).astype(jnp.bfloat16)
    for pair in range(6):
        stage[pair] = attended_grad[:, pair * PAIR : (pair + 1) * PAIR]
    wires.push(0, stage.at[pl.ds(3 * other, 3)], given.at[c], sibling)
    advance(1)
    given[c] = stage[pl.ds(3 * c, 3)]
    carried[...] = middle_grad
    w[:, 144:192, :] = dot(side_by_side(att_ref), branch_one_grad, 0, 0).astype(jnp.bfloat16).reshape(16, 48, WIDE)
    keep(2, 144, 48)
    attention_bias_grad = column_sum(branch_one_grad)
    advance(1)
    qkv_load.wait()
    wires.got(0, given.at[other], sibling)

    for j in range(3):
        dkv[...] = jnp.zeros_like(dkv)

        def queries_step(g, carry):
            keys = qkv[:, j, 0].reshape(4 * TOKENS, PAIR)
            values = qkv[:, j, 1].reshape(4 * TOKENS, PAIR)
            queries = qkv[g, j, 2] * jnp.bfloat16(0.125)
            output_grads = given[g, j]
            key_sums, value_sums, query_parts = 0.0, 0.0, []
            for head in range(2):
                head_queries = only_head(queries, head)
                head_grads = only_head(output_grads, head)
                scores = dot(keys, head_queries, 1, 1)
                probs = jnp.exp(scores - lse_ref[(2 * j + head) * 2 + g])
                weight_grads = dot(values, head_grads, 1, 1)
                centre = jnp.sum(probs * weight_grads, axis=0, keepdims=True)
                score_grads = (probs * (weight_grads - centre)).astype(jnp.bfloat16)
                key_sums = key_sums + dot(score_grads, head_queries)
                value_sums = value_sums + dot(probs.astype(jnp.bfloat16), head_grads)
                query_parts.append(dot(keys, score_grads, 0, 0)[head * HEAD : (head + 1) * HEAD])
            dq[g] = jnp.concatenate(query_parts, axis=0).T * 0.125
            dkv[0] += key_sums.reshape(4, TOKENS, PAIR)
            dkv[1] += value_sums.reshape(4, TOKENS, PAIR)
            return carry

        lax.fori_loop(0, 2, queries_step, 0)
        for g in range(2):
            far_out[j, g] = dkv[:, 2 + g].astype(jnp.bfloat16)
            wires.push(1 + 2 * j + g, far_out.at[j, g], far_in.at[j, c], far[g], 1 + 2 * j + c)
        side_out[j, 0:2] = dkv[:, other].astype(jnp.bfloat16)
        side_out[j, 2] = dq[other].astype(jnp.bfloat16)
        wires.push(7 + j, side_out.at[j], side_in.at[j], sibling)
        own[j, 0:2] = dkv[:, c]
        own[j, 2] = dq[c]
        advance(1 if j == 0 else 2)

    for j in range(3):
        wires.got(7 + j, side_in.at[j], sibling)
        for g in range(2):
            wires.got(1 + 2 * j + g, far_in.at[j, g], far[g])
        for kind in range(2):
            joined[kind, 3 * c + j] = (own[j, kind] + far_in[j, c, kind].astype(jnp.float32)).astype(jnp.bfloat16)
            joined[kind, 3 * other + j] = (
                side_in[j, kind].astype(jnp.float32) + far_in[j, other, kind].astype(jnp.float32)
            ).astype(jnp.bfloat16)
        joined[2, 3 * c + j] = own[j, 2].astype(jnp.bfloat16)
        joined[2, 3 * other + j] = side_in[j, 2]
    mixed_one = mixed_one_ref[...]
    mixed_one_grad, bias_grads = None, []
    for kind, start in ((0, 48), (1, 96), (2, 0)):
        piece = side_by_side(joined, (kind,))
        bias_grads.append(column_sum(piece))
        term = dot(piece, square(w, start), 1, 1)
        mixed_one_grad = term if mixed_one_grad is None else mixed_one_grad + term
        w[:, start : start + 48, :] = dot(mixed_one, piece, 0, 0).astype(jnp.bfloat16).reshape(16, 48, WIDE)
        advance(1)
    keep(3, 0, 144)
    small = jnp.concatenate(
        [
            bias_grads[2],
            bias_grads[1],
            attention_bias_grad,
            *expand_bias_grads,
            contract_bias_grad,
            jnp.zeros((8, WIDE), jnp.float32),
        ],
        axis=0,
    ).astype(jnp.bfloat16)
    w[:, BIAS_ROW : BIAS_ROW + 16, :] = jnp.broadcast_to(small[None], (16, 16, WIDE))
    w[:, 592:608, :] = jnp.zeros((16, 16, WIDE), jnp.bfloat16)
    keep(4, BIAS_ROW, 16)
    keep(5, 592, 16)
    normed_one, inv_one = norm_rows(x_ref[...].astype(jnp.float32))
    terms_ref[...] = jnp.concatenate(
        [
            column_sum(mixed_one_grad),
            column_sum(mixed_one_grad * normed_one),
            gate_one_grad,
            shift_two_grad,
            scale_two_grad,
            gate_two_grad,
            jnp.zeros((2, WIDE), jnp.float32),
        ],
        axis=0,
    )
    result = carried[...] + norm_back(mixed_one_grad * (1.0 + row(1)), normed_one, inv_one)
    input_grad_ref[...] = result.astype(input_grad_ref.dtype)
    advance(16)
    if part == 0:
        rows_save = pltpu.make_async_copy(refs[0].at[me.d], extra_out, load.at[0])
        rows_save.start()
        rows_save.wait()
    else:
        keep_out.wait()
        wires.got(10, extra_out.at[1 - me.s], me.flipped())
    for item in saves:
        item.wait()
    wires.finish()


def block_backward(part, gradient, tokens, modulation, blocks, kept, *later):
    shape = lambda dims, dtype: jax.ShapeDtypeStruct(dims, dtype)
    bf, f32 = jnp.bfloat16, jnp.float32
    whole = pl.BlockSpec(memory_space=pltpu.VMEM)
    away = pl.BlockSpec(memory_space=pl.ANY)
    return pl.pallas_call(
        functools.partial(backward_kernel, part),
        out_shape=[
            shape((TOKENS, WIDE), f32 if part == 0 else bf),
            shape((8, WIDE), f32),
            shape((16, ROWS, WIDE), bf),
        ]
        + [shape((HALF, WIDE), bf) if part == 0 else shape((2, TOKENS, WIDE), bf)],
        in_specs=[whole, whole, whole, away, whole, away, whole, whole, whole, whole, whole, away, whole] + [away for _ in later],
        out_specs=[whole, whole, away, away],
        scratch_shapes=([] if part == 0 else [pltpu.VMEM((TOKENS, WIDE), f32)])
        + [
            pltpu.VMEM((16, ROWS, WIDE), bf),
            pltpu.VMEM((4, TOKENS, WIDE), f32),
            pltpu.VMEM((4, 3, 3, TOKENS, PAIR), bf),
            pltpu.VMEM((6, TOKENS, PAIR), bf),
            pltpu.VMEM((2, 3, TOKENS, PAIR), bf),
            pltpu.VMEM((2, 4, TOKENS, PAIR), f32),
            pltpu.VMEM((2, TOKENS, PAIR), f32),
            pltpu.VMEM((3, 3, TOKENS, PAIR), f32),
            pltpu.VMEM((3, 2, 2, TOKENS, PAIR), bf),
            pltpu.VMEM((3, 2, 2, TOKENS, PAIR), bf),
            pltpu.VMEM((3, 3, TOKENS, PAIR), bf),
            pltpu.VMEM((3, 3, TOKENS, PAIR), bf),
            pltpu.VMEM((3, 6, TOKENS, PAIR), bf),
            pltpu.SemaphoreType.DMA((5,)),
            pltpu.SemaphoreType.DMA((6,)),
            pltpu.SemaphoreType.DMA((46,)),
            pltpu.SemaphoreType.DMA((46,)),
        ]
        + ([*reduce_buffers(), pltpu.SemaphoreType.DMA((16,))] if part == 0 else []),
        compiler_params=pltpu.CompilerParams(
            collective_id=4 + part, has_side_effects=True, vmem_limit_bytes=60 * 1024 * 1024
        ),
        cost_estimate=pl.CostEstimate(flops=12 * 10**9, bytes_accessed=45 * 10**6, transcendentals=4 * 10**6),
        name=("backward_first", "backward_second")[part],
    )(gradient, tokens, modulation, blocks, *kept, *later)


def bias_rows(biases):
    parts = [
        biases[:, :96].reshape(2, WIDE),
        biases[:, 96:144].reshape(1, WIDE),
        biases[:, 144:336].reshape(4, WIDE),
        biases[:, 336:384].reshape(1, WIDE),
    ]
    added = jnp.pad(biases[:, 384:672].reshape(6, WIDE), ((0, 2), (0, 0)))
    return jnp.concatenate(parts), added


def with_biases(made, bias, place):
    own = lambda part, size: lax.dynamic_slice_in_dim(part.reshape(-1), place * size, size)
    projection, attention, expand, contract = made
    return [
        projection,
        own(bias[0:2], 96),
        attention,
        own(bias[2:3], 48),
        expand,
        own(bias[3:7], 192),
        contract,
        own(bias[7:8], 48),
    ]


def on_device(
    latents,
    conditions,
    output_cotangent,
    modulation_weight,
    modulation_bias,
    projection_weight,
    projection_bias,
    attention_weight,
    attention_bias,
    expand_weight,
    expand_bias,
    contract_weight,
    contract_bias,
):
    section = lax.axis_index("section")
    place = lax.axis_index("dp")
    is_first = section == 0
    biases = jnp.concatenate(
        [projection_bias[0], attention_bias[0], expand_bias[0], contract_bias[0], modulation_bias[0]]
    )
    extra = jnp.pad(biases[None], ((0, 15), (0, WIDE - biases.shape[0])))
    pieces = jnp.pad(conditions[:, 0].reshape(2, 16, 48).swapaxes(0, 1), ((0, 0), (0, 6), (0, PAIR - 48)))
    owned_weight = jnp.pad(modulation_weight[0], ((0, PAIR - 48), (0, 0)))
    first_blocks, shard, own_conds, modulations = gather_weights(
        projection_weight[0], attention_weight[0], expand_weight[0], contract_weight[0], extra, pieces, owned_weight
    )
    first_bias, first_added = bias_rows(first_blocks[:, BIAS_ROW].astype(jnp.float32))
    first_modulation = modulations[0] + first_added

    tokens = lax.dynamic_index_in_dim(latents, section, 0, keepdims=False)[0]
    cotangent = lax.dynamic_index_in_dim(output_cotangent, section, 0, keepdims=False)[0]
    first_output, *first_kept, second_blocks = block_forward(0, tokens, first_modulation, first_bias, first_blocks, shard)
    second_bias, second_added = bias_rows(second_blocks[:, BIAS_ROW].astype(jnp.float32))
    second_modulation = modulations[1] + second_added
    second_output, *second_kept = block_forward(1, first_output, second_modulation, second_bias, second_blocks)
    second_grad, second_terms, second_made, section_outputs = block_backward(
        1,
        cotangent,
        first_output,
        second_modulation,
        second_blocks,
        second_kept,
        jnp.where(is_first, first_output, second_output),
        jnp.where(is_first, second_output, first_output),
    )
    first_grad, first_terms, first_made, second_rows = block_backward(
        0, second_grad, tokens, first_modulation, first_blocks, first_kept, second_made
    )

    rounded_grad = second_grad.astype(jnp.float32)
    *made, bias, terms, cond_terms, input_grads = reduce_grads(
        first_made,
        second_rows,
        first_terms,
        second_terms,
        owned_weight,
        jnp.where(is_first, first_grad, rounded_grad),
        jnp.where(is_first, second_grad, first_grad.astype(jnp.bfloat16)),
    )
    reduced = [grad[None] for grad in with_biases(made, bias, place)]
    section_outputs = section_outputs[None, :, None]
    input_grads = input_grads[None, :, None]
    terms = terms[:, :, :6].reshape(16, 2, -1)
    own_silu = jax.nn.silu(own_conds[:, :2, :48]).astype(jnp.bfloat16)
    modulation_weight_grad = jnp.einsum(
        "imk,ime->ke", own_silu, terms.astype(jnp.bfloat16), preferred_element_type=jnp.float32
    )
    modulation_bias_grad = lax.dynamic_slice_in_dim(jnp.sum(terms, axis=(0, 1)), place * 288, 288)
    cond_terms = cond_terms[:, :2, :48].swapaxes(0, 1).reshape(2, 1, WIDE)
    condition_grads = jax.vjp(jax.nn.silu, conditions)[1](cond_terms)[0]
    return (
        section_outputs,
        input_grads,
        condition_grads,
        modulation_weight_grad[None],
        modulation_bias_grad[None],
        *reduced,
    )


def solution(mesh):
    return jax.shard_map(
        on_device,
        mesh=mesh,
        in_specs=(
            P(None, "dp", "seq", None),
            P(None, "dp", None),
            P(None, "dp", "seq", None),
            P("section", "dp", None),
            P("section", "dp"),
            P("section", "dp", None),
            P("section", "dp"),
            P("section", "dp", None),
            P("section", "dp"),
            P("section", "dp", None),
            P("section", "dp"),
            P("section", "dp", None),
            P("section", "dp"),
        ),
        out_specs=(
            P("section", None, "dp", "seq", None),
            P("section", None, "dp", "seq", None),
            P(None, "dp", None),
            P("section", "dp", None),
            P("section", "dp"),
            P("section", "dp", None),
            P("section", "dp"),
            P("section", "dp", None),
            P("section", "dp"),
            P("section", "dp", None),
            P("section", "dp"),
            P("section", "dp", None),
            P("section", "dp"),
        ),
        check_vma=False,
    )
```
